32 devices in a mesh: groups: 2 (over x), chan: 8 (over z, y), seq: 2 (over core).
Axes of the slice: x: 2, y: 2, z: 4, core: 2. Of those that a mesh axis runs over, the one named last changes fastest.
Arguments:
- tokens: bfloat16 [2048, 8192], P(('groups', 'seq'), 'chan'), parts along dimension 0, may hold values from -42 to 42
- norm_gain: float32 [8192], replicated, may hold values from 0.1 to 1.9
- in_weight: bfloat16 [3, 8192, 8192], P(None, None, 'chan'), may hold values from -0.0625 to 0.0625
- short_weight: float32 [3, 7, 8192], P(None, None, 'chan'), may hold values from -2 to 2
- log_decay: float32 [16, 8192], P(None, 'chan'), may hold values from -0.034 to 0
- residue: float32 [16, 8192], P(None, 'chan'), may hold values from -0.15625 to 0.15625
- skip: float32 [8192], P('chan'), may hold values from 0.1 to 1.9
- out_weight: bfloat16 [8192, 8192], P('chan'), may hold values from -0.09375 to 0.09375
Outputs:
- mixed: bfloat16 [2048, 8192], P(('groups', 'seq'), 'chan'), parts along dimension 0
The draws below stay inside these ranges and needn't reach their ends.
There are 2 independent parts, one for each index of `groups`. The reference program is written for one: setup_inputs(seed, part) draws one part's arguments, and reference() takes and returns one part's arrays. A program takes and returns all parts, laid end to end along the dimension named above; an argument that names none is the same for every part. Nothing has to cross between parts.
All inputs are finite; a program needn't handle non-finite values.
Results may differ from the reference program's by a relative error of at most 0.0067.
Values may be sent and summed in bfloat16 or wider, within the bound.
No kernel may reach another device: no remote copies, remote signals or barrier semaphores. Data moves between devices by JAX's collectives and lax.ppermute only.
A program may use at most 448 MiB of HBM per device.

```python
import math
import jax
import jax.numpy as jnp
from jax import lax

D = 8192
POLES = 16
SHORT = 7
SEQ_LEN = 1024


def draw_tokens(key, part):
    keys = jax.random.split(key, 3)
    row_scale = jnp.exp(jax.random.uniform(keys[1], (SEQ_LEN, 1), jnp.float32, math.log(0.3), math.log(3.0)))
    ramp = jnp.sqrt(1.0 + 2.0 * jnp.arange(D, dtype=jnp.float32) / D)
    col_scale = jnp.exp(jax.random.uniform(keys[2], (1, D), jnp.float32, math.log(0.5), math.log(2.0))) * ramp[None, :]
    base = jnp.clip(jax.random.normal(keys[0], (SEQ_LEN, D), jnp.float32), -4.0, 4.0)
    return (base * row_scale * col_scale).astype(jnp.bfloat16)


def draw_log_decay(key, part):
    keys = jax.random.split(key, 3)
    slow = jnp.exp(jax.random.uniform(keys[0], (POLES, D), jnp.float32, math.log(0.1 / SEQ_LEN), math.log(2.0 / SEQ_LEN)))
    fast = jnp.exp(jax.random.uniform(keys[1], (POLES, D), jnp.float32, math.log(1.0 / 50.0), math.log(1.0 / 30.0)))
    share = 0.5
    picked = jax.random.uniform(keys[2], (POLES, D), jnp.float32) < share
    return -jnp.where(picked, fast, slow)


def with_spikes(drawn, own_key, source, target, shards_of, factor):
    def block_of(dim):
        return (jnp.arange(drawn.shape[dim]) // (drawn.shape[dim] // shards_of)).reshape((-1,) + (1,) * (drawn.ndim - 1 - dim))

    near = jax.random.permutation(own_key, shards_of)[block_of(target)]
    second = (block_of(target) + shards_of // 2) % shards_of
    return jnp.where((block_of(source) == near) | (block_of(source) == second), factor * drawn, drawn)


def block_levels(own_key, shape, shards, smallest, largest):
    factor_of = 1.0
    for dim, blocks in shards:
        steps = jax.random.uniform(jax.random.fold_in(jax.random.fold_in(own_key, 6), dim), (blocks,), jnp.float32, smallest / len(shards), largest / len(shards))
        factor_of = factor_of * jnp.repeat(jnp.exp(steps), shape[dim] // blocks).reshape((-1,) + (1,) * (len(shape) - 1 - dim))
    return factor_of


def gaussian(key, extent, spread, reach, shards=(), kind=jnp.bfloat16):
    values = spread * jax.random.normal(key, extent, jnp.float32)
    if shards:
        values = values * block_levels(key, extent, shards, -0.22, 0.18)
    return jnp.clip(values, -reach, reach).astype(kind)


def noise_with(key, extent, spread, most, cuts, heavy, held_as=jnp.bfloat16):
    array = spread * jax.random.normal(key, extent, jnp.float32)
    if cuts:
        array = array * block_levels(key, extent, cuts, -0.22, 0.18)
    return jnp.clip(with_spikes(array, jax.random.fold_in(key, 3), *heavy), -most, most).astype(held_as)


def setup_inputs(seed: int = 0, part: int = 0) -> dict:
    splits = jax.random.split(jax.random.key(seed), 9)
    own_keys = jax.random.split(jax.random.fold_in(splits[8], part), 9)
    return {
        "tokens": draw_tokens(jax.random.fold_in(jax.random.fold_in(splits[8], part), 71), part),
        "norm_gain": jnp.clip(1.0 + 0.18 * jax.random.normal(splits[1], (D,), jnp.float32), 0.1, 1.9),
        "in_weight": gaussian(splits[2], (3, D, D), D ** -0.5, 0.0625, ((2, 8),)),
        "short_weight": gaussian(splits[3], (3, SHORT, D), SHORT ** -0.5, 2.0, ((2, 8),), jnp.float32),
        "log_decay": draw_log_decay(jax.random.fold_in(splits[8], 71), part),
        "residue": gaussian(splits[5], (POLES, D), ((2.0 / (POLES * SEQ_LEN)) ** 0.5), 0.15625, ((1, 8),), jnp.float32),
        "skip": jnp.clip(1.0 + 0.18 * jax.random.normal(splits[6], (D,), jnp.float32), 0.1, 1.9),
        "out_weight": noise_with(splits[7], (D, D), D ** -0.5, 0.09375, ((0, 8),), (0, 1, 8, 2.0)),
    }


EPSILON = 1e-06

def reference(tokens, norm_gain, in_weight, short_weight, log_decay, residue, skip, out_weight):
    seq_total = tokens.shape[0]
    taps = short_weight.shape[1]
    tok_float = tokens.astype(jnp.float32)
    inv_rms = lax.rsqrt(lax.optimization_barrier(jnp.mean(tok_float * tok_float, axis=1, keepdims=True)) + EPSILON)
    scaled = (tok_float * norm_gain[None, :]).astype(jnp.bfloat16)
    proj = jnp.stack([(jnp.dot(scaled, in_weight[which], preferred_element_type=jnp.float32) * inv_rms).astype(jnp.bfloat16) for which in range(3)])
    proj_float = proj.astype(jnp.float32)
    padded = jnp.pad(proj_float, ((0, 0), (taps - 1, 0), (0, 0)))
    conv = jnp.zeros_like(proj_float)
    for tap in range(taps):
        conv = conv + short_weight[:, tap][:, None, :] * padded[:, taps - 1 - tap:taps - 1 - tap + seq_total, :]
    query = conv[0]
    product = conv[1] * conv[2]
    poles = jnp.exp(log_decay)

    def advance(state, row):
        state = poles * state + row[None, :]
        return (state, lax.optimization_barrier(jnp.sum(residue * state, axis=0)))
    _, long_conv = lax.scan(advance, jnp.zeros(log_decay.shape, jnp.float32), product)
    gated = (query * (long_conv + skip[None, :] * product)).astype(jnp.bfloat16)
    return (tok_float + jnp.dot(gated, out_weight, preferred_element_type=jnp.float32)).astype(jnp.bfloat16)
```

```python
import functools

import jax
import jax.numpy as jnp
from jax import lax
from jax.experimental import pallas as pl
from jax.experimental.pallas import tpu as pltpu
from jax.sharding import PartitionSpec as P

EPSILON = 1e-06
LANES = 128
MIB = 1024 * 1024


def from_behind(block, axis, distance):
    count = lax.axis_size(axis)
    route = [(i - distance, i) for i in range(count) if i - distance >= 0]
    return lax.ppermute(block, axis, route)


def proj_kernel(width, x_ref, gain_ref, w_ref, out_ref, scaled_ref, acc_ref, sq_ref):
    feat, step = pl.program_id(0), pl.program_id(1)
    depth = x_ref.shape[1]
    here = pl.ds(pl.multiple_of(step * depth, depth), depth)

    @pl.when(feat == 0)
    def _():
        x = x_ref[...].astype(jnp.float32)
        part = jnp.sum(x * x, axis=1, keepdims=True)

        @pl.when(step == 0)
        def _():
            sq_ref[...] = part

        @pl.when(step > 0)
        def _():
            sq_ref[...] += part

        scaled_ref[:, here] = (x * gain_ref[...]).astype(jnp.bfloat16)

    part = jnp.dot(scaled_ref[:, here], w_ref[0], preferred_element_type=jnp.float32)

    @pl.when(step == 0)
    def _():
        acc_ref[...] = part

    @pl.when(step > 0)
    def _():
        acc_ref[...] += part

    @pl.when(step == pl.num_programs(1) - 1)
    def _():
        inv_rms = lax.rsqrt(sq_ref[...] / width + EPSILON)
        for g in range(out_ref.shape[2]):
            cols = acc_ref[:, g * LANES : (g + 1) * LANES] * inv_rms
            out_ref[0, :, g, :] = cols.astype(jnp.bfloat16).astype(jnp.float32)


def project(tokens, gain, in_weight):
    rows, width = tokens.shape
    chans = in_weight.shape[2]
    depth = min(1024, width)
    groups = chans // LANES
    steps = width // depth
    return pl.pallas_call(
        functools.partial(proj_kernel, width),
        grid=(3, steps),
        in_specs=[
            pl.BlockSpec((rows, depth), lambda i, k: (0, jnp.where(i == 0, k, steps - 1))),
            pl.BlockSpec((1, depth), lambda i, k: (0, jnp.where(i == 0, k, steps - 1))),
            pl.BlockSpec((1, depth, chans), lambda i, k: (i, k, 0)),
        ],
        out_specs=pl.BlockSpec((1, rows, groups, LANES), lambda i, k: (i, 0, 0, 0)),
        out_shape=jax.ShapeDtypeStruct((3, rows, groups, LANES), jnp.float32),
        scratch_shapes=[
            pltpu.VMEM((rows, width), jnp.bfloat16),
            pltpu.VMEM((rows, chans), jnp.float32),
            pltpu.VMEM((rows, 1), jnp.float32),
        ],
        compiler_params=pltpu.CompilerParams(vmem_limit_bytes=48 * MIB),
        cost_estimate=pl.CostEstimate(
            flops=2 * rows * width * 3 * chans,
            bytes_accessed=2 * 3 * width * chans + 2 * rows * width + 12 * rows * chans,
            transcendentals=0,
        ),
        name="project",
    )(tokens, gain[None, :], in_weight)


def tree_sum(terms):
    while len(terms) > 1:
        pairs = [terms[i] + terms[i + 1] for i in range(0, len(terms) - 1, 2)]
        terms = pairs + terms[len(pairs) * 2 :]
    return terms[0]


def mix_kernel(proj_ref, rim_ref, taps_ref, decay_ref, res_ref, skip_ref, q_ref, base_ref, end_ref, win_ref, state_ref):
    step = pl.program_id(0)
    rows = proj_ref.shape[1]
    tap_count = taps_ref.shape[1]
    poles = decay_ref.shape[0]
    keep = rim_ref.shape[1]

    @pl.when(step == 0)
    def _():
        win_ref[:, :keep] = rim_ref[...]
        state_ref[...] = jnp.zeros_like(state_ref)

    win_ref[:, keep:] = proj_ref[...]
    decay = [jnp.exp(decay_ref[n]) for n in range(poles)]
    unroll = 8

    def body(blk, state):
        state = list(state)
        first = blk * unroll
        conv = []
        for i in range(3):
            taps = [taps_ref[i, j] for j in range(tap_count)]
            held = [win_ref[i, first + keep - (tap_count - 1) + r] for r in range(unroll + tap_count - 1)]
            conv.append(
                [
                    functools.reduce(
                        lambda a, b: a + b, [taps[j] * held[r + tap_count - 1 - j] for j in range(tap_count)]
                    )
                    for r in range(unroll)
                ]
            )
        for r in range(unroll):
            query, product = conv[0][r], conv[1][r] * conv[2][r]
            terms = [skip_ref[0] * product]
            for n in range(poles):
                state[n] = decay[n] * state[n] + product
                terms.append(res_ref[n] * state[n])
            q_ref[first + r] = query
            base_ref[first + r] = query * tree_sum(terms)
        return tuple(state)

    state = lax.fori_loop(0, rows // unroll, body, tuple(state_ref[n] for n in range(poles)))
    for n in range(poles):
        state_ref[n] = state[n]
    win_ref[:, :keep] = win_ref[:, rows:]

    @pl.when(step == pl.num_programs(0) - 1)
    def _():
        for n in range(poles):
            end_ref[n] = state[n]


def mix(proj, rim, taps, log_decay, residue, skip):
    rows, groups = proj.shape[1:3]
    tap_count, poles = taps.shape[1], log_decay.shape[0]
    keep = rim.shape[1]
    blk = min(128, rows)
    whole = lambda *shape: pl.BlockSpec(shape, lambda t: (0,) * len(shape))
    row_spec = pl.BlockSpec((blk, groups, LANES), lambda t: (t, 0, 0))
    return pl.pallas_call(
        mix_kernel,
        grid=(rows // blk,),
        in_specs=[
            pl.BlockSpec((3, blk, groups, LANES), lambda t: (0, t, 0, 0)),
            whole(3, keep, groups, LANES),
            whole(3, tap_count, groups, LANES),
            whole(poles, groups, LANES),
            whole(poles, groups, LANES),
            whole(1, groups, LANES),
        ],
        out_specs=[row_spec, row_spec, whole(poles, groups, LANES)],
        out_shape=[
            jax.ShapeDtypeStruct((rows, groups, LANES), jnp.float32),
            jax.ShapeDtypeStruct((rows, groups, LANES), jnp.float32),
            jax.ShapeDtypeStruct((poles, groups, LANES), jnp.float32),
        ],
        scratch_shapes=[
            pltpu.VMEM((3, keep + blk, groups, LANES), jnp.float32),
            pltpu.VMEM((poles, groups, LANES), jnp.float32),
        ],
        compiler_params=pltpu.CompilerParams(vmem_limit_bytes=48 * MIB),
        cost_estimate=pl.CostEstimate(
            flops=110 * rows * groups * LANES, bytes_accessed=20 * rows * groups * LANES, transcendentals=0
        ),
        name="mix",
    )(proj, rim, taps, log_decay, residue, skip)


def carry_kernel(q_ref, base_ref, state_ref, decay_ref, res_ref, out_ref, coef_ref, row_ref):
    step = pl.program_id(0)
    rows, groups = q_ref.shape[:2]
    poles = decay_ref.shape[0]
    decay = [jnp.exp(decay_ref[n]) for n in range(poles)]

    @pl.when(step == 0)
    def _():
        for n in range(poles):
            coef_ref[n] = res_ref[n] * (decay[n] * state_ref[n])

    unroll = 8

    def body(blk, coef):
        coef = list(coef)
        for r in range(unroll):
            t = blk * unroll + r
            row_ref[t] = base_ref[t] + q_ref[t] * tree_sum(list(coef))
            for n in range(poles):
                coef[n] = decay[n] * coef[n]
        return tuple(coef)

    coef = lax.fori_loop(0, rows // unroll, body, tuple(coef_ref[n] for n in range(poles)))
    for n in range(poles):
        coef_ref[n] = coef[n]
    for g in range(groups):
        out_ref[:, g * LANES : (g + 1) * LANES] = row_ref[:, g, :].astype(jnp.bfloat16)


def carry(query, base, state, log_decay, residue):
    rows, groups = query.shape[:2]
    poles = log_decay.shape[0]
    blk = min(128, rows)
    whole = lambda *shape: pl.BlockSpec(shape, lambda t: (0,) * len(shape))
    row_spec = pl.BlockSpec((blk, groups, LANES), lambda t: (t, 0, 0))
    return pl.pallas_call(
        carry_kernel,
        grid=(rows // blk,),
        in_specs=[row_spec, row_spec] + [whole(poles, groups, LANES)] * 3,
        out_specs=pl.BlockSpec((blk, groups * LANES), lambda t: (t, 0)),
        out_shape=jax.ShapeDtypeStruct((rows, groups * LANES), jnp.bfloat16),
        scratch_shapes=[
            pltpu.VMEM((poles, groups, LANES), jnp.float32),
            pltpu.VMEM((blk, groups, LANES), jnp.float32),
        ],
        compiler_params=pltpu.CompilerParams(vmem_limit_bytes=48 * MIB),
        cost_estimate=pl.CostEstimate(
            flops=40 * rows * groups * LANES, bytes_accessed=10 * rows * groups * LANES, transcendentals=0
        ),
        name="carry",
    )(query, base, state, log_decay, residue)


def per_device(tokens, norm_gain, in_weight, short_weight, log_decay, residue, skip, out_weight):
    rows, chans = tokens.shape
    groups = chans // LANES
    by_lane = lambda a: a.reshape(a.shape[:-1] + (groups, LANES))
    taps, log_decay, residue = by_lane(short_weight), by_lane(log_decay), by_lane(residue)
    skip = by_lane(skip[None, :])

    gathered = lax.all_gather(tokens, "chan", axis=1, tiled=True)
    proj = project(gathered, norm_gain, in_weight)
    rim = from_behind(proj[:, rows - 8 :], "seq", 1)
    query, base, end = mix(proj, rim, taps, log_decay, residue, skip)
    shard_decay = jnp.exp(rows * log_decay)
    state, passing = jnp.zeros_like(end), end
    for _ in range(lax.axis_size("seq") - 1):
        passing = from_behind(passing, "seq", 1)
        state = state + passing
        passing = passing * shard_decay
    gated = carry(query, base, state, log_decay, residue)
    partial = jnp.dot(gated, out_weight, preferred_element_type=jnp.float32)
    branch = lax.psum_scatter(partial.astype(jnp.bfloat16), "chan", scatter_dimension=1, tiled=True)
    return (tokens.astype(jnp.float32) + branch.astype(jnp.float32)).astype(jnp.bfloat16)


def solution(mesh):
    return jax.shard_map(
        per_device,
        mesh=mesh,
        in_specs=(
            P(("groups", "seq"), "chan"),
            P(),
            P(None, None, "chan"),
            P(None, None, "chan"),
            P(None, "chan"),
            P(None, "chan"),
            P("chan"),
            P("chan", None),
        ),
        out_specs=P(("groups", "seq"), "chan"),
        check_vma=False,
    )
```

```python
import functools

import jax
import jax.numpy as jnp
from jax import lax
from jax.experimental import pallas as pl
from jax.experimental.pallas import tpu as pltpu
from jax.sharding import PartitionSpec as P

EPSILON = 1e-06
LANES = 128
MIB = 1024 * 1024


def from_behind(block, axis, distance):
    count = lax.axis_size(axis)
    route = [(i - distance, i) for i in range(count) if i - distance >= 0]
    return lax.ppermute(block, axis, route)


def proj_kernel(width, x_ref, gain_ref, w_ref, out_ref, scaled_ref, acc_ref, sq_ref):
    feat, step = pl.program_id(0), pl.program_id(1)
    depth = x_ref.shape[1]
    here = pl.ds(pl.multiple_of(step * depth, depth), depth)

    @pl.when(feat == 0)
    def _():
        x = x_ref[...].astype(jnp.float32)
        part = jnp.sum(x * x, axis=1, keepdims=True)

        @pl.when(step == 0)
        def _():
            sq_ref[...] = part

        @pl.when(step > 0)
        def _():
            sq_ref[...] += part

        scaled_ref[:, here] = (x * gain_ref[...]).astype(jnp.bfloat16)

    part = jnp.dot(scaled_ref[:, here], w_ref[0], preferred_element_type=jnp.float32)

    @pl.when(step == 0)
    def _():
        acc_ref[...] = part

    @pl.when(step > 0)
    def _():
        acc_ref[...] += part

    @pl.when(step == pl.num_programs(1) - 1)
    def _():
        inv_rms = lax.rsqrt(sq_ref[...] / width + EPSILON)
        for g in range(out_ref.shape[2]):
            cols = acc_ref[:, g * LANES : (g + 1) * LANES] * inv_rms
            out_ref[0, :, g, :] = cols.astype(jnp.bfloat16).astype(jnp.float32)


def project(tokens, gain, in_weight):
    rows, width = tokens.shape
    chans = in_weight.shape[2]
    depth = min(1024, width)
    groups = chans // LANES
    steps = width // depth
    return pl.pallas_call(
        functools.partial(proj_kernel, width),
        grid=(3, steps),
        in_specs=[
            pl.BlockSpec((rows, depth), lambda i, k: (0, jnp.where(i == 0, k, steps - 1))),
            pl.BlockSpec((1, depth), lambda i, k: (0, jnp.where(i == 0, k, steps - 1))),
            pl.BlockSpec((1, depth, chans), lambda i, k: (i, k, 0)),
        ],
        out_specs=pl.BlockSpec((1, rows, groups, LANES), lambda i, k: (i, 0, 0, 0)),
        out_shape=jax.ShapeDtypeStruct((3, rows, groups, LANES), jnp.float32),
        scratch_shapes=[
            pltpu.VMEM((rows, width), jnp.bfloat16),
            pltpu.VMEM((rows, chans), jnp.float32),
            pltpu.VMEM((rows, 1), jnp.float32),
        ],
        compiler_params=pltpu.CompilerParams(vmem_limit_bytes=48 * MIB),
        cost_estimate=pl.CostEstimate(
            flops=2 * rows * width * 3 * chans,
            bytes_accessed=2 * 3 * width * chans + 2 * rows * width + 12 * rows * chans,
            transcendentals=0,
        ),
        name="project",
    )(tokens, gain[None, :], in_weight)


def tree_sum(terms):
    while len(terms) > 1:
        pairs = [terms[i] + terms[i + 1] for i in range(0, len(terms) - 1, 2)]
        terms = pairs + terms[len(pairs) * 2 :]
    return terms[0]


def accumulate_kernel(count, width, first, last, place_ref, *refs):
    chunk_refs, refs = refs[:count], refs[count:]
    gain_ref, w_ref, refs = refs[0], refs[1], refs[2:]
    if not first:
        held_ref, held_sq_ref, refs = refs[0], refs[1], refs[2:]
    if last:
        out_ref, scaled_ref, acc_ref, sq_ref = refs
    else:
        acc_ref, sq_ref, scaled_ref = refs
    feat, step = pl.program_id(0), pl.program_id(1)

    for j in range(count):

        @pl.when((feat == 0) & (step == j))
        def _():
            x = chunk_refs[j][...].astype(jnp.float32)
            parts = [x[:, g : g + LANES] * x[:, g : g + LANES] for g in range(0, x.shape[1], LANES)]
            part = tree_sum(parts)
            if j > 0:
                sq_ref[...] += part
            elif first:
                sq_ref[...] = part
            else:
                sq_ref[...] = held_sq_ref[...] + part
            scaled_ref[j] = (x * gain_ref[0]).astype(jnp.bfloat16)

    part = jnp.dot(scaled_ref[step], w_ref[0], preferred_element_type=jnp.float32)
    acc = acc_ref if last else acc_ref.at[0]

    @pl.when(step == 0)
    def _():
        acc[...] = part if first else held_ref[0] + part

    if count > 1:

        @pl.when(step > 0)
        def _():
            acc[...] += part

    if last:

        @pl.when(step == count - 1)
        def _():
            total = jnp.sum(sq_ref[...], axis=1, keepdims=True)
            inv_rms = lax.rsqrt(total / width + EPSILON)
            for g in range(out_ref.shape[2]):
                cols = acc[:, g * LANES : (g + 1) * LANES] * inv_rms
                out_ref[0, :, g, :] = cols.astype(jnp.bfloat16).astype(jnp.float32)


def accumulate(chunks, places, gain, in_weight, held=None, last=False):
    count, (rows, depth) = len(chunks), chunks[0].shape
    width, chans = in_weight.shape[1:]
    groups = chans // LANES
    first = held is None
    feat_spec = pl.BlockSpec((1, rows, chans), lambda i, k, p: (i, 0, 0))
    sq_spec = pl.BlockSpec((rows, LANES), lambda i, k, p: (0, 0))
    in_specs = [pl.BlockSpec((rows, depth), lambda i, k, p: (0, 0))] * count + [
        pl.BlockSpec((1, 1, depth), lambda i, k, p: (p[jnp.where(i == 0, k, count - 1)], 0, 0)),
        pl.BlockSpec((1, depth, chans), lambda i, k, p: (i, p[k], 0)),
    ]
    scratch = [pltpu.VMEM((count, rows, depth), jnp.bfloat16)]
    if last:
        out_specs = pl.BlockSpec((1, rows, groups, LANES), lambda i, k, p: (i, 0, 0, 0))
        out_shape = jax.ShapeDtypeStruct((3, rows, groups, LANES), jnp.float32)
        scratch += [pltpu.VMEM((rows, chans), jnp.float32), pltpu.VMEM((rows, LANES), jnp.float32)]
    else:
        out_specs = [feat_spec, sq_spec]
        out_shape = [
            jax.ShapeDtypeStruct((3, rows, chans), jnp.float32),
            jax.ShapeDtypeStruct((rows, LANES), jnp.float32),
        ]
    extra, aliases = (), {}
    if not first:
        in_specs += [feat_spec, sq_spec]
        extra = tuple(held)
        if not last:
            aliases = {count + 3: 0, count + 4: 1}
    return pl.pallas_call(
        functools.partial(accumulate_kernel, count, width, first, last),
        grid_spec=pltpu.PrefetchScalarGridSpec(
            num_scalar_prefetch=1,
            grid=(3, count),
            in_specs=in_specs,
            out_specs=out_specs,
            scratch_shapes=scratch,
        ),
        out_shape=out_shape,
        input_output_aliases=aliases,
        compiler_params=pltpu.CompilerParams(vmem_limit_bytes=48 * MIB),
        cost_estimate=pl.CostEstimate(
            flops=2 * rows * depth * count * 3 * chans,
            bytes_accessed=6 * depth * count * chans + 24 * rows * chans,
            transcendentals=0,
        ),
        name="accumulate",
    )(jnp.stack(places).astype(jnp.int32), *chunks, gain.reshape(-1, 1, depth), in_weight, *extra)


def piece_kernel(place_ref, gated_ref, w_ref, *refs):
    total = jnp.dot(gated_ref[...], w_ref[...], preferred_element_type=jnp.float32)
    for ref in refs[:-1]:
        total = total + ref[...].astype(jnp.float32)
    refs[-1][...] = total.astype(jnp.bfloat16)


def piece(gated, out_weight, place, *terms):
    rows, chans = gated.shape
    tile = min(512, chans)
    tiles = chans // tile
    spec = pl.BlockSpec((rows, tile), lambda t, p: (0, t))
    return pl.pallas_call(
        piece_kernel,
        grid_spec=pltpu.PrefetchScalarGridSpec(
            num_scalar_prefetch=1,
            grid=(tiles,),
            in_specs=[
                pl.BlockSpec((rows, chans), lambda t, p: (0, 0)),
                pl.BlockSpec((chans, tile), lambda t, p: (0, p[0] * tiles + t)),
            ]
            + [spec] * len(terms),
            out_specs=spec,
        ),
        out_shape=jax.ShapeDtypeStruct((rows, chans), jnp.bfloat16),
        compiler_params=pltpu.CompilerParams(vmem_limit_bytes=48 * MIB),
        cost_estimate=pl.CostEstimate(
            flops=2 * rows * chans * chans,
            bytes_accessed=2 * chans * chans + 2 * rows * chans * (2 + len(terms)),
            transcendentals=0,
        ),
        name="piece",
    )(place.astype(jnp.int32)[None], gated, out_weight, *terms)


def along_line(block, pairs):
    return lax.ppermute(block, "chan", [(2 * a + y, 2 * b + y) for a, b in pairs for y in (0, 1)])


def across(block):
    count = lax.axis_size("chan")
    return lax.ppermute(block, "chan", [(c, c ^ 1) for c in range(count)])


def after(block, *earlier):
    return lax.optimization_barrier((block,) + earlier)[0]


PAIRS = [(0, 1), (1, 0), (2, 3), (3, 2)]
MIDDLE = [(1, 2), (2, 1)]
OUTWARD = [(1, 0), (2, 3)]
INWARD = [(0, 1), (3, 2)]


def gather_and_project(tokens, gain, in_weight):
    me = lax.axis_index("chan")
    mine = lambda k: me ^ (2 * k)
    other = lambda k: me ^ (2 * k + 1)
    at_end = (me < 2) | (me >= 6)
    next_one = along_line(tokens, PAIRS)
    middle = along_line(tokens, MIDDLE)
    own_over = across(tokens)
    held = accumulate([tokens], [me], gain, in_weight)
    next_over = across(next_one)
    second_out = along_line(middle, OUTWARD)
    second_mid = along_line(next_one, MIDDLE)
    held = accumulate([own_over, next_one], [other(0), mine(1)], gain, in_weight, held)
    second = jnp.where(at_end, second_out, second_mid)
    second_over = across(second)
    third_out = along_line(second_mid, OUTWARD)
    held = accumulate([next_over, second], [other(1), mine(2)], gain, in_weight, held)
    third = jnp.where(at_end, third_out, middle)
    third_over = across(third)
    held = accumulate([second_over, third], [other(2), mine(3)], gain, in_weight, held)
    return accumulate([third_over], [other(3)], gain, in_weight, held, last=True)


def project_and_reduce(gated, out_weight, tokens):
    me = lax.axis_index("chan")
    at_mine = lambda k, *terms: piece(gated, out_weight, me ^ (2 * k), *terms)
    at_other = lambda k: piece(gated, out_weight, me ^ (2 * k + 1))
    third_over = across(at_other(3))
    third = at_mine(3, third_over)
    third_in = along_line(third, INWARD)
    second_over = across(after(at_other(2), third_over))
    second = at_mine(2, second_over, third_in)
    second_in = along_line(second, INWARD)
    second_mid = along_line(second, MIDDLE)
    next_over = across(after(at_other(1), second_over))
    next_one = at_mine(1, next_over, second_mid)
    next_in = along_line(next_one, PAIRS)
    middle = (third.astype(jnp.float32) + second_in.astype(jnp.float32)).astype(jnp.bfloat16)
    middle_in = along_line(middle, MIDDLE)
    own_over = across(after(at_other(0), next_over))
    return at_mine(0, own_over, next_in, middle_in, tokens)


def mix_kernel(proj_ref, rim_ref, taps_ref, decay_ref, res_ref, skip_ref, q_ref, base_ref, end_ref, win_ref, state_ref):
    step = pl.program_id(0)
    rows = proj_ref.shape[1]
    tap_count = taps_ref.shape[1]
    poles = decay_ref.shape[0]
    keep = rim_ref.shape[1]

    @pl.when(step == 0)
    def _():
        win_ref[:, :keep] = rim_ref[...]
        state_ref[...] = jnp.zeros_like(state_ref)

    win_ref[:, keep:] = proj_ref[...]
    decay = [jnp.exp(decay_ref[n]) for n in range(poles)]
    unroll = 8

    def body(blk, state):
        state = list(state)
        first = blk * unroll
        conv = []
        for i in range(3):
            taps = [taps_ref[i, j] for j in range(tap_count)]
            held = [win_ref[i, first + keep - (tap_count - 1) + r] for r in range(unroll + tap_count - 1)]
            conv.append(
                [
                    functools.reduce(
                        lambda a, b: a + b, [taps[j] * held[r + tap_count - 1 - j] for j in range(tap_count)]
                    )
                    for r in range(unroll)
                ]
            )
        for r in range(unroll):
            query, product = conv[0][r], conv[1][r] * conv[2][r]
            terms = [skip_ref[0] * product]
            for n in range(poles):
                state[n] = decay[n] * state[n] + product
                terms.append(res_ref[n] * state[n])
            q_ref[first + r] = query
            base_ref[first + r] = query * tree_sum(terms)
        return tuple(state)

    state = lax.fori_loop(0, rows // unroll, body, tuple(state_ref[n] for n in range(poles)))
    for n in range(poles):
        state_ref[n] = state[n]
    win_ref[:, :keep] = win_ref[:, rows:]

    @pl.when(step == pl.num_programs(0) - 1)
    def _():
        for n in range(poles):
            end_ref[n] = state[n]


def mix(proj, rim, taps, log_decay, residue, skip):
    rows, groups = proj.shape[1:3]
    tap_count, poles = taps.shape[1], log_decay.shape[0]
    keep = rim.shape[1]
    blk = min(128, rows)
    whole = lambda *shape: pl.BlockSpec(shape, lambda t: (0,) * len(shape))
    row_spec = pl.BlockSpec((blk, groups, LANES), lambda t: (t, 0, 0))
    return pl.pallas_call(
        mix_kernel,
        grid=(rows // blk,),
        in_specs=[
            pl.BlockSpec((3, blk, groups, LANES), lambda t: (0, t, 0, 0)),
            whole(3, keep, groups, LANES),
            whole(3, tap_count, groups, LANES),
            whole(poles, groups, LANES),
            whole(poles, groups, LANES),
            whole(1, groups, LANES),
        ],
        out_specs=[row_spec, row_spec, whole(poles, groups, LANES)],
        out_shape=[
            jax.ShapeDtypeStruct((rows, groups, LANES), jnp.float32),
            jax.ShapeDtypeStruct((rows, groups, LANES), jnp.float32),
            jax.ShapeDtypeStruct((poles, groups, LANES), jnp.float32),
        ],
        scratch_shapes=[
            pltpu.VMEM((3, keep + blk, groups, LANES), jnp.float32),
            pltpu.VMEM((poles, groups, LANES), jnp.float32),
        ],
        compiler_params=pltpu.CompilerParams(vmem_limit_bytes=48 * MIB),
        cost_estimate=pl.CostEstimate(
            flops=110 * rows * groups * LANES, bytes_accessed=20 * rows * groups * LANES, transcendentals=0
        ),
        name="mix",
    )(proj, rim, taps, log_decay, residue, skip)


def carry_kernel(q_ref, base_ref, state_ref, decay_ref, res_ref, out_ref, coef_ref, row_ref):
    step = pl.program_id(0)
    rows, groups = q_ref.shape[:2]
    poles = decay_ref.shape[0]
    decay = [jnp.exp(decay_ref[n]) for n in range(poles)]

    @pl.when(step == 0)
    def _():
        for n in range(poles):
            coef_ref[n] = res_ref[n] * (decay[n] * state_ref[n])

    unroll = 8

    def body(blk, coef):
        coef = list(coef)
        for r in range(unroll):
            t = blk * unroll + r
            row_ref[t] = base_ref[t] + q_ref[t] * tree_sum(list(coef))
            for n in range(poles):
                coef[n] = decay[n] * coef[n]
        return tuple(coef)

    coef = lax.fori_loop(0, rows // unroll, body, tuple(coef_ref[n] for n in range(poles)))
    for n in range(poles):
        coef_ref[n] = coef[n]
    for g in range(groups):
        out_ref[:, g * LANES : (g + 1) * LANES] = row_ref[:, g, :].astype(jnp.bfloat16)


def carry(query, base, state, log_decay, residue):
    rows, groups = query.shape[:2]
    poles = log_decay.shape[0]
    blk = min(128, rows)
    whole = lambda *shape: pl.BlockSpec(shape, lambda t: (0,) * len(shape))
    row_spec = pl.BlockSpec((blk, groups, LANES), lambda t: (t, 0, 0))
    return pl.pallas_call(
        carry_kernel,
        grid=(rows // blk,),
        in_specs=[row_spec, row_spec] + [whole(poles, groups, LANES)] * 3,
        out_specs=pl.BlockSpec((blk, groups * LANES), lambda t: (t, 0)),
        out_shape=jax.ShapeDtypeStruct((rows, groups * LANES), jnp.bfloat16),
        scratch_shapes=[
            pltpu.VMEM((poles, groups, LANES), jnp.float32),
            pltpu.VMEM((blk, groups, LANES), jnp.float32),
        ],
        compiler_params=pltpu.CompilerParams(vmem_limit_bytes=48 * MIB),
        cost_estimate=pl.CostEstimate(
            flops=40 * rows * groups * LANES, bytes_accessed=10 * rows * groups * LANES, transcendentals=0
        ),
        name="carry",
    )(query, base, state, log_decay, residue)


def per_device(tokens, norm_gain, in_weight, short_weight, log_decay, residue, skip, out_weight):
    rows, chans = tokens.shape
    groups = chans // LANES
    by_lane = lambda a: a.reshape(a.shape[:-1] + (groups, LANES))
    taps, log_decay, residue = by_lane(short_weight), by_lane(log_decay), by_lane(residue)
    skip = by_lane(skip[None, :])

    paired_line = lax.axis_size("chan") == 8
    if paired_line:
        proj = gather_and_project(tokens, norm_gain, in_weight)
    else:
        gathered = lax.all_gather(tokens, "chan", axis=1, tiled=True)
        proj = project(gathered, norm_gain, in_weight)
    rim = from_behind(proj[:, rows - 8 :], "seq", 1)
    query, base, end = mix(proj, rim, taps, log_decay, residue, skip)
    shard_decay = jnp.exp(rows * log_decay)
    state, passing = jnp.zeros_like(end), end
    for _ in range(lax.axis_size("seq") - 1):
        passing = from_behind(passing, "seq", 1)
        state = state + passing
        passing = passing * shard_decay
    gated = carry(query, base, state, log_decay, residue)
    if paired_line:
        return project_and_reduce(gated, out_weight, tokens)
    partial = jnp.dot(gated, out_weight, preferred_element_type=jnp.float32)
    branch = lax.psum_scatter(partial.astype(jnp.bfloat16), "chan", scatter_dimension=1, tiled=True)
    return (tokens.astype(jnp.float32) + branch.astype(jnp.float32)).astype(jnp.bfloat16)


def solution(mesh):
    return jax.shard_map(
        per_device,
        mesh=mesh,
        in_specs=(
            P(("groups", "seq"), "chan"),
            P(),
            P(None, None, "chan"),
            P(None, None, "chan"),
            P(None, "chan"),
            P(None, "chan"),
            P("chan"),
            P("chan", None),
        ),
        out_specs=P(("groups", "seq"), "chan"),
        check_vma=False,
    )
```

```python
import functools

import jax
import jax.numpy as jnp
from jax import lax
from jax.experimental import pallas as pl
from jax.experimental.pallas import tpu as pltpu
from jax.sharding import PartitionSpec as P

EPSILON = 1e-06
LANES = 128
MIB = 1024 * 1024


def from_behind(block, axis, distance):
    count = lax.axis_size(axis)
    route = [(i - distance, i) for i in range(count) if i - distance >= 0]
    return lax.ppermute(block, axis, route)


def tree_sum(terms):
    while len(terms) > 1:
        pairs = [terms[i] + terms[i + 1] for i in range(0, len(terms) - 1, 2)]
        terms = pairs + terms[len(pairs) * 2 :]
    return terms[0]


def piece_kernel(place_ref, gated_ref, w_ref, out_ref):
    total = jnp.dot(gated_ref[...], w_ref[...], preferred_element_type=jnp.float32)
    out_ref[...] = total.astype(out_ref.dtype)


def piece(gated, out_weight, place, width, dtype):
    rows, chans = gated.shape
    tile = min(256, width)
    tiles = width // tile
    return pl.pallas_call(
        piece_kernel,
        grid_spec=pltpu.PrefetchScalarGridSpec(
            num_scalar_prefetch=1,
            grid=(tiles,),
            in_specs=[
                pl.BlockSpec((rows, chans), lambda t, p: (0, 0)),
                pl.BlockSpec((chans, tile), lambda t, p: (0, p[0] * tiles + t)),
            ],
            out_specs=pl.BlockSpec((rows, tile), lambda t, p: (0, t)),
        ),
        out_shape=jax.ShapeDtypeStruct((rows, width), dtype),
        compiler_params=pltpu.CompilerParams(vmem_limit_bytes=24 * MIB),
        cost_estimate=pl.CostEstimate(
            flops=2 * rows * chans * width,
            bytes_accessed=2 * chans * width + 2 * rows * chans + 4 * rows * width,
            transcendentals=0,
        ),
        name="piece",
    )(place.astype(jnp.int32)[None], gated, out_weight)


def along_line(block, pairs):
    return lax.ppermute(block, "chan", [(2 * a + y, 2 * b + y) for a, b in pairs for y in (0, 1)])


def across(block, *earlier):
    count = lax.axis_size("chan")
    if earlier:
        block = lax.optimization_barrier((block,) + earlier)[0]
    return lax.ppermute(block, "chan", [(c, c ^ 1) for c in range(count)])


def total(*terms):
    return functools.reduce(lambda a, b: a + b, [t.astype(jnp.float32) for t in terms])


PAIRS = [(0, 1), (1, 0), (2, 3), (3, 2)]
MIDDLE = [(1, 2), (2, 1)]
OUTWARD = [(1, 0), (2, 3)]
INWARD = [(0, 1), (3, 2)]


def gather_and_project(tokens, gain, in_weight):
    me = lax.axis_index("chan")
    depth = tokens.shape[1]
    half = depth // 2
    at_end = (me < 2) | (me >= 6)
    acc = squares = None

    def add(chunk, shard, start=0):
        nonlocal acc, squares
        first, deep = shard * depth + start, chunk.shape[1]
        x = chunk.astype(jnp.float32)
        scaled = (x * lax.dynamic_slice_in_dim(gain, first, deep)).astype(jnp.bfloat16)
        w = lax.dynamic_slice_in_dim(in_weight, first, deep, axis=1)
        part = jnp.einsum("td,kdc->ktc", scaled, w, preferred_element_type=jnp.float32)
        square = jnp.sum(x * x, axis=1, keepdims=True)
        acc = part if acc is None else lax.optimization_barrier(acc + part)
        squares = square if squares is None else squares + square

    own_over = across(tokens)
    next_one = along_line(tokens, PAIRS)
    middle = along_line(tokens, MIDDLE)
    add(tokens, me)
    next_over = across(next_one, own_over)
    second_out = along_line(middle, OUTWARD)
    second_mid = along_line(next_one, MIDDLE)
    add(own_over, me ^ 1)
    add(next_one, me ^ 2)
    second = jnp.where(at_end, second_out, second_mid)
    second_over = across(second, next_over)
    third_out = along_line(second_mid, OUTWARD)
    add(next_over, me ^ 3)
    add(second, me ^ 4)
    third = jnp.where(at_end, third_out, middle)
    third_over = across(third[:, :half], second_over)
    rest_out = along_line(second_over[:, half:], OUTWARD)
    rest_mid = along_line(lax.optimization_barrier((own_over[:, half:], second_mid))[0], MIDDLE)
    add(second_over, me ^ 5)
    add(third, me ^ 6)
    add(jnp.where(at_end, rest_out, rest_mid), me ^ 7, half)
    add(third_over, me ^ 7)
    return acc, squares


def project_and_reduce(gated, out_weight, tokens):
    me = lax.axis_index("chan")
    half = tokens.shape[1] // 2
    send = lambda k, h: piece(gated, out_weight, (me ^ (2 * k + 1)) * 2 + h, half, jnp.bfloat16)
    keep = lambda k, h: piece(gated, out_weight, (me ^ (2 * k)) * 2 + h, half, jnp.float32)
    narrow = lambda a: a.astype(jnp.bfloat16)
    both = (0, 1)

    send_third = [send(3, h) for h in both]
    third_over = across(send_third[0])
    rest_in = along_line(send_third[1], INWARD)
    rest_mid = along_line(send_third[1], MIDDLE)
    third = [narrow(total(keep(3, 0), third_over)), piece(gated, out_weight, (me ^ 6) * 2 + 1, half, jnp.bfloat16)]
    third_in = [along_line(third[0], INWARD), along_line(third[1], INWARD)]
    send_second = [send(2, 0), narrow(total(send(2, 1), rest_in))]
    second_over = [across(send_second[h], third_over) for h in both]
    second = [narrow(total(keep(2, h), second_over[h], third_in[h])) for h in both]
    second_in = [along_line(second[h], INWARD) for h in both]
    second_mid = [along_line(second[h], MIDDLE) for h in both]
    next_over = [across(send(1, h), second_over[h]) for h in both]
    next_one = [narrow(total(keep(1, h), next_over[h], second_mid[h])) for h in both]
    next_in = [along_line(next_one[h], PAIRS) for h in both]
    middle_in = [along_line(narrow(total(third[h], second_in[h])), MIDDLE) for h in both]
    send_own = [send(0, 0), narrow(total(send(0, 1), rest_mid))]
    own_over = [across(send_own[h], next_over[h]) for h in both]
    sums = [total(keep(0, h), own_over[h], next_in[h], middle_in[h]) for h in both]
    return narrow(total(tokens, jnp.concatenate(sums, axis=1)))


def mix_kernel(
    acc_ref, rms_ref, rim_ref, taps_ref, decay_ref, res_ref, skip_ref, q_ref, base_ref, end_ref, win_ref, prod_ref, state_ref
):
    step = pl.program_id(0)
    rows = acc_ref.shape[1]
    groups = taps_ref.shape[2]
    tap_count = taps_ref.shape[1]
    poles = decay_ref.shape[0]
    keep = rim_ref.shape[1]
    unroll = 8

    @pl.when(step == 0)
    def _():
        for g in range(groups):
            win_ref[:, :keep, g, :] = rim_ref[:, :, g * LANES : (g + 1) * LANES]
        state_ref[...] = jnp.zeros_like(state_ref)

    inv_rms = rms_ref[...]
    for i in range(3):
        for g in range(groups):
            cols = acc_ref[i, :, g * LANES : (g + 1) * LANES] * inv_rms
            win_ref[i, keep:, g, :] = cols.astype(jnp.bfloat16).astype(jnp.float32)

    def convolve(blk, nothing):
        first = blk * unroll
        conv = []
        for i in range(3):
            taps = [taps_ref[i, j] for j in range(tap_count)]
            held = [win_ref[i, first + keep - (tap_count - 1) + r] for r in range(unroll + tap_count - 1)]
            conv.append(
                [
                    functools.reduce(
                        lambda a, b: a + b, [taps[j] * held[r + tap_count - 1 - j] for j in range(tap_count)]
                    )
                    for r in range(unroll)
                ]
            )
        for r in range(unroll):
            q_ref[first + r] = conv[0][r]
            prod_ref[first + r] = conv[1][r] * conv[2][r]
        return nothing

    lax.fori_loop(0, rows // unroll, convolve, 0)
    win_ref[:, :keep] = win_ref[:, rows:]
    decay = [jnp.exp(decay_ref[n]) for n in range(poles)]
    res = [res_ref[n] for n in range(poles)]
    skip = skip_ref[0]

    def recur(blk, state):
        state = list(state)
        for r in range(unroll):
            t = blk * unroll + r
            product = prod_ref[t]
            terms = [skip * product]
            for n in range(poles):
                state[n] = decay[n] * state[n] + product
                terms.append(res[n] * state[n])
            base_ref[t] = q_ref[t] * tree_sum(terms)
        return tuple(state)

    state = lax.fori_loop(0, rows // unroll, recur, tuple(state_ref[n] for n in range(poles)))
    for n in range(poles):
        state_ref[n] = state[n]

    @pl.when(step == pl.num_programs(0) - 1)
    def _():
        for n in range(poles):
            end_ref[n] = state[n]


def mix(acc, inv_rms, rim, taps, log_decay, residue, skip):
    rows, chans = acc.shape[1:]
    groups = chans // LANES
    tap_count, poles = taps.shape[1], log_decay.shape[0]
    keep = rim.shape[1]
    blk = min(128, rows)
    whole = lambda *shape: pl.BlockSpec(shape, lambda t: (0,) * len(shape))
    row_spec = pl.BlockSpec((blk, groups, LANES), lambda t: (t, 0, 0))
    return pl.pallas_call(
        mix_kernel,
        grid=(rows // blk,),
        in_specs=[
            pl.BlockSpec((3, blk, chans), lambda t: (0, t, 0)),
            pl.BlockSpec((blk, 1), lambda t: (t, 0)),
            whole(3, keep, chans),
            whole(3, tap_count, groups, LANES),
            whole(poles, groups, LANES),
            whole(poles, groups, LANES),
            whole(1, groups, LANES),
        ],
        out_specs=[row_spec, row_spec, whole(poles, groups, LANES)],
        out_shape=[
            jax.ShapeDtypeStruct((rows, groups, LANES), jnp.float32),
            jax.ShapeDtypeStruct((rows, groups, LANES), jnp.float32),
            jax.ShapeDtypeStruct((poles, groups, LANES), jnp.float32),
        ],
        scratch_shapes=[
            pltpu.VMEM((3, keep + blk, groups, LANES), jnp.float32),
            pltpu.VMEM((blk, groups, LANES), jnp.float32),
            pltpu.VMEM((poles, groups, LANES), jnp.float32),
        ],
        compiler_params=pltpu.CompilerParams(vmem_limit_bytes=32 * MIB),
        cost_estimate=pl.CostEstimate(
            flops=110 * rows * groups * LANES, bytes_accessed=20 * rows * groups * LANES, transcendentals=0
        ),
        name="mix",
    )(acc, inv_rms, rim, taps, log_decay, residue, skip)


def carry_kernel(q_ref, base_ref, state_ref, decay_ref, res_ref, out_ref, coef_ref, row_ref):
    step = pl.program_id(0)
    rows, groups = q_ref.shape[:2]
    poles = decay_ref.shape[0]
    decay = [jnp.exp(decay_ref[n]) for n in range(poles)]

    @pl.when(step == 0)
    def _():
        for n in range(poles):
            coef_ref[n] = res_ref[n] * (decay[n] * state_ref[n])

    unroll = 8

    def body(blk, coef):
        coef = list(coef)
        for r in range(unroll):
            t = blk * unroll + r
            row_ref[t] = base_ref[t] + q_ref[t] * tree_sum(list(coef))
            for n in range(poles):
                coef[n] = decay[n] * coef[n]
        return tuple(coef)

    coef = lax.fori_loop(0, rows // unroll, body, tuple(coef_ref[n] for n in range(poles)))
    for n in range(poles):
        coef_ref[n] = coef[n]
    for g in range(groups):
        out_ref[:, g * LANES : (g + 1) * LANES] = row_ref[:, g, :].astype(jnp.bfloat16)


def carry(query, base, state, log_decay, residue):
    rows, groups = query.shape[:2]
    poles = log_decay.shape[0]
    blk = min(128, rows)
    whole = lambda *shape: pl.BlockSpec(shape, lambda t: (0,) * len(shape))
    row_spec = pl.BlockSpec((blk, groups, LANES), lambda t: (t, 0, 0))
    return pl.pallas_call(
        carry_kernel,
        grid=(rows // blk,),
        in_specs=[row_spec, row_spec] + [whole(poles, groups, LANES)] * 3,
        out_specs=pl.BlockSpec((blk, groups * LANES), lambda t: (t, 0)),
        out_shape=jax.ShapeDtypeStruct((rows, groups * LANES), jnp.bfloat16),
        scratch_shapes=[
            pltpu.VMEM((poles, groups, LANES), jnp.float32),
            pltpu.VMEM((blk, groups, LANES), jnp.float32),
        ],
        compiler_params=pltpu.CompilerParams(vmem_limit_bytes=48 * MIB),
        cost_estimate=pl.CostEstimate(
            flops=40 * rows * groups * LANES, bytes_accessed=10 * rows * groups * LANES, transcendentals=0
        ),
        name="carry",
    )(query, base, state, log_decay, residue)


def per_device(tokens, norm_gain, in_weight, short_weight, log_decay, residue, skip, out_weight):
    rows, chans = tokens.shape
    groups = chans // LANES
    by_lane = lambda a: a.reshape(a.shape[:-1] + (groups, LANES))
    taps, log_decay, residue = by_lane(short_weight), by_lane(log_decay), by_lane(residue)
    skip = by_lane(skip[None, :])

    model_width, keep = norm_gain.shape[0], 8
    paired_line = lax.axis_size("chan") == 8
    if paired_line:
        acc, squares = gather_and_project(tokens, norm_gain, in_weight)
    else:
        gathered = lax.all_gather(tokens, "chan", axis=1, tiled=True).astype(jnp.float32)
        squares = jnp.sum(gathered * gathered, axis=1, keepdims=True)
        scaled = (gathered * norm_gain[None, :]).astype(jnp.bfloat16)
        acc = jnp.einsum("td,kdc->ktc", scaled, in_weight, preferred_element_type=jnp.float32)
    inv_rms = lax.rsqrt(squares / model_width + EPSILON)
    rim = (acc[:, rows - keep :] * inv_rms[None, rows - keep :]).astype(jnp.bfloat16)
    rim = from_behind(rim, "seq", 1).astype(jnp.float32)
    query, base, end = mix(acc, inv_rms, rim, taps, log_decay, residue, skip)
    shard_decay = jnp.exp(rows * log_decay)
    state, passing = jnp.zeros_like(end), end
    for _ in range(lax.axis_size("seq") - 1):
        passing = from_behind(passing, "seq", 1)
        state = state + passing
        passing = passing * shard_decay
    gated = carry(query, base, state, log_decay, residue)
    if paired_line:
        return project_and_reduce(gated, out_weight, tokens)
    partial = jnp.dot(gated, out_weight, preferred_element_type=jnp.float32)
    branch = lax.psum_scatter(partial.astype(jnp.bfloat16), "chan", scatter_dimension=1, tiled=True)
    return (tokens.astype(jnp.float32) + branch.astype(jnp.float32)).astype(jnp.bfloat16)


def solution(mesh):
    return jax.shard_map(
        per_device,
        mesh=mesh,
        in_specs=(
            P(("groups", "seq"), "chan"),
            P(),
            P(None, None, "chan"),
            P(None, None, "chan"),
            P(None, "chan"),
            P(None, "chan"),
            P("chan"),
            P("chan", None),
        ),
        out_specs=P(("groups", "seq"), "chan"),
        check_vma=False,
    )
```

```python
import functools

import jax
import jax.numpy as jnp
from jax import lax
from jax.experimental import pallas as pl
from jax.experimental.pallas import tpu as pltpu
from jax.sharding import PartitionSpec as P

EPSILON = 1e-06
LANES = 128
KEEP = 8
VMEM_LIMIT = 48 * 1024 * 1024


def from_behind(block, axis, distance):
    count = lax.axis_size(axis)
    route = [(i - distance, i) for i in range(count) if i - distance >= 0]
    return lax.ppermute(block, axis, route)


def tree_sum(terms):
    while len(terms) > 1:
        pairs = [terms[i] + terms[i + 1] for i in range(0, len(terms) - 1, 2)]
        terms = pairs + terms[len(pairs) * 2 :]
    return terms[0]


def accumulate_kernel(depths, pairs, width, first, last, place_ref, *refs):
    chunk_refs, refs = refs[: len(depths) + sum(pairs)], refs[len(depths) + sum(pairs) :]
    gain_refs, refs = refs[: len(depths)], refs[len(depths) :]
    w_refs, refs = refs[: len(depths)], refs[len(depths) :]
    if not first:
        held_ref, held_sq_ref, refs = refs[0], refs[1], refs[2:]
    if last:
        acc_ref, sq_ref, rim_ref, scaled_ref = refs
    else:
        acc_ref, sq_ref, scaled_ref = refs
    feat, col = pl.program_id(0), pl.program_id(1)

    @pl.when((feat == 0) & (col == 0))
    def _():
        square = None if first else held_sq_ref[...]
        start = at = 0
        for j, depth in enumerate(depths):
            x = chunk_refs[at][...]
            at += 1
            if pairs[j]:
                x = jnp.where(place_ref[len(depths)] == 1, x, chunk_refs[at][...])
                at += 1
            x = x.astype(jnp.float32)
            parts = [x[:, g : g + LANES] * x[:, g : g + LANES] for g in range(0, depth, LANES)]
            part = tree_sum(parts)
            square = part if square is None else square + part
            scaled_ref[:, start : start + depth] = (x * gain_refs[j][0]).astype(jnp.bfloat16)
            start += depth
        if last:
            total = jnp.sum(square, axis=1, keepdims=True)
            square = jnp.broadcast_to(lax.rsqrt(total / width + EPSILON), square.shape)
        sq_ref[...] = square

    start, part = 0, None
    for j, depth in enumerate(depths):
        one = jnp.dot(scaled_ref[:, start : start + depth], w_refs[j][0], preferred_element_type=jnp.float32)
        part = one if part is None else part + one
        start += depth
    acc_ref[0] = part if first else held_ref[0] + part
    if last:
        keep = rim_ref.shape[1]
        rows = acc_ref.shape[1]
        rim = acc_ref[0, rows - keep :, :] * sq_ref[rows - keep :, :1]
        rim_ref[0] = rim.astype(jnp.bfloat16).astype(jnp.float32)


def accumulate(chunks, places, gain, in_weight, held=None, last=False, use_first=None):
    pairs = [isinstance(c, tuple) for c in chunks]
    arrays = [a for c in chunks for a in (c if isinstance(c, tuple) else (c,))]
    depths = [(c[0] if isinstance(c, tuple) else c).shape[1] for c in chunks]
    rows = arrays[0].shape[0]
    width, chans = in_weight.shape[1:]
    tile = min(512, chans)
    first = held is None
    acc_spec = pl.BlockSpec((1, rows, tile), lambda i, c, p: (i, 0, c))
    sq_spec = pl.BlockSpec((rows, LANES), lambda i, c, p: (0, 0))
    in_specs = [pl.BlockSpec(a.shape, lambda i, c, p: (0, 0)) for a in arrays]
    in_specs += [pl.BlockSpec((1, 1, d), lambda i, c, p, j=j: (p[j], 0, 0)) for j, d in enumerate(depths)]
    in_specs += [pl.BlockSpec((1, d, tile), lambda i, c, p, j=j: (i, p[j], c)) for j, d in enumerate(depths)]
    out_specs = [acc_spec, sq_spec]
    out_shape = [
        jax.ShapeDtypeStruct((3, rows, chans), jnp.float32),
        jax.ShapeDtypeStruct((rows, LANES), jnp.float32),
    ]
    if last:
        out_specs.append(pl.BlockSpec((1, KEEP, tile), lambda i, c, p: (i, 0, c)))
        out_shape.append(jax.ShapeDtypeStruct((3, KEEP, chans), jnp.float32))
    extra, aliases = (), {}
    if not first:
        in_specs += [acc_spec, sq_spec]
        extra = tuple(held)
        base = 1 + len(arrays) + 2 * len(depths)
        aliases = {base: 0, base + 1: 1}
    scalars = list(places) + ([] if use_first is None else [use_first])
    return pl.pallas_call(
        functools.partial(accumulate_kernel, depths, pairs, width, first, last),
        grid_spec=pltpu.PrefetchScalarGridSpec(
            num_scalar_prefetch=1,
            grid=(3, chans // tile),
            in_specs=in_specs,
            out_specs=out_specs,
            scratch_shapes=[pltpu.VMEM((rows, sum(depths)), jnp.bfloat16)],
        ),
        out_shape=out_shape,
        input_output_aliases=aliases,
        compiler_params=pltpu.CompilerParams(vmem_limit_bytes=VMEM_LIMIT),
        cost_estimate=pl.CostEstimate(
            flops=rows * sum(depths) * chans,
            bytes_accessed=6 * sum(depths) * chans,
            transcendentals=0,
        ),
        name="accumulate",
    )(
        jnp.stack([jnp.asarray(n, jnp.int32) for n in scalars]),
        *arrays,
        *[gain.reshape(-1, 1, d) for d in depths],
        *[in_weight] * len(depths),
        *extra,
    )


def pieces_kernel(count, place_ref, gated_ref, w_ref, *refs):
    outs = refs[-count:]
    total = jnp.dot(gated_ref[...], w_ref[...], preferred_element_type=jnp.float32)
    for j in range(count):

        @pl.when(pl.program_id(0) == j)
        def _():
            outs[j][...] = total.astype(outs[j].dtype)


def pieces(gated, out_weight, width, wanted, *earlier):
    rows, chans = gated.shape
    count = len(wanted)
    out = pl.pallas_call(
        functools.partial(pieces_kernel, count),
        grid_spec=pltpu.PrefetchScalarGridSpec(
            num_scalar_prefetch=1,
            grid=(count,),
            in_specs=[
                pl.BlockSpec((rows, chans), lambda t, p: (0, 0)),
                pl.BlockSpec((chans, width), lambda t, p: (0, p[t])),
            ]
            + [pl.BlockSpec(memory_space=pl.ANY)] * len(earlier),
            out_specs=[pl.BlockSpec((rows, width), lambda t, p: (0, 0))] * count,
        ),
        out_shape=[jax.ShapeDtypeStruct((rows, width), dtype) for place, dtype in wanted],
        compiler_params=pltpu.CompilerParams(vmem_limit_bytes=VMEM_LIMIT),
        cost_estimate=pl.CostEstimate(
            flops=2 * rows * chans * width * count,
            bytes_accessed=(2 * chans * width + 4 * rows * width) * count + 2 * rows * chans,
            transcendentals=0,
        ),
        name="pieces",
    )(jnp.stack([place.astype(jnp.int32) for place, dtype in wanted]), gated, out_weight, *earlier)
    return list(out)


def finish_kernel(*refs):
    out_ref, half = refs[-1], refs[0].shape[1]
    count = (len(refs) - 1) // 2
    for h in range(2):
        total = refs[h * count][...].astype(jnp.float32)
        for ref in refs[h * count + 1 : (h + 1) * count]:
            total = total + ref[...].astype(jnp.float32)
        out_ref[:, h * half : (h + 1) * half] = total.astype(jnp.bfloat16)


def finish(left, right):
    rows, half = left[0].shape
    blk = min(128, rows)
    return pl.pallas_call(
        finish_kernel,
        grid=(rows // blk,),
        in_specs=[pl.BlockSpec((blk, half), lambda t: (t, 0))] * (2 * len(left)),
        out_specs=pl.BlockSpec((blk, 2 * half), lambda t: (t, 0)),
        out_shape=jax.ShapeDtypeStruct((rows, 2 * half), jnp.bfloat16),
        compiler_params=pltpu.CompilerParams(vmem_limit_bytes=VMEM_LIMIT),
        name="finish",
    )(*left, *right)


def along_line(block, pairs):
    return lax.ppermute(block, "chan", [(2 * a + y, 2 * b + y) for a, b in pairs for y in (0, 1)])


def after(block, *earlier):
    return lax.optimization_barrier((block,) + earlier)[0]


def across(block, *earlier):
    count = lax.axis_size("chan")
    if earlier:
        block = after(block, *earlier)
    return lax.ppermute(block, "chan", [(c, c ^ 1) for c in range(count)])


def total(*terms):
    return functools.reduce(lambda a, b: a + b, [t.astype(jnp.float32) for t in terms])


PAIRS = [(0, 1), (1, 0), (2, 3), (3, 2)]
MIDDLE = [(1, 2), (2, 1)]
OUTWARD = [(1, 0), (2, 3)]
INWARD = [(0, 1), (3, 2)]


def gather_and_project(tokens, gain, in_weight):
    me = lax.axis_index("chan")
    half = tokens.shape[1] // 2
    at_end = (me < 2) | (me >= 6)
    own_over = across(tokens)
    next_one = along_line(tokens, PAIRS)
    middle = along_line(tokens, MIDDLE)
    held = accumulate([tokens], [me], gain, in_weight)
    next_over = across(next_one, own_over, held[1])
    second_out = along_line(after(middle, held[1]), OUTWARD)
    second_mid = along_line(after(next_one, held[1]), MIDDLE)
    held = accumulate([own_over, next_one], [me ^ 1, me ^ 2], gain, in_weight, held)
    second = jnp.where(at_end, second_out, second_mid)
    second_over = across(second, next_over, held[1])
    third_out = along_line(after(second_mid, held[1]), OUTWARD)
    rest_mid = along_line(after(own_over[:, half:], second_mid, held[1]), MIDDLE)
    held = accumulate([next_over, second], [me ^ 3, me ^ 4], gain, in_weight, held)
    third = jnp.where(at_end, third_out, middle)
    third_over = across(third[:, :half], second_over, held[1])
    rest_out = along_line(after(second_over[:, half:], held[1]), OUTWARD)
    held = accumulate([second_over, third], [me ^ 5, me ^ 6], gain, in_weight, held)
    last = [third_over, (rest_out, rest_mid)]
    place = (me ^ 7) * 2
    return accumulate(last, [place, place + 1], gain, in_weight, held, last=True, use_first=at_end)


def project_and_reduce(gated, out_weight, tokens):
    me = lax.axis_index("chan")
    half = tokens.shape[1] // 2
    send = lambda k, h: ((me ^ (2 * k + 1)) * 2 + h, jnp.bfloat16)
    keep = lambda k, h: ((me ^ (2 * k)) * 2 + h, jnp.float32)
    narrow = lambda a: a.astype(jnp.bfloat16)
    make = functools.partial(pieces, gated, out_weight, half)
    both = (0, 1)

    send_third = make([send(3, 0), send(3, 1)])
    third_over = across(send_third[0])
    rest_in = along_line(send_third[1], INWARD)
    rest_mid = along_line(send_third[1], MIDDLE)
    send_second = make([send(2, 0), send(2, 1)], send_third[0])
    keep_third = make([keep(3, 0), (keep(3, 1)[0], jnp.bfloat16)], send_second[0])
    third = [narrow(total(keep_third[0], third_over)), keep_third[1]]
    third_in = [along_line(third[h], INWARD) for h in both]
    send_second[1] = narrow(total(send_second[1], rest_in))
    second_over = [across(send_second[h], third_over) for h in both]
    keep_second = make([keep(2, 0), keep(2, 1)], third_over)
    send_next = make([send(1, 0), send(1, 1)], third_over)
    second = [narrow(total(keep_second[h], second_over[h], third_in[h])) for h in both]
    second_in = [along_line(second[h], INWARD) for h in both]
    second_mid = [along_line(second[h], MIDDLE) for h in both]
    next_over = [across(send_next[h], second_over[h]) for h in both]
    keep_next = make([keep(1, 0), keep(1, 1)], second_over[0])
    send_own = make([send(0, 0), send(0, 1)], second_over[0])
    send_own[1] = narrow(total(send_own[1], rest_mid))
    next_one = [narrow(total(keep_next[h], next_over[h], second_mid[h])) for h in both]
    next_in = [along_line(next_one[h], PAIRS) for h in both]
    middle_in = [along_line(narrow(total(third[h], second_in[h])), MIDDLE) for h in both]
    own_over = [across(send_own[h], next_over[h]) for h in both]
    keep_own = make([keep(0, 0), keep(0, 1)], next_over[0])
    base = [total(keep_own[h], tokens[:, h * half : (h + 1) * half]) for h in both]
    return finish(*[[base[h], own_over[h], next_in[h], middle_in[h]] for h in both])


def mix_kernel(
    acc_ref, rms_ref, rim_ref, taps_ref, decay_ref, res_ref, skip_ref, q_ref, base_ref, end_ref, win_ref, prod_ref, state_ref
):
    step = pl.program_id(0)
    rows = acc_ref.shape[1]
    groups = taps_ref.shape[2]
    tap_count = taps_ref.shape[1]
    poles = decay_ref.shape[0]
    keep = rim_ref.shape[1]
    unroll = 8

    @pl.when(step == 0)
    def _():
        for g in range(groups):
            win_ref[:, :keep, g, :] = rim_ref[:, :, g * LANES : (g + 1) * LANES]
        state_ref[...] = jnp.zeros_like(state_ref)

    inv_rms = rms_ref[:, :1]
    for i in range(3):
        for g in range(groups):
            cols = acc_ref[i, :, g * LANES : (g + 1) * LANES] * inv_rms
            win_ref[i, keep:, g, :] = cols.astype(jnp.bfloat16).astype(jnp.float32)

    def convolve(blk, nothing):
        first = blk * unroll
        conv = []
        for i in range(3):
            taps = [taps_ref[i, j] for j in range(tap_count)]
            held = [win_ref[i, first + keep - (tap_count - 1) + r] for r in range(unroll + tap_count - 1)]
            conv.append(
                [
                    functools.reduce(
                        lambda a, b: a + b, [taps[j] * held[r + tap_count - 1 - j] for j in range(tap_count)]
                    )
                    for r in range(unroll)
                ]
            )
        for r in range(unroll):
            q_ref[first + r] = conv[0][r]
            prod_ref[first + r] = conv[1][r] * conv[2][r]
        return nothing

    lax.fori_loop(0, rows // unroll, convolve, 0)
    win_ref[:, :keep] = win_ref[:, rows:]
    decay = [jnp.exp(decay_ref[n]) for n in range(poles)]
    res = [res_ref[n] for n in range(poles)]
    skip = skip_ref[0]

    def recur(blk, state):
        state = list(state)
        for r in range(unroll):
            t = blk * unroll + r
            product = prod_ref[t]
            sums = [skip * product]
            for n in range(poles):
                state[n] = decay[n] * state[n] + product
                term = res[n] * state[n]
                if n < 3:
                    sums.append(term)
                else:
                    sums[n % 4] = sums[n % 4] + term
            base_ref[t] = q_ref[t] * tree_sum(sums)
        return tuple(state)

    state = lax.fori_loop(0, rows // unroll, recur, tuple(state_ref[n] for n in range(poles)))
    for n in range(poles):
        state_ref[n] = state[n]

    @pl.when(step == pl.num_programs(0) - 1)
    def _():
        for n in range(poles):
            end_ref[n] = state[n]


def mix(acc, inv_rms, rim, taps, log_decay, residue, skip):
    rows, chans = acc.shape[1:]
    groups = chans // LANES
    tap_count, poles = taps.shape[1], log_decay.shape[0]
    keep = rim.shape[1]
    blk = min(128, rows)
    whole = lambda *shape: pl.BlockSpec(shape, lambda t: (0,) * len(shape))
    row_spec = pl.BlockSpec((blk, groups, LANES), lambda t: (t, 0, 0))
    return pl.pallas_call(
        mix_kernel,
        grid=(rows // blk,),
        in_specs=[
            pl.BlockSpec((3, blk, chans), lambda t: (0, t, 0)),
            pl.BlockSpec((blk, LANES), lambda t: (t, 0)),
            whole(3, keep, chans),
            whole(3, tap_count, groups, LANES),
            whole(poles, groups, LANES),
            whole(poles, groups, LANES),
            whole(1, groups, LANES),
        ],
        out_specs=[row_spec, row_spec, whole(poles, groups, LANES)],
        out_shape=[
            jax.ShapeDtypeStruct((rows, groups, LANES), jnp.float32),
            jax.ShapeDtypeStruct((rows, groups, LANES), jnp.float32),
            jax.ShapeDtypeStruct((poles, groups, LANES), jnp.float32),
        ],
        scratch_shapes=[
            pltpu.VMEM((3, keep + blk, groups, LANES), jnp.float32),
            pltpu.VMEM((blk, groups, LANES), jnp.float32),
            pltpu.VMEM((poles, groups, LANES), jnp.float32),
        ],
        compiler_params=pltpu.CompilerParams(vmem_limit_bytes=VMEM_LIMIT),
        cost_estimate=pl.CostEstimate(
            flops=110 * rows * groups * LANES, bytes_accessed=20 * rows * groups * LANES, transcendentals=0
        ),
        name="mix",
    )(acc, inv_rms, rim, taps, log_decay, residue, skip)


def carry_kernel(q_ref, base_ref, state_ref, decay_ref, res_ref, out_ref, coef_ref, row_ref):
    step = pl.program_id(0)
    rows, groups = q_ref.shape[:2]
    poles = decay_ref.shape[0]
    decay = [jnp.exp(decay_ref[n]) for n in range(poles)]

    @pl.when(step == 0)
    def _():
        for n in range(poles):
            coef_ref[n] = res_ref[n] * (decay[n] * state_ref[n])

    unroll = 8

    def body(blk, coef):
        coef = list(coef)
        for r in range(unroll):
            t = blk * unroll + r
            row_ref[t] = base_ref[t] + q_ref[t] * tree_sum(list(coef))
            for n in range(poles):
                coef[n] = decay[n] * coef[n]
        return tuple(coef)

    coef = lax.fori_loop(0, rows // unroll, body, tuple(coef_ref[n] for n in range(poles)))
    for n in range(poles):
        coef_ref[n] = coef[n]
    for g in range(groups):
        out_ref[:, g * LANES : (g + 1) * LANES] = row_ref[:, g, :].astype(jnp.bfloat16)


def carry(query, base, state, log_decay, residue):
    rows, groups = query.shape[:2]
    poles = log_decay.shape[0]
    blk = min(128, rows)
    whole = lambda *shape: pl.BlockSpec(shape, lambda t: (0,) * len(shape))
    row_spec = pl.BlockSpec((blk, groups, LANES), lambda t: (t, 0, 0))
    return pl.pallas_call(
        carry_kernel,
        grid=(rows // blk,),
        in_specs=[row_spec, row_spec] + [whole(poles, groups, LANES)] * 3,
        out_specs=pl.BlockSpec((blk, groups * LANES), lambda t: (t, 0)),
        out_shape=jax.ShapeDtypeStruct((rows, groups * LANES), jnp.bfloat16),
        scratch_shapes=[
            pltpu.VMEM((poles, groups, LANES), jnp.float32),
            pltpu.VMEM((blk, groups, LANES), jnp.float32),
        ],
        compiler_params=pltpu.CompilerParams(vmem_limit_bytes=VMEM_LIMIT),
        cost_estimate=pl.CostEstimate(
            flops=40 * rows * groups * LANES, bytes_accessed=10 * rows * groups * LANES, transcendentals=0
        ),
        name="carry",
    )(query, base, state, log_decay, residue)


def per_device(tokens, norm_gain, in_weight, short_weight, log_decay, residue, skip, out_weight):
    rows, chans = tokens.shape
    groups = chans // LANES
    by_lane = lambda a: a.reshape(a.shape[:-1] + (groups, LANES))
    taps, log_decay, residue = by_lane(short_weight), by_lane(log_decay), by_lane(residue)
    skip = by_lane(skip[None, :])

    paired_line = lax.axis_size("chan") == 8
    if paired_line:
        acc, inv_rms, rim = gather_and_project(tokens, norm_gain, in_weight)
    else:
        gathered = lax.all_gather(tokens, "chan", axis=1, tiled=True)
        depth = min(1024, gathered.shape[1])
        parts = [gathered[:, k : k + depth] for k in range(0, gathered.shape[1], depth)]
        held = None
        for k, part in enumerate(parts):
            held = accumulate([part], [k], norm_gain, in_weight, held, last=k == len(parts) - 1)
        acc, inv_rms, rim = held
    rim = from_behind(rim, "seq", 1)
    query, base, end = mix(acc, inv_rms, rim, taps, log_decay, residue, skip)
    shard_decay = jnp.exp(rows * log_decay)
    state, passing = jnp.zeros_like(end), end
    for _ in range(lax.axis_size("seq") - 1):
        passing = from_behind(passing, "seq", 1)
        state = state + passing
        passing = passing * shard_decay
    gated = carry(query, base, state, log_decay, residue)
    if paired_line:
        return project_and_reduce(gated, out_weight, tokens)
    partial = jnp.dot(gated, out_weight, preferred_element_type=jnp.float32)
    branch = lax.psum_scatter(partial.astype(jnp.bfloat16), "chan", scatter_dimension=1, tiled=True)
    return (tokens.astype(jnp.float32) + branch.astype(jnp.float32)).astype(jnp.bfloat16)


def solution(mesh):
    return jax.shard_map(
        per_device,
        mesh=mesh,
        in_specs=(
            P(("groups", "seq"), "chan"),
            P(),
            P(None, None, "chan"),
            P(None, None, "chan"),
            P(None, "chan"),
            P(None, "chan"),
            P("chan"),
            P("chan", None),
        ),
        out_specs=P(("groups", "seq"), "chan"),
        check_vma=False,
    )
```

```python
import functools

import jax
import jax.numpy as jnp
from jax import lax
from jax.experimental import pallas as pl
from jax.experimental.pallas import tpu as pltpu
from jax.sharding import PartitionSpec as P

EPSILON = 1e-06
LANES = 128
KEEP = 8
VMEM_LIMIT = 48 * 1024 * 1024


def from_behind(block, axis, distance):
    count = lax.axis_size(axis)
    route = [(i - distance, i) for i in range(count) if i - distance >= 0]
    return lax.ppermute(block, axis, route)


def tree_sum(terms):
    while len(terms) > 1:
        pairs = [terms[i] + terms[i + 1] for i in range(0, len(terms) - 1, 2)]
        terms = pairs + terms[len(pairs) * 2 :]
    return terms[0]


def accumulate_kernel(depths, pairs, width, first, last, place_ref, *refs):
    chunk_refs, refs = refs[: len(depths) + sum(pairs)], refs[len(depths) + sum(pairs) :]
    gain_refs, refs = refs[: len(depths)], refs[len(depths) :]
    w_refs, refs = refs[: len(depths)], refs[len(depths) :]
    if not first:
        held_ref, held_sq_ref, refs = refs[0], refs[1], refs[2:]
    if last:
        acc_ref, sq_ref, rim_ref, scaled_ref = refs
    else:
        acc_ref, sq_ref, scaled_ref = refs
    feat, col = pl.program_id(0), pl.program_id(1)

    @pl.when((feat == 0) & (col == 0))
    def _():
        square = None if first else held_sq_ref[...]
        start = at = 0
        for j, depth in enumerate(depths):
            x = chunk_refs[at][...]
            at += 1
            if pairs[j]:
                x = jnp.where(place_ref[len(depths)] == 1, x, chunk_refs[at][...])
                at += 1
            x = x.astype(jnp.float32)
            parts = [x[:, g : g + LANES] * x[:, g : g + LANES] for g in range(0, depth, LANES)]
            part = tree_sum(parts)
            square = part if square is None else square + part
            scaled_ref[:, start : start + depth] = (x * gain_refs[j][0]).astype(jnp.bfloat16)
            start += depth
        if last:
            total = jnp.sum(square, axis=1, keepdims=True)
            square = jnp.broadcast_to(lax.rsqrt(total / width + EPSILON), square.shape)
        sq_ref[...] = square

    start, part = 0, None
    for j, depth in enumerate(depths):
        one = jnp.dot(scaled_ref[:, start : start + depth], w_refs[j][0], preferred_element_type=jnp.float32)
        part = one if part is None else part + one
        start += depth
    acc_ref[0] = part if first else held_ref[0] + part
    if last:
        keep = rim_ref.shape[1]
        rows = acc_ref.shape[1]
        rim = acc_ref[0, rows - keep :, :] * sq_ref[rows - keep :, :1]
        rim_ref[0] = rim.astype(jnp.bfloat16).astype(jnp.float32)


def accumulate(chunks, places, gain, in_weight, held=None, last=False, use_first=None):
    pairs = [isinstance(c, tuple) for c in chunks]
    arrays = [a for c in chunks for a in (c if isinstance(c, tuple) else (c,))]
    depths = [(c[0] if isinstance(c, tuple) else c).shape[1] for c in chunks]
    rows = arrays[0].shape[0]
    width, chans = in_weight.shape[1:]
    tile = min(512, chans)
    first = held is None
    acc_spec = pl.BlockSpec((1, rows, tile), lambda i, c, p: (i, 0, c))
    sq_spec = pl.BlockSpec((rows, LANES), lambda i, c, p: (0, 0))
    in_specs = [pl.BlockSpec(a.shape, lambda i, c, p: (0, 0)) for a in arrays]
    in_specs += [pl.BlockSpec((1, 1, d), lambda i, c, p, j=j: (p[j], 0, 0)) for j, d in enumerate(depths)]
    in_specs += [pl.BlockSpec((1, d, tile), lambda i, c, p, j=j: (i, p[j], c)) for j, d in enumerate(depths)]
    out_specs = [acc_spec, sq_spec]
    out_shape = [
        jax.ShapeDtypeStruct((3, rows, chans), jnp.float32),
        jax.ShapeDtypeStruct((rows, LANES), jnp.float32),
    ]
    if last:
        out_specs.append(pl.BlockSpec((1, KEEP, tile), lambda i, c, p: (i, 0, c)))
        out_shape.append(jax.ShapeDtypeStruct((3, KEEP, chans), jnp.float32))
    extra, aliases = (), {}
    if not first:
        in_specs += [acc_spec, sq_spec]
        extra = tuple(held)
        base = 1 + len(arrays) + 2 * len(depths)
        aliases = {base: 0, base + 1: 1}
    scalars = list(places) + ([] if use_first is None else [use_first])
    return pl.pallas_call(
        functools.partial(accumulate_kernel, depths, pairs, width, first, last),
        grid_spec=pltpu.PrefetchScalarGridSpec(
            num_scalar_prefetch=1,
            grid=(3, chans // tile),
            in_specs=in_specs,
            out_specs=out_specs,
            scratch_shapes=[pltpu.VMEM((rows, sum(depths)), jnp.bfloat16)],
        ),
        out_shape=out_shape,
        input_output_aliases=aliases,
        compiler_params=pltpu.CompilerParams(vmem_limit_bytes=26 * 1024 * 1024),
        cost_estimate=pl.CostEstimate(
            flops=rows * sum(depths) * chans,
            bytes_accessed=6 * sum(depths) * chans,
            transcendentals=0,
        ),
        name="accumulate",
    )(
        jnp.stack([jnp.asarray(n, jnp.int32) for n in scalars]),
        *arrays,
        *[gain.reshape(-1, 1, d) for d in depths],
        *[in_weight] * len(depths),
        *extra,
    )


def pieces_kernel(count, place_ref, gated_ref, w_ref, *refs):
    outs = refs[-count:]
    total = jnp.dot(gated_ref[...], w_ref[...], preferred_element_type=jnp.float32)
    for j in range(count):

        @pl.when(pl.program_id(0) == j)
        def _():
            outs[j][...] = total.astype(outs[j].dtype)


def pieces(out_weight, gated, wanted, *earlier):
    rows, chans = gated.shape
    count = len(wanted)
    out = pl.pallas_call(
        functools.partial(pieces_kernel, count),
        grid_spec=pltpu.PrefetchScalarGridSpec(
            num_scalar_prefetch=1,
            grid=(count,),
            in_specs=[
                pl.BlockSpec((rows, chans), lambda t, p: (0, 0)),
                pl.BlockSpec((chans, chans), lambda t, p: (0, p[t])),
            ]
            + [pl.BlockSpec(memory_space=pl.ANY)] * len(earlier),
            out_specs=[pl.BlockSpec((rows, chans), lambda t, p: (0, 0))] * count,
        ),
        out_shape=[jax.ShapeDtypeStruct((rows, chans), dtype) for place, dtype in wanted],
        compiler_params=pltpu.CompilerParams(vmem_limit_bytes=VMEM_LIMIT),
        cost_estimate=pl.CostEstimate(flops=count * 1000000, bytes_accessed=count * 100000, transcendentals=0),
        name="pieces",
    )(jnp.stack([place.astype(jnp.int32) for place, dtype in wanted]), gated, out_weight, *earlier)
    return list(out)


def finish_kernel(*refs):
    out_ref = refs[-1]
    count = (len(refs) - 1) // 2
    step, per_half = pl.program_id(0), pl.num_programs(0) // 2

    for h in range(2):

        @pl.when((step >= h * per_half) & (step < (h + 1) * per_half))
        def _():
            total = refs[h * count][...].astype(jnp.float32)
            for ref in refs[h * count + 1 : (h + 1) * count]:
                total = total + ref[...].astype(jnp.float32)
            out_ref[...] = total.astype(jnp.bfloat16)


def finish(upper, lower):
    rows, chans = upper[0].shape
    blk = min(128, rows)
    per_half = rows // blk
    spec = lambda h: pl.BlockSpec((blk, chans), lambda t: (jnp.clip(t - h * per_half, 0, per_half - 1), 0))
    return pl.pallas_call(
        finish_kernel,
        grid=(2 * per_half,),
        in_specs=[spec(0)] * len(upper) + [spec(1)] * len(lower),
        out_specs=pl.BlockSpec((blk, chans), lambda t: (t, 0)),
        out_shape=jax.ShapeDtypeStruct((2 * rows, chans), jnp.bfloat16),
        compiler_params=pltpu.CompilerParams(vmem_limit_bytes=VMEM_LIMIT),
        name="finish",
    )(*upper, *lower)


def along_line(block, pairs):
    return lax.ppermute(block, "chan", [(2 * a + y, 2 * b + y) for a, b in pairs for y in (0, 1)])


def after(block, *earlier):
    return lax.optimization_barrier((block,) + earlier)[0]


def across(block, *earlier):
    count = lax.axis_size("chan")
    if earlier:
        block = after(block, *earlier)
    return lax.ppermute(block, "chan", [(c, c ^ 1) for c in range(count)])


def total(*terms):
    return functools.reduce(lambda a, b: a + b, [t.astype(jnp.float32) for t in terms])


PAIRS = [(0, 1), (1, 0), (2, 3), (3, 2)]
MIDDLE = [(1, 2), (2, 1)]
OUTWARD = [(1, 0), (2, 3)]
INWARD = [(0, 1), (3, 2)]


def gather_and_project(tokens, gain, in_weight, params):
    me = lax.axis_index("chan")
    half = tokens.shape[1] // 2
    at_end = (me < 2) | (me >= 6)
    own_over = across(tokens)
    next_one = along_line(tokens, PAIRS)
    middle = along_line(tokens, MIDDLE)
    held = accumulate([tokens], [me], gain, in_weight)
    next_over = across(next_one, own_over, held[1])
    second_out = along_line(after(middle, held[1]), OUTWARD)
    second_mid = along_line(after(next_one, held[1]), MIDDLE)
    held = accumulate([own_over, next_one], [me ^ 1, me ^ 2], gain, in_weight, held)
    second = jnp.where(at_end, second_out, second_mid)
    second_over = across(second, next_over, held[1])
    third_out = along_line(after(second_mid, second_out, held[1]), OUTWARD)
    rest_mid = along_line(after(own_over[:, half:], second_mid, held[1]), MIDDLE)
    held = accumulate([next_over, second], [me ^ 3, me ^ 4], gain, in_weight, held)
    third = jnp.where(at_end, third_out, middle)
    third_over = across(third[:, :half], second_over, held[1])
    rest_out = along_line(after(second_over[:, half:], held[1]), OUTWARD)
    square, *params = lax.optimization_barrier((held[1], *params))
    held = (held[0], square)
    held = accumulate([second_over, third], [me ^ 5, me ^ 6], gain, in_weight, held)
    last = [third_over, (rest_out, rest_mid)]
    place = (me ^ 7) * 2
    return accumulate(last, [place, place + 1], gain, in_weight, held, last=True, use_first=at_end), params


def project_and_reduce(gated, out_weight, tokens):
    me = lax.axis_index("chan")
    half = tokens.shape[0] // 2
    send = lambda k: (me ^ (2 * k + 1), jnp.bfloat16)
    keep = lambda k: (me ^ (2 * k), jnp.float32)
    narrow = lambda a: a.astype(jnp.bfloat16)
    make = functools.partial(pieces, out_weight)
    both = (0, 1)

    upper = gated(0)
    third_send_0 = make(upper, [send(3)])[0]
    third_over = across(third_send_0)
    lower = gated(1, third_send_0)
    third_send_1 = make(lower, [send(3)])[0]
    rest_in = along_line(third_send_1, INWARD)
    rest_mid = along_line(third_send_1, MIDDLE)
    second_send_0, third_keep_0 = make(upper, [send(2), keep(3)], third_send_1)
    second_send_1, third_1 = make(lower, [send(2), (keep(3)[0], jnp.bfloat16)], second_send_0)
    third = [narrow(total(third_keep_0, third_over)), third_1]
    third_in = [along_line(third[h], INWARD) for h in both]
    second_send = [second_send_0, narrow(total(second_send_1, rest_in))]
    second_over = [across(second_send[h], third_over) for h in both]
    halves = (upper, lower)
    later = [make(halves[h], [keep(2), send(1)], third_1) for h in both]
    second = [narrow(total(later[h][0], second_over[h], third_in[h])) for h in both]
    second_in = [along_line(second[h], INWARD) for h in both]
    second_mid = [along_line(second[h], MIDDLE) for h in both]
    next_over = [across(later[h][1], second_over[h]) for h in both]
    later = [make(halves[h], [keep(1), send(0)], third_over) for h in both]
    own_send = [later[0][1], narrow(total(later[1][1], rest_mid))]
    next_one = [narrow(total(later[h][0], next_over[h], second_mid[h])) for h in both]
    next_in = [along_line(next_one[h], PAIRS) for h in both]
    middle_in = [along_line(narrow(total(third[h], second_in[h])), MIDDLE) for h in both]
    own_over = [across(own_send[h], next_over[h]) for h in both]
    own_keep = [make(halves[h], [keep(0)], second_over[0])[0] for h in both]
    base = [total(own_keep[h], tokens[h * half : (h + 1) * half]) for h in both]
    return finish(*[[base[h], own_over[h], next_in[h], middle_in[h]] for h in both])


def mix_kernel(
    acc_ref, rms_ref, rim_ref, taps_ref, decay_ref, res_ref, skip_ref, q_ref, base_ref, end_ref, win_ref, prod_ref, state_ref
):
    step = pl.program_id(0)
    rows = acc_ref.shape[1]
    groups = taps_ref.shape[2]
    tap_count = taps_ref.shape[1]
    poles = decay_ref.shape[0]
    keep = rim_ref.shape[1]
    unroll = 8

    @pl.when(step == 0)
    def _():
        for g in range(groups):
            win_ref[:, :keep, g, :] = rim_ref[:, :, g * LANES : (g + 1) * LANES]
        state_ref[...] = jnp.zeros_like(state_ref)

    inv_rms = rms_ref[:, :1]
    for i in range(3):
        for g in range(groups):
            cols = acc_ref[i, :, g * LANES : (g + 1) * LANES] * inv_rms
            win_ref[i, keep:, g, :] = cols.astype(jnp.bfloat16).astype(jnp.float32)

    def convolve(blk, nothing):
        first = blk * unroll
        conv = []
        for i in range(3):
            taps = [taps_ref[i, j] for j in range(tap_count)]
            held = [win_ref[i, first + keep - (tap_count - 1) + r] for r in range(unroll + tap_count - 1)]
            conv.append(
                [
                    functools.reduce(
                        lambda a, b: a + b, [taps[j] * held[r + tap_count - 1 - j] for j in range(tap_count)]
                    )
                    for r in range(unroll)
                ]
            )
        for r in range(unroll):
            q_ref[first + r] = conv[0][r]
            prod_ref[first + r] = conv[1][r] * conv[2][r]
        return nothing

    lax.fori_loop(0, rows // unroll, convolve, 0)
    win_ref[:, :keep] = win_ref[:, rows:]
    decay = [jnp.exp(decay_ref[n]) for n in range(poles)]
    res = [res_ref[n] for n in range(poles)]
    skip = skip_ref[0]

    def recur(blk, state):
        state = list(state)
        for r in range(unroll):
            t = blk * unroll + r
            product = prod_ref[t]
            sums = [skip * product]
            for n in range(poles):
                state[n] = decay[n] * state[n] + product
                term = res[n] * state[n]
                if n < 3:
                    sums.append(term)
                else:
                    sums[n % 4] = sums[n % 4] + term
            base_ref[t] = q_ref[t] * tree_sum(sums)
        return tuple(state)

    state = lax.fori_loop(0, rows // unroll, recur, tuple(state_ref[n] for n in range(poles)))
    for n in range(poles):
        state_ref[n] = state[n]

    @pl.when(step == pl.num_programs(0) - 1)
    def _():
        for n in range(poles):
            end_ref[n] = state[n]


def mix(acc, inv_rms, rim, taps, log_decay, residue, skip):
    rows, chans = acc.shape[1:]
    groups = chans // LANES
    tap_count, poles = taps.shape[1], log_decay.shape[0]
    keep = rim.shape[1]
    blk = min(128, rows)
    whole = lambda *shape: pl.BlockSpec(shape, lambda t: (0,) * len(shape))
    row_spec = pl.BlockSpec((blk, groups, LANES), lambda t: (t, 0, 0))
    return pl.pallas_call(
        mix_kernel,
        grid=(rows // blk,),
        in_specs=[
            pl.BlockSpec((3, blk, chans), lambda t: (0, t, 0)),
            pl.BlockSpec((blk, LANES), lambda t: (t, 0)),
            whole(3, keep, chans),
            whole(3, tap_count, groups, LANES),
            whole(poles, groups, LANES),
            whole(poles, groups, LANES),
            whole(1, groups, LANES),
        ],
        out_specs=[row_spec, row_spec, whole(poles, groups, LANES)],
        out_shape=[
            jax.ShapeDtypeStruct((rows, groups, LANES), jnp.float32),
            jax.ShapeDtypeStruct((rows, groups, LANES), jnp.float32),
            jax.ShapeDtypeStruct((poles, groups, LANES), jnp.float32),
        ],
        scratch_shapes=[
            pltpu.VMEM((3, keep + blk, groups, LANES), jnp.float32),
            pltpu.VMEM((blk, groups, LANES), jnp.float32),
            pltpu.VMEM((poles, groups, LANES), jnp.float32),
        ],
        compiler_params=pltpu.CompilerParams(vmem_limit_bytes=26 * 1024 * 1024),
        cost_estimate=pl.CostEstimate(
            flops=110 * rows * groups * LANES, bytes_accessed=20 * rows * groups * LANES, transcendentals=0
        ),
        name="mix",
    )(acc, inv_rms, rim, taps, log_decay, residue, skip)


def carry_kernel(start, q_ref, base_ref, state_ref, decay_ref, res_ref, *refs):
    out_ref, coef_ref, row_ref = refs[-3:]
    step = pl.program_id(0)
    rows, groups = q_ref.shape[:2]
    poles = decay_ref.shape[0]
    decay = [jnp.exp(decay_ref[n]) for n in range(poles)]

    @pl.when(step == 0)
    def _():
        for n in range(poles):
            coef_ref[n] = res_ref[n] * (jnp.exp((start + 1.0) * decay_ref[n]) * state_ref[n])

    unroll = 8

    def body(blk, coef):
        coef = list(coef)
        for r in range(unroll):
            t = blk * unroll + r
            row_ref[t] = base_ref[t] + q_ref[t] * tree_sum(list(coef))
            for n in range(poles):
                coef[n] = decay[n] * coef[n]
        return tuple(coef)

    coef = lax.fori_loop(0, rows // unroll, body, tuple(coef_ref[n] for n in range(poles)))
    for n in range(poles):
        coef_ref[n] = coef[n]
    for g in range(groups):
        out_ref[:, g * LANES : (g + 1) * LANES] = row_ref[:, g, :].astype(jnp.bfloat16)


def carry(query, base, state, log_decay, residue, start, rows, *earlier):
    groups = query.shape[1]
    poles = log_decay.shape[0]
    blk = min(128, rows)
    whole = lambda *shape: pl.BlockSpec(shape, lambda t: (0,) * len(shape))
    row_spec = pl.BlockSpec((blk, groups, LANES), lambda t: (t + start // blk, 0, 0))
    return pl.pallas_call(
        functools.partial(carry_kernel, start),
        grid=(rows // blk,),
        in_specs=[row_spec, row_spec]
        + [whole(poles, groups, LANES)] * 3
        + [pl.BlockSpec(memory_space=pl.ANY)] * len(earlier),
        out_specs=pl.BlockSpec((blk, groups * LANES), lambda t: (t, 0)),
        out_shape=jax.ShapeDtypeStruct((rows, groups * LANES), jnp.bfloat16),
        scratch_shapes=[
            pltpu.VMEM((poles, groups, LANES), jnp.float32),
            pltpu.VMEM((blk, groups, LANES), jnp.float32),
        ],
        compiler_params=pltpu.CompilerParams(vmem_limit_bytes=26 * 1024 * 1024),
        cost_estimate=pl.CostEstimate(
            flops=40 * rows * groups * LANES, bytes_accessed=80 * rows * groups * LANES, transcendentals=0
        ),
        name="carry",
    )(query, base, state, log_decay, residue, *earlier)


def per_device(tokens, norm_gain, in_weight, short_weight, log_decay, residue, skip, out_weight):
    rows, chans = tokens.shape
    groups = chans // LANES
    by_lane = lambda a: a.reshape(a.shape[:-1] + (groups, LANES))
    taps, log_decay, residue = by_lane(short_weight), by_lane(log_decay), by_lane(residue)
    skip = by_lane(skip[None, :])

    paired_line = lax.axis_size("chan") == 8
    if paired_line:
        params = (taps, log_decay, residue, skip)
        (acc, inv_rms, rim), params = gather_and_project(tokens, norm_gain, in_weight, params)
        taps, log_decay, residue, skip = params
    else:
        gathered = lax.all_gather(tokens, "chan", axis=1, tiled=True)
        depth = min(1024, gathered.shape[1])
        parts = [gathered[:, k : k + depth] for k in range(0, gathered.shape[1], depth)]
        held = None
        for k, part in enumerate(parts):
            held = accumulate([part], [k], norm_gain, in_weight, held, last=k == len(parts) - 1)
        acc, inv_rms, rim = held
    rim = from_behind(rim, "seq", 1)
    query, base, end = mix(acc, inv_rms, rim, taps, log_decay, residue, skip)
    shard_decay = jnp.exp(rows * log_decay)
    state, passing = jnp.zeros_like(end), end
    for _ in range(lax.axis_size("seq") - 1):
        passing = from_behind(passing, "seq", 1)
        state = state + passing
        passing = passing * shard_decay
    if paired_line:

        def half_gated(h, *earlier):
            return carry(query, base, state, log_decay, residue, h * rows // 2, rows // 2, *earlier)

        return project_and_reduce(half_gated, out_weight, tokens)
    gated = carry(query, base, state, log_decay, residue, 0, rows)
    partial = jnp.dot(gated, out_weight, preferred_element_type=jnp.float32)
    branch = lax.psum_scatter(partial.astype(jnp.bfloat16), "chan", scatter_dimension=1, tiled=True)
    return (tokens.astype(jnp.float32) + branch.astype(jnp.float32)).astype(jnp.bfloat16)


def solution(mesh):
    return jax.shard_map(
        per_device,
        mesh=mesh,
        in_specs=(
            P(("groups", "seq"), "chan"),
            P(),
            P(None, None, "chan"),
            P(None, None, "chan"),
            P(None, "chan"),
            P(None, "chan"),
            P("chan"),
            P("chan", None),
        ),
        out_specs=P(("groups", "seq"), "chan"),
        check_vma=False,
    )
```

```python
import functools

import jax
import jax.numpy as jnp
from jax import lax
from jax.experimental import pallas as pl
from jax.experimental.pallas import tpu as pltpu
from jax.sharding import PartitionSpec as P

EPSILON = 1e-06
LANES = 128
KEEP = 8
VMEM_LIMIT = 48 * 1024 * 1024


def from_behind(block, axis, distance):
    count = lax.axis_size(axis)
    route = [(i - distance, i) for i in range(count) if i - distance >= 0]
    return lax.ppermute(block, axis, route)


def tree_sum(terms):
    while len(terms) > 1:
        pairs = [terms[i] + terms[i + 1] for i in range(0, len(terms) - 1, 2)]
        terms = pairs + terms[len(pairs) * 2 :]
    return terms[0]


def accumulate_kernel(depths, pairs, width, first, last, place_ref, *refs):
    chunk_refs, refs = refs[: len(depths) + sum(pairs)], refs[len(depths) + sum(pairs) :]
    gain_refs, refs = refs[: len(depths)], refs[len(depths) :]
    w_refs, refs = refs[: len(depths)], refs[len(depths) :]
    if not first:
        held_ref, held_sq_ref, refs = refs[0], refs[1], refs[2:]
    if last:
        acc_ref, sq_ref, rim_ref, scaled_ref = refs
    else:
        acc_ref, sq_ref, scaled_ref = refs
    feat, col = pl.program_id(0), pl.program_id(1)

    @pl.when((feat == 0) & (col == 0))
    def _():
        square = None if first else held_sq_ref[...]
        start = at = 0
        for j, depth in enumerate(depths):
            x = chunk_refs[at][...]
            at += 1
            if pairs[j]:
                x = jnp.where(place_ref[len(depths)] == 1, x, chunk_refs[at][...])
                at += 1
            x = x.astype(jnp.float32)
            parts = [x[:, g : g + LANES] * x[:, g : g + LANES] for g in range(0, depth, LANES)]
            part = tree_sum(parts)
            square = part if square is None else square + part
            scaled_ref[:, start : start + depth] = (x * gain_refs[j][0]).astype(jnp.bfloat16)
            start += depth
        if last:
            total = jnp.sum(square, axis=1, keepdims=True)
            square = jnp.broadcast_to(lax.rsqrt(total / width + EPSILON), square.shape)
        sq_ref[...] = square

    start, part = 0, None
    for j, depth in enumerate(depths):
        one = jnp.dot(scaled_ref[:, start : start + depth], w_refs[j][0], preferred_element_type=jnp.float32)
        part = one if part is None else part + one
        start += depth
    acc_ref[0] = part if first else held_ref[0] + part
    if last:
        keep = rim_ref.shape[1]
        rows = acc_ref.shape[1]
        rim = acc_ref[0, rows - keep :, :] * sq_ref[rows - keep :, :1]
        rim_ref[0] = rim.astype(jnp.bfloat16).astype(jnp.float32)


def accumulate(chunks, places, gain, in_weight, held=None, last=False, use_first=None):
    pairs = [isinstance(c, tuple) for c in chunks]
    arrays = [a for c in chunks for a in (c if isinstance(c, tuple) else (c,))]
    depths = [(c[0] if isinstance(c, tuple) else c).shape[1] for c in chunks]
    rows = arrays[0].shape[0]
    width, chans = in_weight.shape[1:]
    tile = min(512, chans)
    first = held is None
    acc_spec = pl.BlockSpec((1, rows, tile), lambda i, c, p: (i, 0, c))
    sq_spec = pl.BlockSpec((rows, LANES), lambda i, c, p: (0, 0))
    in_specs = [pl.BlockSpec(a.shape, lambda i, c, p: (0, 0)) for a in arrays]
    in_specs += [pl.BlockSpec((1, 1, d), lambda i, c, p, j=j: (p[j], 0, 0)) for j, d in enumerate(depths)]
    in_specs += [pl.BlockSpec((1, d, tile), lambda i, c, p, j=j: (i, p[j], c)) for j, d in enumerate(depths)]
    out_specs = [acc_spec, sq_spec]
    out_shape = [
        jax.ShapeDtypeStruct((3, rows, chans), jnp.float32),
        jax.ShapeDtypeStruct((rows, LANES), jnp.float32),
    ]
    if last:
        out_specs.append(pl.BlockSpec((1, KEEP, tile), lambda i, c, p: (i, 0, c)))
        out_shape.append(jax.ShapeDtypeStruct((3, KEEP, chans), jnp.float32))
    extra, aliases = (), {}
    if not first:
        in_specs += [acc_spec, sq_spec]
        extra = tuple(held)
        base = 1 + len(arrays) + 2 * len(depths)
        aliases = {base: 0, base + 1: 1}
    scalars = list(places) + ([] if use_first is None else [use_first])
    return pl.pallas_call(
        functools.partial(accumulate_kernel, depths, pairs, width, first, last),
        grid_spec=pltpu.PrefetchScalarGridSpec(
            num_scalar_prefetch=1,
            grid=(3, chans // tile),
            in_specs=in_specs,
            out_specs=out_specs,
            scratch_shapes=[pltpu.VMEM((rows, sum(depths)), jnp.bfloat16)],
        ),
        out_shape=out_shape,
        input_output_aliases=aliases,
        compiler_params=pltpu.CompilerParams(vmem_limit_bytes=VMEM_LIMIT),
        cost_estimate=pl.CostEstimate(
            flops=rows * sum(depths) * chans,
            bytes_accessed=6 * sum(depths) * chans,
            transcendentals=0,
        ),
        name="accumulate",
    )(
        jnp.stack([jnp.asarray(n, jnp.int32) for n in scalars]),
        *arrays,
        *[gain.reshape(-1, 1, d) for d in depths],
        *[in_weight] * len(depths),
        *extra,
    )


def pieces_kernel(count, place_ref, gated_ref, w_ref, *refs):
    outs = refs[-count:]
    total = jnp.dot(gated_ref[...], w_ref[...], preferred_element_type=jnp.float32)
    for j in range(count):

        @pl.when(pl.program_id(0) == j)
        def _():
            outs[j][...] = total.astype(outs[j].dtype)


def pieces(out_weight, gated, wanted, *earlier):
    rows, chans = gated.shape
    count = len(wanted)
    out = pl.pallas_call(
        functools.partial(pieces_kernel, count),
        grid_spec=pltpu.PrefetchScalarGridSpec(
            num_scalar_prefetch=1,
            grid=(count,),
            in_specs=[
                pl.BlockSpec((rows, chans), lambda t, p: (0, 0)),
                pl.BlockSpec((chans, chans), lambda t, p: (0, p[t])),
            ]
            + [pl.BlockSpec(memory_space=pl.ANY)] * len(earlier),
            out_specs=[pl.BlockSpec((rows, chans), lambda t, p: (0, 0))] * count,
        ),
        out_shape=[jax.ShapeDtypeStruct((rows, chans), dtype) for place, dtype in wanted],
        compiler_params=pltpu.CompilerParams(vmem_limit_bytes=VMEM_LIMIT),
        cost_estimate=pl.CostEstimate(flops=count * 1000000, bytes_accessed=count * 100000, transcendentals=0),
        name="pieces",
    )(jnp.stack([place.astype(jnp.int32) for place, dtype in wanted]), gated, out_weight, *earlier)
    return list(out)


def finish_kernel(*refs):
    out_ref = refs[-1]
    count = (len(refs) - 1) // 2
    step, per_half = pl.program_id(0), pl.num_programs(0) // 2

    for h in range(2):

        @pl.when((step >= h * per_half) & (step < (h + 1) * per_half))
        def _():
            total = refs[h * count][...].astype(jnp.float32)
            for ref in refs[h * count + 1 : (h + 1) * count]:
                total = total + ref[...].astype(jnp.float32)
            out_ref[...] = total.astype(jnp.bfloat16)


def finish(upper, lower):
    rows, chans = upper[0].shape
    blk = min(128, rows)
    per_half = rows // blk
    spec = lambda h: pl.BlockSpec((blk, chans), lambda t: (jnp.clip(t - h * per_half, 0, per_half - 1), 0))
    return pl.pallas_call(
        finish_kernel,
        grid=(2 * per_half,),
        in_specs=[spec(0)] * len(upper) + [spec(1)] * len(lower),
        out_specs=pl.BlockSpec((blk, chans), lambda t: (t, 0)),
        out_shape=jax.ShapeDtypeStruct((2 * rows, chans), jnp.bfloat16),
        compiler_params=pltpu.CompilerParams(vmem_limit_bytes=VMEM_LIMIT),
        name="finish",
    )(*upper, *lower)


def along_line(block, pairs):
    return lax.ppermute(block, "chan", [(2 * a + y, 2 * b + y) for a, b in pairs for y in (0, 1)])


def after(block, *earlier):
    return lax.optimization_barrier((block,) + earlier)[0]


def across(block, *earlier):
    count = lax.axis_size("chan")
    if earlier:
        block = after(block, *earlier)
    return lax.ppermute(block, "chan", [(c, c ^ 1) for c in range(count)])


def total(*terms):
    return functools.reduce(lambda a, b: a + b, [t.astype(jnp.float32) for t in terms])


PAIRS = [(0, 1), (1, 0), (2, 3), (3, 2)]
MIDDLE = [(1, 2), (2, 1)]
OUTWARD = [(1, 0), (2, 3)]
INWARD = [(0, 1), (3, 2)]


def gather_and_project(tokens, gain, in_weight, params):
    me = lax.axis_index("chan")
    half = tokens.shape[1] // 2
    at_end = (me < 2) | (me >= 6)
    own_over = across(tokens)
    next_one = along_line(tokens, PAIRS)
    middle = along_line(tokens, MIDDLE)
    held = accumulate([tokens], [me], gain, in_weight)
    next_over = across(next_one, own_over, held[1])
    second_out = along_line(after(middle, held[1]), OUTWARD)
    second_mid = along_line(after(next_one, held[1]), MIDDLE)
    square, *params = lax.optimization_barrier((held[1], *params))
    held = accumulate([own_over, next_one], [me ^ 1, me ^ 2], gain, in_weight, (held[0], square))
    second = jnp.where(at_end, second_out, second_mid)
    second_over = across(second, next_over, held[1])
    third_out = along_line(after(second_mid, second_out, held[1]), OUTWARD)
    rest_mid = along_line(after(own_over[:, half:], second_mid, held[1]), MIDDLE)
    held = accumulate([next_over, second], [me ^ 3, me ^ 4], gain, in_weight, held)
    third_over = across(jnp.where(at_end, third_out[:, :half], middle[:, :half]), second_over, held[1])
    rest_out = along_line(after(second_over[:, half:], held[1]), OUTWARD)
    third = (third_out, middle)
    held = accumulate([second_over, third], [me ^ 5, me ^ 6], gain, in_weight, held, use_first=at_end)
    last = [third_over, (rest_out, rest_mid)]
    place = (me ^ 7) * 2
    return accumulate(last, [place, place + 1], gain, in_weight, held, last=True, use_first=at_end), params


def project_and_reduce(gated, out_weight, tokens):
    me = lax.axis_index("chan")
    half = tokens.shape[0] // 2
    send = lambda k: (me ^ (2 * k + 1), jnp.bfloat16)
    keep = lambda k: (me ^ (2 * k), jnp.float32)
    narrow = lambda a: a.astype(jnp.bfloat16)
    make = functools.partial(pieces, out_weight)
    both = (0, 1)

    upper = gated(0)
    third_send_0 = make(upper, [send(3)])[0]
    third_over = across(third_send_0)
    lower = gated(1, third_send_0)
    third_send_1 = make(lower, [send(3)])[0]
    rest_in = along_line(third_send_1, INWARD)
    rest_mid = along_line(third_send_1, MIDDLE)
    second_send_0, third_keep_0 = make(upper, [send(2), keep(3)], third_send_1)
    second_send_1, third_1 = make(lower, [send(2), (keep(3)[0], jnp.bfloat16)], second_send_0)
    third = [narrow(total(third_keep_0, third_over)), third_1]
    third_in = [along_line(third[h], INWARD) for h in both]
    second_send = [second_send_0, narrow(total(second_send_1, rest_in))]
    second_over = [across(second_send[h], third_over) for h in both]
    halves = (upper, lower)
    later = [make(halves[h], [keep(2), send(1)], (third_over, second_send[1])[h]) for h in both]
    second = [narrow(total(later[h][0], second_over[h], third_in[h])) for h in both]
    second_in = [along_line(second[h], INWARD) for h in both]
    second_mid = [along_line(second[h], MIDDLE) for h in both]
    next_over = [across(later[h][1], second_over[h]) for h in both]
    later = [make(halves[h], [keep(1), send(0)], third_over) for h in both]
    own_send = [later[0][1], narrow(total(later[1][1], rest_mid))]
    next_one = [narrow(total(later[h][0], next_over[h], second_mid[h])) for h in both]
    next_in = [along_line(next_one[h], PAIRS) for h in both]
    middle_in = [along_line(narrow(total(third[h], second_in[h])), MIDDLE) for h in both]
    own_over = [across(own_send[h], next_over[h]) for h in both]
    own_keep = [make(halves[h], [keep(0)], second_over[0])[0] for h in both]
    base = [total(own_keep[h], tokens[h * half : (h + 1) * half]) for h in both]
    return finish(*[[base[h], own_over[h], next_in[h], middle_in[h]] for h in both])


def mix_kernel(
    acc_ref, rms_ref, rim_ref, taps_ref, decay_ref, res_ref, skip_ref, q_ref, base_ref, end_ref, win_ref, prod_ref, state_ref
):
    step = pl.program_id(0)
    rows = acc_ref.shape[1]
    groups = taps_ref.shape[2]
    tap_count = taps_ref.shape[1]
    poles = decay_ref.shape[0]
    keep = rim_ref.shape[1]
    unroll = 8

    @pl.when(step == 0)
    def _():
        for g in range(groups):
            win_ref[:, :keep, g, :] = rim_ref[:, :, g * LANES : (g + 1) * LANES]
        state_ref[...] = jnp.zeros_like(state_ref)

    inv_rms = rms_ref[:, :1]
    for i in range(3):
        for g in range(groups):
            cols = acc_ref[i, :, g * LANES : (g + 1) * LANES] * inv_rms
            win_ref[i, keep:, g, :] = cols.astype(jnp.bfloat16).astype(jnp.float32)

    def convolve(blk, nothing):
        first = blk * unroll
        conv = []
        for i in range(3):
            taps = [taps_ref[i, j] for j in range(tap_count)]
            held = [win_ref[i, first + keep - (tap_count - 1) + r] for r in range(unroll + tap_count - 1)]
            conv.append(
                [
                    functools.reduce(
                        lambda a, b: a + b, [taps[j] * held[r + tap_count - 1 - j] for j in range(tap_count)]
                    )
                    for r in range(unroll)
                ]
            )
        for r in range(unroll):
            q_ref[first + r] = conv[0][r]
            prod_ref[first + r] = conv[1][r] * conv[2][r]
        return nothing

    lax.fori_loop(0, rows // unroll, convolve, 0)
    win_ref[:, :keep] = win_ref[:, rows:]
    decay = [jnp.exp(decay_ref[n]) for n in range(poles)]
    res = [res_ref[n] for n in range(poles)]
    skip = skip_ref[0]

    def recur(blk, state):
        state = list(state)
        for r in range(unroll):
            t = blk * unroll + r
            product = prod_ref[t]
            sums = [skip * product]
            for n in range(poles):
                state[n] = decay[n] * state[n] + product
                term = res[n] * state[n]
                if n < 3:
                    sums.append(term)
                else:
                    sums[n % 4] = sums[n % 4] + term
            base_ref[t] = q_ref[t] * tree_sum(sums)
        return tuple(state)

    state = lax.fori_loop(0, rows // unroll, recur, tuple(state_ref[n] for n in range(poles)))
    for n in range(poles):
        state_ref[n] = state[n]

    @pl.when(step == pl.num_programs(0) - 1)
    def _():
        for n in range(poles):
            end_ref[n] = state[n]


def mix(acc, inv_rms, rim, taps, log_decay, residue, skip):
    rows, chans = acc.shape[1:]
    groups = chans // LANES
    tap_count, poles = taps.shape[1], log_decay.shape[0]
    keep = rim.shape[1]
    blk = min(128, rows)
    whole = lambda *shape: pl.BlockSpec(shape, lambda t: (0,) * len(shape))
    row_spec = pl.BlockSpec((blk, groups, LANES), lambda t: (t, 0, 0))
    return pl.pallas_call(
        mix_kernel,
        grid=(rows // blk,),
        in_specs=[
            pl.BlockSpec((3, blk, chans), lambda t: (0, t, 0)),
            pl.BlockSpec((blk, LANES), lambda t: (t, 0)),
            whole(3, keep, chans),
            whole(3, tap_count, groups, LANES),
            whole(poles, groups, LANES),
            whole(poles, groups, LANES),
            whole(1, groups, LANES),
        ],
        out_specs=[row_spec, row_spec, whole(poles, groups, LANES)],
        out_shape=[
            jax.ShapeDtypeStruct((rows, groups, LANES), jnp.float32),
            jax.ShapeDtypeStruct((rows, groups, LANES), jnp.float32),
            jax.ShapeDtypeStruct((poles, groups, LANES), jnp.float32),
        ],
        scratch_shapes=[
            pltpu.VMEM((3, keep + blk, groups, LANES), jnp.float32),
            pltpu.VMEM((blk, groups, LANES), jnp.float32),
            pltpu.VMEM((poles, groups, LANES), jnp.float32),
        ],
        compiler_params=pltpu.CompilerParams(vmem_limit_bytes=VMEM_LIMIT),
        cost_estimate=pl.CostEstimate(
            flops=110 * rows * groups * LANES, bytes_accessed=20 * rows * groups * LANES, transcendentals=0
        ),
        name="mix",
    )(acc, inv_rms, rim, taps, log_decay, residue, skip)


def carry_kernel(start, q_ref, base_ref, state_ref, decay_ref, res_ref, *refs):
    out_ref, coef_ref, row_ref = refs[-3:]
    step = pl.program_id(0)
    rows, groups = q_ref.shape[:2]
    poles = decay_ref.shape[0]
    decay = [jnp.exp(decay_ref[n]) for n in range(poles)]

    @pl.when(step == 0)
    def _():
        for n in range(poles):
            coef_ref[n] = res_ref[n] * (jnp.exp((start + 1.0) * decay_ref[n]) * state_ref[n])

    unroll = 8

    def body(blk, coef):
        coef = list(coef)
        for r in range(unroll):
            t = blk * unroll + r
            row_ref[t] = base_ref[t] + q_ref[t] * tree_sum(list(coef))
            for n in range(poles):
                coef[n] = decay[n] * coef[n]
        return tuple(coef)

    coef = lax.fori_loop(0, rows // unroll, body, tuple(coef_ref[n] for n in range(poles)))
    for n in range(poles):
        coef_ref[n] = coef[n]
    for g in range(groups):
        out_ref[:, g * LANES : (g + 1) * LANES] = row_ref[:, g, :].astype(jnp.bfloat16)


def carry(query, base, state, log_decay, residue, start, rows, *earlier):
    groups = query.shape[1]
    poles = log_decay.shape[0]
    blk = min(128, rows)
    whole = lambda *shape: pl.BlockSpec(shape, lambda t: (0,) * len(shape))
    row_spec = pl.BlockSpec((blk, groups, LANES), lambda t: (t + start // blk, 0, 0))
    return pl.pallas_call(
        functools.partial(carry_kernel, start),
        grid=(rows // blk,),
        in_specs=[row_spec, row_spec]
        + [whole(poles, groups, LANES)] * 3
        + [pl.BlockSpec(memory_space=pl.ANY)] * len(earlier),
        out_specs=pl.BlockSpec((blk, groups * LANES), lambda t: (t, 0)),
        out_shape=jax.ShapeDtypeStruct((rows, groups * LANES), jnp.bfloat16),
        scratch_shapes=[
            pltpu.VMEM((poles, groups, LANES), jnp.float32),
            pltpu.VMEM((blk, groups, LANES), jnp.float32),
        ],
        compiler_params=pltpu.CompilerParams(vmem_limit_bytes=VMEM_LIMIT),
        cost_estimate=pl.CostEstimate(
            flops=40 * rows * groups * LANES, bytes_accessed=80 * rows * groups * LANES, transcendentals=0
        ),
        name="carry",
    )(query, base, state, log_decay, residue, *earlier)


def per_device(tokens, norm_gain, in_weight, short_weight, log_decay, residue, skip, out_weight):
    rows, chans = tokens.shape
    groups = chans // LANES
    by_lane = lambda a: a.reshape(a.shape[:-1] + (groups, LANES))
    taps, log_decay, residue = by_lane(short_weight), by_lane(log_decay), by_lane(residue)
    skip = by_lane(skip[None, :])

    paired_line = lax.axis_size("chan") == 8
    if paired_line:
        params = (taps, log_decay, residue, skip)
        (acc, inv_rms, rim), params = gather_and_project(tokens, norm_gain, in_weight, params)
        taps, log_decay, residue, skip = params
    else:
        gathered = lax.all_gather(tokens, "chan", axis=1, tiled=True)
        depth = min(1024, gathered.shape[1])
        parts = [gathered[:, k : k + depth] for k in range(0, gathered.shape[1], depth)]
        held = None
        for k, part in enumerate(parts):
            held = accumulate([part], [k], norm_gain, in_weight, held, last=k == len(parts) - 1)
        acc, inv_rms, rim = held
    rim = from_behind(rim, "seq", 1)
    query, base, end = mix(acc, inv_rms, rim, taps, log_decay, residue, skip)
    shard_decay = jnp.exp(rows * log_decay)
    state, passing = jnp.zeros_like(end), end
    for _ in range(lax.axis_size("seq") - 1):
        passing = from_behind(passing, "seq", 1)
        state = state + passing
        passing = passing * shard_decay
    if paired_line:

        def half_gated(h, *earlier):
            return carry(query, base, state, log_decay, residue, h * rows // 2, rows // 2, *earlier)

        return project_and_reduce(half_gated, out_weight, tokens)
    gated = carry(query, base, state, log_decay, residue, 0, rows)
    partial = jnp.dot(gated, out_weight, preferred_element_type=jnp.float32)
    branch = lax.psum_scatter(partial.astype(jnp.bfloat16), "chan", scatter_dimension=1, tiled=True)
    return (tokens.astype(jnp.float32) + branch.astype(jnp.float32)).astype(jnp.bfloat16)


def solution(mesh):
    return jax.shard_map(
        per_device,
        mesh=mesh,
        in_specs=(
            P(("groups", "seq"), "chan"),
            P(),
            P(None, None, "chan"),
            P(None, None, "chan"),
            P(None, "chan"),
            P(None, "chan"),
            P("chan"),
            P("chan", None),
        ),
        out_specs=P(("groups", "seq"), "chan"),
        check_vma=False,
    )
```

```python
import functools

import jax
import jax.numpy as jnp
from jax import lax
from jax.experimental import pallas as pl
from jax.experimental.pallas import tpu as pltpu
from jax.sharding import PartitionSpec as P

EPSILON = 1e-06
LANES = 128
KEEP = 8
VMEM_LIMIT = 48 * 1024 * 1024


def from_behind(block, axis, distance):
    count = lax.axis_size(axis)
    route = [(i - distance, i) for i in range(count) if i - distance >= 0]
    return lax.ppermute(block, axis, route)


def tree_sum(terms):
    while len(terms) > 1:
        pairs = [terms[i] + terms[i + 1] for i in range(0, len(terms) - 1, 2)]
        terms = pairs + terms[len(pairs) * 2 :]
    return terms[0]


def accumulate_kernel(depths, pairs, width, has_acc, has_sq, part_count, place_ref, *refs):
    def take(count):
        nonlocal refs
        taken, refs = refs[:count], refs[count:]
        return taken

    chunk_refs = take(len(depths) + sum(pairs))
    gain_refs, w_refs = take(len(depths)), take(len(depths))
    held_refs, held_sq_refs = take(int(has_acc)), take(int(has_sq))
    part_refs = take(part_count or 0)
    acc_ref, sq_ref = take(2)
    scaled_ref = refs[-1]
    feat, col = pl.program_id(0), pl.program_id(1)
    last = part_count is not None

    @pl.when((feat == 0) & (col == 0))
    def _():
        square = held_sq_refs[0][...] if has_sq else None
        start = at = 0
        for j, depth in enumerate(depths):
            x = chunk_refs[at][...]
            at += 1
            if pairs[j]:
                x = jnp.where(place_ref[len(depths)] == 1, x, chunk_refs[at][...])
                at += 1
            x = x.astype(jnp.float32)
            parts = [x[:, g : g + LANES] * x[:, g : g + LANES] for g in range(0, depth, LANES)]
            part = tree_sum(parts)
            square = part if square is None else square + part
            scaled_ref[:, start : start + depth] = (x * gain_refs[j][0]).astype(jnp.bfloat16)
            start += depth
        if last:
            total = jnp.sum(square, axis=1, keepdims=True)
            square = jnp.broadcast_to(lax.rsqrt(total / width + EPSILON), square.shape)
        sq_ref[...] = square

    start, part = 0, None
    for j, depth in enumerate(depths):
        one = jnp.dot(scaled_ref[:, start : start + depth], w_refs[j][0], preferred_element_type=jnp.float32)
        part = one if part is None else part + one
        start += depth
    acc_ref[0] = held_refs[0][0] + part if has_acc else part
    if last:
        rim_ref = refs[0]
        keep = rim_ref.shape[1]
        rows = acc_ref.shape[1]
        rim = acc_ref[0, rows - keep :, :]
        for ref in part_refs:
            rim = rim + ref[0]
        rim_ref[0] = (rim * sq_ref[rows - keep :, :1]).astype(jnp.bfloat16).astype(jnp.float32)


def accumulate(chunks, places, gain, in_weight, acc=None, square=None, parts=None, use_first=None):
    pairs = [isinstance(c, tuple) for c in chunks]
    arrays = [a for c in chunks for a in (c if isinstance(c, tuple) else (c,))]
    depths = [(c[0] if isinstance(c, tuple) else c).shape[1] for c in chunks]
    rows = arrays[0].shape[0]
    width, chans = in_weight.shape[1:]
    tile = min(512, chans)
    acc_spec = pl.BlockSpec((1, rows, tile), lambda i, c, p: (i, 0, c))
    sq_spec = pl.BlockSpec((rows, LANES), lambda i, c, p: (0, 0))
    in_specs = [pl.BlockSpec(a.shape, lambda i, c, p: (0, 0)) for a in arrays]
    in_specs += [pl.BlockSpec((1, 1, d), lambda i, c, p, j=j: (p[j], 0, 0)) for j, d in enumerate(depths)]
    in_specs += [pl.BlockSpec((1, d, tile), lambda i, c, p, j=j: (i, p[j], c)) for j, d in enumerate(depths)]
    out_specs = [acc_spec, sq_spec]
    out_shape = [
        jax.ShapeDtypeStruct((3, rows, chans), jnp.float32),
        jax.ShapeDtypeStruct((rows, LANES), jnp.float32),
    ]
    extra, aliases = [], {}
    before = 1 + len(arrays) + 2 * len(depths)
    for n, (held, spec) in enumerate(((acc, acc_spec), (square, sq_spec))):
        if held is not None:
            aliases[before + len(extra)] = n
            extra.append(held)
            in_specs.append(spec)
    if parts is not None:
        extra += parts
        in_specs += [pl.BlockSpec((1, KEEP, tile), lambda i, c, p: (i, rows // KEEP - 1, c))] * len(parts)
        out_specs.append(pl.BlockSpec((1, KEEP, tile), lambda i, c, p: (i, 0, c)))
        out_shape.append(jax.ShapeDtypeStruct((3, KEEP, chans), jnp.float32))
    scalars = list(places) + ([] if use_first is None else [use_first])
    part_count = None if parts is None else len(parts)
    return pl.pallas_call(
        functools.partial(
            accumulate_kernel, depths, pairs, width, acc is not None, square is not None, part_count
        ),
        grid_spec=pltpu.PrefetchScalarGridSpec(
            num_scalar_prefetch=1,
            grid=(3, chans // tile),
            in_specs=in_specs,
            out_specs=out_specs,
            scratch_shapes=[pltpu.VMEM((rows, sum(depths)), jnp.bfloat16)],
        ),
        out_shape=out_shape,
        input_output_aliases=aliases,
        compiler_params=pltpu.CompilerParams(vmem_limit_bytes=VMEM_LIMIT),
        cost_estimate=pl.CostEstimate(
            flops=rows * sum(depths) * chans,
            bytes_accessed=6 * sum(depths) * chans,
            transcendentals=0,
        ),
        name="accumulate",
    )(
        jnp.stack([jnp.asarray(n, jnp.int32) for n in scalars]),
        *arrays,
        *[gain.reshape(-1, 1, d) for d in depths],
        *[in_weight] * len(depths),
        *extra,
    )


def pieces_kernel(count, place_ref, gated_ref, w_ref, *refs):
    outs = refs[-count:]
    total = jnp.dot(gated_ref[...], w_ref[...], preferred_element_type=jnp.float32)
    for j in range(count):

        @pl.when(pl.program_id(0) == j)
        def _():
            outs[j][...] = total.astype(outs[j].dtype)


def pieces(out_weight, gated, wanted, *earlier):
    rows, chans = gated.shape
    count = len(wanted)
    out = pl.pallas_call(
        functools.partial(pieces_kernel, count),
        grid_spec=pltpu.PrefetchScalarGridSpec(
            num_scalar_prefetch=1,
            grid=(count,),
            in_specs=[
                pl.BlockSpec((rows, chans), lambda t, p: (0, 0)),
                pl.BlockSpec((chans, chans), lambda t, p: (0, p[t])),
            ]
            + [pl.BlockSpec(memory_space=pl.ANY)] * len(earlier),
            out_specs=[pl.BlockSpec((rows, chans), lambda t, p: (0, 0))] * count,
        ),
        out_shape=[jax.ShapeDtypeStruct((rows, chans), dtype) for place, dtype in wanted],
        compiler_params=pltpu.CompilerParams(vmem_limit_bytes=VMEM_LIMIT),
        cost_estimate=pl.CostEstimate(flops=count * 1000000, bytes_accessed=count * 100000, transcendentals=0),
        name="pieces",
    )(jnp.stack([place.astype(jnp.int32) for place, dtype in wanted]), gated, out_weight, *earlier)
    return list(out)


def finish_kernel(*refs):
    out_ref = refs[-1]
    count = (len(refs) - 1) // 2
    step, per_half = pl.program_id(0), pl.num_programs(0) // 2

    for h in range(2):

        @pl.when((step >= h * per_half) & (step < (h + 1) * per_half))
        def _():
            total = refs[h * count][...].astype(jnp.float32)
            for ref in refs[h * count + 1 : (h + 1) * count]:
                total = total + ref[...].astype(jnp.float32)
            out_ref[...] = total.astype(jnp.bfloat16)


def finish(upper, lower):
    rows, chans = upper[0].shape
    blk = min(128, rows)
    per_half = rows // blk
    spec = lambda h: pl.BlockSpec((blk, chans), lambda t: (jnp.clip(t - h * per_half, 0, per_half - 1), 0))
    return pl.pallas_call(
        finish_kernel,
        grid=(2 * per_half,),
        in_specs=[spec(0)] * len(upper) + [spec(1)] * len(lower),
        out_specs=pl.BlockSpec((blk, chans), lambda t: (t, 0)),
        out_shape=jax.ShapeDtypeStruct((2 * rows, chans), jnp.bfloat16),
        compiler_params=pltpu.CompilerParams(vmem_limit_bytes=VMEM_LIMIT),
        name="finish",
    )(*upper, *lower)


def along_line(block, pairs):
    return lax.ppermute(block, "chan", [(2 * a + y, 2 * b + y) for a, b in pairs for y in (0, 1)])


def after(block, *earlier):
    return lax.optimization_barrier((block,) + earlier)[0]


def across(block, *earlier):
    count = lax.axis_size("chan")
    if earlier:
        block = after(block, *earlier)
    return lax.ppermute(block, "chan", [(c, c ^ 1) for c in range(count)])


def total(*terms):
    return functools.reduce(lambda a, b: a + b, [t.astype(jnp.float32) for t in terms])


PAIRS = [(0, 1), (1, 0), (2, 3), (3, 2)]
MIDDLE = [(1, 2), (2, 1)]
OUTWARD = [(1, 0), (2, 3)]
INWARD = [(0, 1), (3, 2)]


def gather_and_project(tokens, gain, in_weight, params):
    me = lax.axis_index("chan")
    half = tokens.shape[1] // 2
    at_end = (me < 2) | (me >= 6)
    own_over = across(tokens)
    next_one = along_line(tokens, PAIRS)
    middle = along_line(tokens, MIDDLE)
    acc, square = accumulate([tokens], [me], gain, in_weight)
    next_over = across(next_one, own_over, square)
    second_out = along_line(after(middle, square), OUTWARD)
    second_mid = along_line(after(next_one, square), MIDDLE)
    square, *params = lax.optimization_barrier((square, *params))
    acc, square = accumulate([own_over, next_one], [me ^ 1, me ^ 2], gain, in_weight, acc, square)
    second = jnp.where(at_end, second_out, second_mid)
    second_over = across(second, next_over, square)
    third_out = along_line(after(second_mid, second_out, square), OUTWARD)
    rest_mid = along_line(after(own_over[:, half:], second_mid, square), MIDDLE)
    acc, square = accumulate([next_over, second], [me ^ 3, me ^ 4], gain, in_weight, acc, square)
    third_over = across(jnp.where(at_end, third_out[:, :half], middle[:, :half]), second_over, square)
    rest_out = along_line(after(second_over[:, half:], square), OUTWARD)
    third = (third_out, middle)
    more, square = accumulate(
        [second_over, third], [me ^ 5, me ^ 6], gain, in_weight, None, square, use_first=at_end
    )
    place = (me ^ 7) * 2
    rest, inv_rms, rim = accumulate(
        [third_over, (rest_out, rest_mid)],
        [place, place + 1],
        gain,
        in_weight,
        None,
        square,
        [acc, more],
        use_first=at_end,
    )
    return [acc, more, rest], inv_rms, rim, params


def project_and_reduce(upper, lower, out_weight, tokens):
    me = lax.axis_index("chan")
    half = tokens.shape[0] // 2
    send = lambda k: (me ^ (2 * k + 1), jnp.bfloat16)
    keep = lambda k: (me ^ (2 * k), jnp.float32)
    narrow = lambda a: a.astype(jnp.bfloat16)
    make = functools.partial(pieces, out_weight)
    both = (0, 1)

    third_send_0 = make(upper, [send(3)])[0]
    third_over = across(third_send_0)
    lower = lower(third_send_0)
    third_send_1 = make(lower, [send(3)])[0]
    rest_in = along_line(third_send_1, INWARD)
    rest_mid = along_line(third_send_1, MIDDLE)
    second_send_0, third_keep_0 = make(upper, [send(2), keep(3)], third_send_1)
    second_send_1, third_1 = make(lower, [send(2), (keep(3)[0], jnp.bfloat16)], second_send_0)
    third = [narrow(total(third_keep_0, third_over)), third_1]
    third_in = [along_line(third[h], INWARD) for h in both]
    second_send = [second_send_0, narrow(total(second_send_1, rest_in))]
    second_over = [across(second_send[h], third_over) for h in both]
    halves = (upper, lower)
    later = [make(halves[h], [keep(2), send(1)], (third_over, second_send[1])[h]) for h in both]
    second = [narrow(total(later[h][0], second_over[h], third_in[h])) for h in both]
    second_in = [along_line(second[h], INWARD) for h in both]
    second_mid = [along_line(second[h], MIDDLE) for h in both]
    next_over = [across(later[h][1], second_over[h]) for h in both]
    later = [make(halves[h], [keep(1), send(0)], third_over) for h in both]
    own_send = [later[0][1], narrow(total(later[1][1], rest_mid))]
    next_one = [narrow(total(later[h][0], next_over[h], second_mid[h])) for h in both]
    next_in = [along_line(next_one[h], PAIRS) for h in both]
    middle_in = [along_line(narrow(total(third[h], second_in[h])), MIDDLE) for h in both]
    own_over = [across(own_send[h], next_over[h]) for h in both]
    own_keep = [make(halves[h], [keep(0)], second_over[0])[0] for h in both]
    base = [total(own_keep[h], tokens[h * half : (h + 1) * half]) for h in both]
    return finish(*[[base[h], own_over[h], next_in[h], middle_in[h]] for h in both])


def convolve_kernel(part_count, *refs):
    part_refs, refs = refs[:part_count], refs[part_count:]
    rms_ref, rim_ref, taps_ref, decay_ref, q_ref, prod_ref, end_ref, win_ref, state_ref = refs
    step = pl.program_id(0)
    rows = q_ref.shape[0]
    tap_count, groups = taps_ref.shape[1:3]
    poles = decay_ref.shape[0]
    keep = rim_ref.shape[1]
    unroll = 8

    @pl.when(step == 0)
    def _():
        for g in range(groups):
            win_ref[:, :keep, g, :] = rim_ref[:, :, g * LANES : (g + 1) * LANES]
        state_ref[...] = jnp.zeros_like(state_ref)

    inv_rms = rms_ref[:, :1]
    for i in range(3):
        for g in range(groups):
            cols = tree_sum([ref[i, :, g * LANES : (g + 1) * LANES] for ref in part_refs]) * inv_rms
            win_ref[i, keep:, g, :] = cols.astype(jnp.bfloat16).astype(jnp.float32)
    decay = [jnp.exp(decay_ref[n]) for n in range(poles)]

    def advance(blk, state):
        state = list(state)
        first = blk * unroll
        conv = []
        for i in range(3):
            taps = [taps_ref[i, j] for j in range(tap_count)]
            held = [win_ref[i, first + keep - (tap_count - 1) + r] for r in range(unroll + tap_count - 1)]
            conv.append(
                [
                    functools.reduce(
                        lambda a, b: a + b, [taps[j] * held[r + tap_count - 1 - j] for j in range(tap_count)]
                    )
                    for r in range(unroll)
                ]
            )
        for r in range(unroll):
            q_ref[first + r] = conv[0][r]
            product = conv[1][r] * conv[2][r]
            prod_ref[first + r] = product
            for n in range(poles):
                state[n] = decay[n] * state[n] + product
        return tuple(state)

    state = lax.fori_loop(0, rows // unroll, advance, tuple(state_ref[n] for n in range(poles)))
    for n in range(poles):
        state_ref[n] = state[n]
    win_ref[:, :keep] = win_ref[:, rows:]

    @pl.when(step == pl.num_programs(0) - 1)
    def _():
        for n in range(poles):
            end_ref[n] = state[n]


def convolve(parts, inv_rms, rim, taps, log_decay):
    rows, chans = parts[0].shape[1:]
    groups = chans // LANES
    tap_count, poles = taps.shape[1], log_decay.shape[0]
    keep = rim.shape[1]
    blk = min(128, rows)
    whole = lambda *shape: pl.BlockSpec(shape, lambda t: (0,) * len(shape))
    row_spec = pl.BlockSpec((blk, groups, LANES), lambda t: (t, 0, 0))
    return pl.pallas_call(
        functools.partial(convolve_kernel, len(parts)),
        grid=(rows // blk,),
        in_specs=[pl.BlockSpec((3, blk, chans), lambda t: (0, t, 0))] * len(parts)
        + [
            pl.BlockSpec((blk, LANES), lambda t: (t, 0)),
            whole(3, keep, chans),
            whole(3, tap_count, groups, LANES),
            whole(poles, groups, LANES),
        ],
        out_specs=[row_spec, row_spec, whole(poles, groups, LANES)],
        out_shape=[
            jax.ShapeDtypeStruct((rows, groups, LANES), jnp.float32),
            jax.ShapeDtypeStruct((rows, groups, LANES), jnp.float32),
            jax.ShapeDtypeStruct((poles, groups, LANES), jnp.float32),
        ],
        scratch_shapes=[
            pltpu.VMEM((3, keep + blk, groups, LANES), jnp.float32),
            pltpu.VMEM((poles, groups, LANES), jnp.float32),
        ],
        compiler_params=pltpu.CompilerParams(vmem_limit_bytes=VMEM_LIMIT),
        cost_estimate=pl.CostEstimate(
            flops=110 * rows * groups * LANES, bytes_accessed=20 * rows * groups * LANES, transcendentals=0
        ),
        name="convolve",
    )(*parts, inv_rms, rim, taps, log_decay)


def respond_kernel(q_ref, prod_ref, enter_ref, decay_ref, res_ref, skip_ref, *refs):
    out_ref, end_ref, state_ref, row_ref = refs[-4:]
    step = pl.program_id(0)
    rows, groups = q_ref.shape[:2]
    poles = decay_ref.shape[0]
    unroll = 8

    @pl.when(step == 0)
    def _():
        state_ref[...] = enter_ref[...]

    decay = [jnp.exp(decay_ref[n]) for n in range(poles)]
    res = [res_ref[n] for n in range(poles)]
    skip = skip_ref[0]

    def recur(blk, state):
        state = list(state)
        for r in range(unroll):
            t = blk * unroll + r
            product = prod_ref[t]
            sums = [skip * product]
            for n in range(poles):
                state[n] = decay[n] * state[n] + product
                term = res[n] * state[n]
                if n < 3:
                    sums.append(term)
                else:
                    sums[n % 4] = sums[n % 4] + term
            row_ref[t] = q_ref[t] * tree_sum(sums)
        return tuple(state)

    state = lax.fori_loop(0, rows // unroll, recur, tuple(state_ref[n] for n in range(poles)))
    for n in range(poles):
        state_ref[n] = state[n]
        end_ref[n] = state[n]
    for g in range(groups):
        out_ref[:, g * LANES : (g + 1) * LANES] = row_ref[:, g, :].astype(jnp.bfloat16)


def respond(query, product, enter, log_decay, residue, skip, start, rows, *earlier):
    groups = query.shape[1]
    poles = log_decay.shape[0]
    blk = min(128, rows)
    whole = lambda *shape: pl.BlockSpec(shape, lambda t: (0,) * len(shape))
    row_spec = pl.BlockSpec((blk, groups, LANES), lambda t: (t + start // blk, 0, 0))
    return pl.pallas_call(
        respond_kernel,
        grid=(rows // blk,),
        in_specs=[row_spec, row_spec]
        + [whole(poles, groups, LANES)] * 3
        + [whole(1, groups, LANES)]
        + [pl.BlockSpec(memory_space=pl.ANY)] * len(earlier),
        out_specs=[pl.BlockSpec((blk, groups * LANES), lambda t: (t, 0)), whole(poles, groups, LANES)],
        out_shape=[
            jax.ShapeDtypeStruct((rows, groups * LANES), jnp.bfloat16),
            jax.ShapeDtypeStruct((poles, groups, LANES), jnp.float32),
        ],
        scratch_shapes=[
            pltpu.VMEM((poles, groups, LANES), jnp.float32),
            pltpu.VMEM((blk, groups, LANES), jnp.float32),
        ],
        compiler_params=pltpu.CompilerParams(vmem_limit_bytes=VMEM_LIMIT),
        cost_estimate=pl.CostEstimate(
            flops=70 * rows * groups * LANES, bytes_accessed=80 * rows * groups * LANES, transcendentals=0
        ),
        name="respond",
    )(query, product, enter, log_decay, residue, skip, *earlier)


def per_device(tokens, norm_gain, in_weight, short_weight, log_decay, residue, skip, out_weight):
    rows, chans = tokens.shape
    groups = chans // LANES
    by_lane = lambda a: a.reshape(a.shape[:-1] + (groups, LANES))
    taps, log_decay, residue = by_lane(short_weight), by_lane(log_decay), by_lane(residue)
    skip = by_lane(skip[None, :])

    paired_line = lax.axis_size("chan") == 8
    if paired_line:
        params = (taps, log_decay, residue, skip)
        parts, inv_rms, rim, params = gather_and_project(tokens, norm_gain, in_weight, params)
        taps, log_decay, residue, skip = params
    else:
        gathered = lax.all_gather(tokens, "chan", axis=1, tiled=True)
        depth = min(1024, gathered.shape[1])
        chunks = [gathered[:, k : k + depth] for k in range(0, gathered.shape[1], depth)]
        acc = square = None
        for k, chunk in enumerate(chunks[:-1]):
            acc, square = accumulate([chunk], [k], norm_gain, in_weight, acc, square)
        acc, inv_rms, rim = accumulate(chunks[-1:], [len(chunks) - 1], norm_gain, in_weight, acc, square, [])
        parts = [acc]
    rim = from_behind(rim, "seq", 1)
    query, product, end = convolve(parts, inv_rms, rim, taps, log_decay)
    shard_decay = jnp.exp(rows * log_decay)
    state, passing = jnp.zeros_like(end), end
    for _ in range(lax.axis_size("seq") - 1):
        passing = from_behind(passing, "seq", 1)
        state = state + passing
        passing = passing * shard_decay
    filt = (log_decay, residue, skip)
    if paired_line:
        half = rows // 2
        upper, state = respond(query, product, state, *filt, 0, half)
        lower = lambda *earlier: respond(query, product, state, *filt, half, half, *earlier)[0]
        return project_and_reduce(upper, lower, out_weight, tokens)
    gated = respond(query, product, state, *filt, 0, rows)[0]
    partial = jnp.dot(gated, out_weight, preferred_element_type=jnp.float32)
    branch = lax.psum_scatter(partial.astype(jnp.bfloat16), "chan", scatter_dimension=1, tiled=True)
    return (tokens.astype(jnp.float32) + branch.astype(jnp.float32)).astype(jnp.bfloat16)


def solution(mesh):
    return jax.shard_map(
        per_device,
        mesh=mesh,
        in_specs=(
            P(("groups", "seq"), "chan"),
            P(),
            P(None, None, "chan"),
            P(None, None, "chan"),
            P(None, "chan"),
            P(None, "chan"),
            P("chan"),
            P("chan", None),
        ),
        out_specs=P(("groups", "seq"), "chan"),
        check_vma=False,
    )
```

```python
import functools

import jax
import jax.numpy as jnp
from jax import lax
from jax.experimental import pallas as pl
from jax.experimental.pallas import tpu as pltpu
from jax.sharding import PartitionSpec as P

EPSILON = 1e-06
LANES = 128
KEEP = 8
VMEM_LIMIT = 48 * 1024 * 1024


def from_behind(block, axis, distance):
    count = lax.axis_size(axis)
    route = [(i - distance, i) for i in range(count) if i - distance >= 0]
    return lax.ppermute(block, axis, route)


def tree_sum(terms):
    while len(terms) > 1:
        pairs = [terms[i] + terms[i + 1] for i in range(0, len(terms) - 1, 2)]
        terms = pairs + terms[len(pairs) * 2 :]
    return terms[0]


def accumulate_kernel(depths, pairs, width, has_acc, has_sq, part_count, place_ref, *refs):
    def take(count):
        nonlocal refs
        taken, refs = refs[:count], refs[count:]
        return taken

    chunk_refs = take(len(depths) + sum(pairs))
    gain_refs, w_refs = take(len(depths)), take(len(depths))
    held_refs, held_sq_refs = take(int(has_acc)), take(int(has_sq))
    part_refs = take(part_count or 0)
    acc_ref, sq_ref = take(2)
    scaled_ref = refs[-1]
    feat, col = pl.program_id(0), pl.program_id(1)
    last = part_count is not None

    @pl.when((feat == 0) & (col == 0))
    def _():
        square = held_sq_refs[0][...] if has_sq else None
        start = at = 0
        for j, depth in enumerate(depths):
            x = chunk_refs[at][...]
            at += 1
            if pairs[j]:
                x = jnp.where(place_ref[len(depths)] == 1, x, chunk_refs[at][...])
                at += 1
            x = x.astype(jnp.float32)
            parts = [x[:, g : g + LANES] * x[:, g : g + LANES] for g in range(0, depth, LANES)]
            part = tree_sum(parts)
            square = part if square is None else square + part
            scaled_ref[:, start : start + depth] = (x * gain_refs[j][0]).astype(jnp.bfloat16)
            start += depth
        if last:
            total = jnp.sum(square, axis=1, keepdims=True)
            square = jnp.broadcast_to(lax.rsqrt(total / width + EPSILON), square.shape)
        sq_ref[...] = square

    start, part = 0, None
    for j, depth in enumerate(depths):
        one = jnp.dot(scaled_ref[:, start : start + depth], w_refs[j][0], preferred_element_type=jnp.float32)
        part = one if part is None else part + one
        start += depth
    acc_ref[0] = held_refs[0][0] + part if has_acc else part
    if last:
        rim_ref = refs[0]
        keep = rim_ref.shape[1]
        rows = acc_ref.shape[1]
        rim = acc_ref[0, rows - keep :, :]
        for ref in part_refs:
            rim = rim + ref[0]
        rim_ref[0] = (rim * sq_ref[rows - keep :, :1]).astype(jnp.bfloat16).astype(jnp.float32)


def accumulate(chunks, places, gain, in_weight, acc=None, square=None, parts=None, use_first=None):
    pairs = [isinstance(c, tuple) for c in chunks]
    arrays = [a for c in chunks for a in (c if isinstance(c, tuple) else (c,))]
    depths = [(c[0] if isinstance(c, tuple) else c).shape[1] for c in chunks]
    rows = arrays[0].shape[0]
    width, chans = in_weight.shape[1:]
    tile = min(512, chans)
    acc_spec = pl.BlockSpec((1, rows, tile), lambda i, c, p: (i, 0, c))
    sq_spec = pl.BlockSpec((rows, LANES), lambda i, c, p: (0, 0))
    in_specs = [pl.BlockSpec(a.shape, lambda i, c, p: (0, 0)) for a in arrays]
    in_specs += [pl.BlockSpec((1, 1, d), lambda i, c, p, j=j: (p[j], 0, 0)) for j, d in enumerate(depths)]
    in_specs += [pl.BlockSpec((1, d, tile), lambda i, c, p, j=j: (i, p[j], c)) for j, d in enumerate(depths)]
    out_specs = [acc_spec, sq_spec]
    out_shape = [
        jax.ShapeDtypeStruct((3, rows, chans), jnp.float32),
        jax.ShapeDtypeStruct((rows, LANES), jnp.float32),
    ]
    extra, aliases = [], {}
    before = 1 + len(arrays) + 2 * len(depths)
    for n, (held, spec) in enumerate(((acc, acc_spec), (square, sq_spec))):
        if held is not None:
            aliases[before + len(extra)] = n
            extra.append(held)
            in_specs.append(spec)
    if parts is not None:
        extra += parts
        in_specs += [pl.BlockSpec((1, KEEP, tile), lambda i, c, p: (i, rows // KEEP - 1, c))] * len(parts)
        out_specs.append(pl.BlockSpec((1, KEEP, tile), lambda i, c, p: (i, 0, c)))
        out_shape.append(jax.ShapeDtypeStruct((3, KEEP, chans), jnp.float32))
    scalars = list(places) + ([] if use_first is None else [use_first])
    part_count = None if parts is None else len(parts)
    return pl.pallas_call(
        functools.partial(
            accumulate_kernel, depths, pairs, width, acc is not None, square is not None, part_count
        ),
        grid_spec=pltpu.PrefetchScalarGridSpec(
            num_scalar_prefetch=1,
            grid=(3, chans // tile),
            in_specs=in_specs,
            out_specs=out_specs,
            scratch_shapes=[pltpu.VMEM((rows, sum(depths)), jnp.bfloat16)],
        ),
        out_shape=out_shape,
        input_output_aliases=aliases,
        compiler_params=pltpu.CompilerParams(vmem_limit_bytes=VMEM_LIMIT),
        cost_estimate=pl.CostEstimate(
            flops=rows * sum(depths) * chans,
            bytes_accessed=6 * sum(depths) * chans,
            transcendentals=0,
        ),
        name="accumulate",
    )(
        jnp.stack([jnp.asarray(n, jnp.int32) for n in scalars]),
        *arrays,
        *[gain.reshape(-1, 1, d) for d in depths],
        *[in_weight] * len(depths),
        *extra,
    )


def pieces_kernel(count, place_ref, gated_ref, w_ref, *refs):
    outs = refs[-count:]
    total = jnp.dot(gated_ref[...], w_ref[...], preferred_element_type=jnp.float32)
    for j in range(count):

        @pl.when(pl.program_id(0) == j)
        def _():
            outs[j][...] = total.astype(outs[j].dtype)


def pieces(out_weight, gated, wanted, *earlier):
    rows, chans = gated.shape
    count = len(wanted)
    out = pl.pallas_call(
        functools.partial(pieces_kernel, count),
        grid_spec=pltpu.PrefetchScalarGridSpec(
            num_scalar_prefetch=1,
            grid=(count,),
            in_specs=[
                pl.BlockSpec((rows, chans), lambda t, p: (0, 0)),
                pl.BlockSpec((chans, chans), lambda t, p: (0, p[t])),
            ]
            + [pl.BlockSpec(memory_space=pl.ANY)] * len(earlier),
            out_specs=[pl.BlockSpec((rows, chans), lambda t, p: (0, 0))] * count,
        ),
        out_shape=[jax.ShapeDtypeStruct((rows, chans), dtype) for place, dtype in wanted],
        compiler_params=pltpu.CompilerParams(vmem_limit_bytes=VMEM_LIMIT),
        cost_estimate=pl.CostEstimate(flops=count * 1000000, bytes_accessed=count * 100000, transcendentals=0),
        name="pieces",
    )(jnp.stack([place.astype(jnp.int32) for place, dtype in wanted]), gated, out_weight, *earlier)
    return list(out)


def finish_kernel(*refs):
    out_ref = refs[-1]
    count = (len(refs) - 1) // 2
    step, per_half = pl.program_id(0), pl.num_programs(0) // 2

    for h in range(2):

        @pl.when((step >= h * per_half) & (step < (h + 1) * per_half))
        def _():
            total = refs[h * count][...].astype(jnp.float32)
            for ref in refs[h * count + 1 : (h + 1) * count]:
                total = total + ref[...].astype(jnp.float32)
            out_ref[...] = total.astype(jnp.bfloat16)


def finish(upper, lower):
    rows, chans = upper[0].shape
    blk = min(128, rows)
    per_half = rows // blk
    spec = lambda h: pl.BlockSpec((blk, chans), lambda t: (jnp.clip(t - h * per_half, 0, per_half - 1), 0))
    return pl.pallas_call(
        finish_kernel,
        grid=(2 * per_half,),
        in_specs=[spec(0)] * len(upper) + [spec(1)] * len(lower),
        out_specs=pl.BlockSpec((blk, chans), lambda t: (t, 0)),
        out_shape=jax.ShapeDtypeStruct((2 * rows, chans), jnp.bfloat16),
        compiler_params=pltpu.CompilerParams(vmem_limit_bytes=VMEM_LIMIT),
        name="finish",
    )(*upper, *lower)


def along_line(block, pairs):
    return lax.ppermute(block, "chan", [(2 * a + y, 2 * b + y) for a, b in pairs for y in (0, 1)])


def after(block, *earlier):
    return lax.optimization_barrier((block,) + earlier)[0]


def across(block, *earlier):
    count = lax.axis_size("chan")
    if earlier:
        block = after(block, *earlier)
    return lax.ppermute(block, "chan", [(c, c ^ 1) for c in range(count)])


def total(*terms):
    return functools.reduce(lambda a, b: a + b, [t.astype(jnp.float32) for t in terms])


PAIRS = [(0, 1), (1, 0), (2, 3), (3, 2)]
MIDDLE = [(1, 2), (2, 1)]
OUTWARD = [(1, 0), (2, 3)]
INWARD = [(0, 1), (3, 2)]


def gather_and_project(tokens, gain, in_weight, params):
    me = lax.axis_index("chan")
    half = tokens.shape[1] // 2
    at_end = (me < 2) | (me >= 6)
    own_over = across(tokens)
    next_one = along_line(tokens, PAIRS)
    middle = along_line(tokens, MIDDLE)
    acc, square = accumulate([tokens], [me], gain, in_weight)
    next_over = across(next_one, own_over, square)
    second_out = along_line(after(middle, square), OUTWARD)
    second_mid = along_line(after(next_one, square), MIDDLE)
    square, *params = lax.optimization_barrier((square, *params))
    acc, square = accumulate([own_over, next_one], [me ^ 1, me ^ 2], gain, in_weight, acc, square)
    second = jnp.where(at_end, second_out, second_mid)
    second_over = across(second, next_over, square)
    third_out = along_line(after(second_mid, second_out, square), OUTWARD)
    rest_mid = along_line(after(own_over[:, half:], second_mid, square), MIDDLE)
    acc, square = accumulate([next_over, second], [me ^ 3, me ^ 4], gain, in_weight, acc, square)
    third_over = across(jnp.where(at_end, third_out[:, :half], middle[:, :half]), second_over, square)
    rest_out = along_line(after(second_over[:, half:], square), OUTWARD)
    third = (third_out, middle)
    more, square = accumulate(
        [second_over, third], [me ^ 5, me ^ 6], gain, in_weight, None, square, use_first=at_end
    )
    place = (me ^ 7) * 2
    rest, inv_rms, rim = accumulate(
        [third_over, (rest_out, rest_mid)],
        [place, place + 1],
        gain,
        in_weight,
        None,
        square,
        [acc, more],
        use_first=at_end,
    )
    return [acc, more, rest], inv_rms, rim, params


def project_and_reduce(upper, lower, out_weight, tokens):
    me = lax.axis_index("chan")
    half = tokens.shape[0] // 2
    send = lambda k: (me ^ (2 * k + 1), jnp.bfloat16)
    keep = lambda k: (me ^ (2 * k), jnp.float32)
    narrow = lambda a: a.astype(jnp.bfloat16)
    make = functools.partial(pieces, out_weight)
    both = (0, 1)

    third_send_0 = make(upper, [send(3)])[0]
    third_over = across(third_send_0)
    lower = lower(third_send_0)
    third_send_1 = make(lower, [send(3)])[0]
    rest_in = along_line(third_send_1, INWARD)
    rest_mid = along_line(third_send_1, MIDDLE)
    second_send_0, third_keep_0 = make(upper, [send(2), keep(3)], third_send_1)
    second_send_1, third_1 = make(lower, [send(2), (keep(3)[0], jnp.bfloat16)], second_send_0)
    third = [narrow(total(third_keep_0, third_over)), third_1]
    third_in = [along_line(third[h], INWARD) for h in both]
    second_send = [second_send_0, narrow(total(second_send_1, rest_in))]
    second_over = [across(second_send[h], third_over) for h in both]
    halves = (upper, lower)
    later = [make(halves[h], [keep(2), send(1)], (third_over, second_send[1])[h]) for h in both]
    second = [narrow(total(later[h][0], second_over[h], third_in[h])) for h in both]
    second_in = [along_line(second[h], INWARD) for h in both]
    second_mid = [along_line(second[h], MIDDLE) for h in both]
    next_over = [across(later[h][1], second_over[h]) for h in both]
    later = [make(halves[h], [keep(1), send(0)], third_over) for h in both]
    own_send = [later[0][1], narrow(total(later[1][1], rest_mid))]
    next_one = [narrow(total(later[h][0], next_over[h], second_mid[h])) for h in both]
    next_in = [along_line(next_one[h], PAIRS) for h in both]
    middle_in = [along_line(narrow(total(third[h], second_in[h])), MIDDLE) for h in both]
    own_over = [across(own_send[h], next_over[h]) for h in both]
    own_keep = [make(halves[h], [keep(0)], second_over[0])[0] for h in both]
    base = [total(own_keep[h], tokens[h * half : (h + 1) * half]) for h in both]
    return finish(*[[base[h], own_over[h], next_in[h], middle_in[h]] for h in both])


def convolve_kernel(part_count, *refs):
    part_refs, refs = refs[:part_count], refs[part_count:]
    rms_ref, rim_ref, taps_ref, decay_ref, q_ref, prod_ref, end_ref, win_ref, state_ref = refs
    step = pl.program_id(0)
    rows = q_ref.shape[0]
    tap_count, groups = taps_ref.shape[1:3]
    poles = decay_ref.shape[0]
    keep = rim_ref.shape[1]
    unroll = 8

    @pl.when(step == 0)
    def _():
        for g in range(groups):
            for i in range(3):
                win_ref[i, pl.ds(g, keep, stride=groups), :] = rim_ref[i, :, g * LANES : (g + 1) * LANES]
        state_ref[...] = jnp.zeros_like(state_ref)

    inv_rms = rms_ref[:, :1]
    for i in range(3):
        for g in range(groups):
            cols = tree_sum([ref[i, :, g * LANES : (g + 1) * LANES] for ref in part_refs]) * inv_rms
            cols = cols.astype(jnp.bfloat16).astype(jnp.float32)
            win_ref[i, pl.ds(keep * groups + g, rows, stride=groups), :] = cols
    decay = [jnp.exp(decay_ref[n]) for n in range(poles)]

    def row_of(i, t):
        return win_ref[i, pl.ds(pl.multiple_of(t * groups, groups), groups), :]

    def advance(blk, state):
        state = list(state)
        first = blk * unroll
        conv = []
        for i in range(3):
            taps = [taps_ref[i, j] for j in range(tap_count)]
            held = [row_of(i, first + keep - (tap_count - 1) + r) for r in range(unroll + tap_count - 1)]
            conv.append(
                [
                    functools.reduce(
                        lambda a, b: a + b, [taps[j] * held[r + tap_count - 1 - j] for j in range(tap_count)]
                    )
                    for r in range(unroll)
                ]
            )
        for r in range(unroll):
            q_ref[first + r] = conv[0][r]
            product = conv[1][r] * conv[2][r]
            prod_ref[first + r] = product
            for n in range(poles):
                state[n] = decay[n] * state[n] + product
        return tuple(state)

    state = lax.fori_loop(0, rows // unroll, advance, tuple(state_ref[n] for n in range(poles)))
    for n in range(poles):
        state_ref[n] = state[n]
    win_ref[:, : keep * groups] = win_ref[:, rows * groups :]

    @pl.when(step == pl.num_programs(0) - 1)
    def _():
        for n in range(poles):
            end_ref[n] = state[n]


def convolve(parts, inv_rms, rim, taps, log_decay):
    rows, chans = parts[0].shape[1:]
    groups = chans // LANES
    tap_count, poles = taps.shape[1], log_decay.shape[0]
    keep = rim.shape[1]
    blk = min(128, rows)
    whole = lambda *shape: pl.BlockSpec(shape, lambda t: (0,) * len(shape))
    row_spec = pl.BlockSpec((blk, groups, LANES), lambda t: (t, 0, 0))
    return pl.pallas_call(
        functools.partial(convolve_kernel, len(parts)),
        grid=(rows // blk,),
        in_specs=[pl.BlockSpec((3, blk, chans), lambda t: (0, t, 0))] * len(parts)
        + [
            pl.BlockSpec((blk, LANES), lambda t: (t, 0)),
            whole(3, keep, chans),
            whole(3, tap_count, groups, LANES),
            whole(poles, groups, LANES),
        ],
        out_specs=[row_spec, row_spec, whole(poles, groups, LANES)],
        out_shape=[
            jax.ShapeDtypeStruct((rows, groups, LANES), jnp.float32),
            jax.ShapeDtypeStruct((rows, groups, LANES), jnp.float32),
            jax.ShapeDtypeStruct((poles, groups, LANES), jnp.float32),
        ],
        scratch_shapes=[
            pltpu.VMEM((3, (keep + blk) * groups, LANES), jnp.float32),
            pltpu.VMEM((poles, groups, LANES), jnp.float32),
        ],
        compiler_params=pltpu.CompilerParams(vmem_limit_bytes=VMEM_LIMIT),
        cost_estimate=pl.CostEstimate(
            flops=110 * rows * groups * LANES, bytes_accessed=20 * rows * groups * LANES, transcendentals=0
        ),
        name="convolve",
    )(*parts, inv_rms, rim, taps, log_decay)


def respond_kernel(q_ref, prod_ref, enter_ref, decay_ref, res_ref, skip_ref, *refs):
    out_ref, end_ref, state_ref, row_ref = refs[-4:]
    step = pl.program_id(0)
    rows, groups = q_ref.shape[:2]
    poles = decay_ref.shape[0]
    unroll = 8

    @pl.when(step == 0)
    def _():
        state_ref[...] = enter_ref[...]

    decay = [jnp.exp(decay_ref[n]) for n in range(poles)]
    res = [res_ref[n] for n in range(poles)]
    skip = skip_ref[0]

    def recur(blk, state):
        state = list(state)
        for r in range(unroll):
            t = blk * unroll + r
            product = prod_ref[t]
            sums = [skip * product]
            for n in range(poles):
                state[n] = decay[n] * state[n] + product
                term = res[n] * state[n]
                if n < 3:
                    sums.append(term)
                else:
                    sums[n % 4] = sums[n % 4] + term
            row_ref[pl.ds(pl.multiple_of(t * groups, groups), groups), :] = q_ref[t] * tree_sum(sums)
        return tuple(state)

    state = lax.fori_loop(0, rows // unroll, recur, tuple(state_ref[n] for n in range(poles)))
    for n in range(poles):
        state_ref[n] = state[n]
        end_ref[n] = state[n]
    for g in range(groups):
        out_ref[:, g * LANES : (g + 1) * LANES] = row_ref[pl.ds(g, rows, stride=groups), :].astype(jnp.bfloat16)


def respond(query, product, enter, log_decay, residue, skip, start, rows, *earlier):
    groups = query.shape[1]
    poles = log_decay.shape[0]
    blk = min(128, rows)
    whole = lambda *shape: pl.BlockSpec(shape, lambda t: (0,) * len(shape))
    row_spec = pl.BlockSpec((blk, groups, LANES), lambda t: (t + start // blk, 0, 0))
    return pl.pallas_call(
        respond_kernel,
        grid=(rows // blk,),
        in_specs=[row_spec, row_spec]
        + [whole(poles, groups, LANES)] * 3
        + [whole(1, groups, LANES)]
        + [pl.BlockSpec(memory_space=pl.ANY)] * len(earlier),
        out_specs=[pl.BlockSpec((blk, groups * LANES), lambda t: (t, 0)), whole(poles, groups, LANES)],
        out_shape=[
            jax.ShapeDtypeStruct((rows, groups * LANES), jnp.bfloat16),
            jax.ShapeDtypeStruct((poles, groups, LANES), jnp.float32),
        ],
        scratch_shapes=[
            pltpu.VMEM((poles, groups, LANES), jnp.float32),
            pltpu.VMEM((blk * groups, LANES), jnp.float32),
        ],
        compiler_params=pltpu.CompilerParams(vmem_limit_bytes=VMEM_LIMIT),
        cost_estimate=pl.CostEstimate(
            flops=70 * rows * groups * LANES, bytes_accessed=80 * rows * groups * LANES, transcendentals=0
        ),
        name="respond",
    )(query, product, enter, log_decay, residue, skip, *earlier)


def per_device(tokens, norm_gain, in_weight, short_weight, log_decay, residue, skip, out_weight):
    rows, chans = tokens.shape
    groups = chans // LANES
    by_lane = lambda a: a.reshape(a.shape[:-1] + (groups, LANES))
    taps, log_decay, residue = by_lane(short_weight), by_lane(log_decay), by_lane(residue)
    skip = by_lane(skip[None, :])

    paired_line = lax.axis_size("chan") == 8
    if paired_line:
        params = (taps, log_decay, residue, skip)
        parts, inv_rms, rim, params = gather_and_project(tokens, norm_gain, in_weight, params)
        taps, log_decay, residue, skip = params
    else:
        gathered = lax.all_gather(tokens, "chan", axis=1, tiled=True)
        depth = min(1024, gathered.shape[1])
        chunks = [gathered[:, k : k + depth] for k in range(0, gathered.shape[1], depth)]
        acc = square = None
        for k, chunk in enumerate(chunks[:-1]):
            acc, square = accumulate([chunk], [k], norm_gain, in_weight, acc, square)
        acc, inv_rms, rim = accumulate(chunks[-1:], [len(chunks) - 1], norm_gain, in_weight, acc, square, [])
        parts = [acc]
    rim = from_behind(rim, "seq", 1)
    query, product, end = convolve(parts, inv_rms, rim, taps, log_decay)
    shard_decay = jnp.exp(rows * log_decay)
    state, passing = jnp.zeros_like(end), end
    for _ in range(lax.axis_size("seq") - 1):
        passing = from_behind(passing, "seq", 1)
        state = state + passing
        passing = passing * shard_decay
    filt = (log_decay, residue, skip)
    if paired_line:
        half = rows // 2
        upper, state = respond(query, product, state, *filt, 0, half)
        lower = lambda *earlier: respond(query, product, state, *filt, half, half, *earlier)[0]
        return project_and_reduce(upper, lower, out_weight, tokens)
    gated = respond(query, product, state, *filt, 0, rows)[0]
    partial = jnp.dot(gated, out_weight, preferred_element_type=jnp.float32)
    branch = lax.psum_scatter(partial.astype(jnp.bfloat16), "chan", scatter_dimension=1, tiled=True)
    return (tokens.astype(jnp.float32) + branch.astype(jnp.float32)).astype(jnp.bfloat16)


def solution(mesh):
    return jax.shard_map(
        per_device,
        mesh=mesh,
        in_specs=(
            P(("groups", "seq"), "chan"),
            P(),
            P(None, None, "chan"),
            P(None, None, "chan"),
            P(None, "chan"),
            P(None, "chan"),
            P("chan"),
            P("chan", None),
        ),
        out_specs=P(("groups", "seq"), "chan"),
        check_vma=False,
    )
```

```python
import functools

import jax
import jax.numpy as jnp
from jax import lax
from jax.experimental import pallas as pl
from jax.experimental.pallas import tpu as pltpu
from jax.sharding import PartitionSpec as P

EPSILON = 1e-06
LANES = 128
KEEP = 8
VMEM_LIMIT = 48 * 1024 * 1024


def from_behind(block, axis, distance):
    count = lax.axis_size(axis)
    route = [(i - distance, i) for i in range(count) if i - distance >= 0]
    return lax.ppermute(block, axis, route)


def tree_sum(terms):
    while len(terms) > 1:
        pairs = [terms[i] + terms[i + 1] for i in range(0, len(terms) - 1, 2)]
        terms = pairs + terms[len(pairs) * 2 :]
    return terms[0]


def accumulate_kernel(depths, pairs, width, has_acc, has_sq, part_count, place_ref, *refs):
    def take(count):
        nonlocal refs
        taken, refs = refs[:count], refs[count:]
        return taken

    chunk_refs = take(len(depths) + sum(pairs))
    gain_refs, w_refs = take(len(depths)), take(len(depths))
    held_refs, held_sq_refs = take(int(has_acc)), take(int(has_sq))
    part_refs = take(part_count or 0)
    acc_ref, sq_ref = take(2)
    scaled_ref = refs[-1]
    feat, col = pl.program_id(0), pl.program_id(1)
    last = part_count is not None

    @pl.when((feat == 0) & (col == 0))
    def _():
        square = held_sq_refs[0][...] if has_sq else None
        start = at = 0
        for j, depth in enumerate(depths):
            x = chunk_refs[at][...]
            at += 1
            if pairs[j]:
                x = jnp.where(place_ref[len(depths)] == 1, x, chunk_refs[at][...])
                at += 1
            x = x.astype(jnp.float32)
            parts = [x[:, g : g + LANES] * x[:, g : g + LANES] for g in range(0, depth, LANES)]
            part = tree_sum(parts)
            square = part if square is None else square + part
            scaled_ref[:, start : start + depth] = (x * gain_refs[j][0]).astype(jnp.bfloat16)
            start += depth
        if last:
            total = jnp.sum(square, axis=1, keepdims=True)
            square = jnp.broadcast_to(lax.rsqrt(total / width + EPSILON), square.shape)
        sq_ref[...] = square

    start, part = 0, None
    for j, depth in enumerate(depths):
        one = jnp.dot(scaled_ref[:, start : start + depth], w_refs[j][0], preferred_element_type=jnp.float32)
        part = one if part is None else part + one
        start += depth
    acc_ref[0] = held_refs[0][0] + part if has_acc else part
    if last:
        rim_ref = refs[0]
        keep = rim_ref.shape[1]
        rows = acc_ref.shape[1]
        rim = acc_ref[0, rows - keep :, :]
        for ref in part_refs:
            rim = rim + ref[0]
        rim_ref[0] = (rim * sq_ref[rows - keep :, :1]).astype(jnp.bfloat16).astype(jnp.float32)


def accumulate(chunks, places, gain, in_weight, acc=None, square=None, parts=None, use_first=None):
    pairs = [isinstance(c, tuple) for c in chunks]
    arrays = [a for c in chunks for a in (c if isinstance(c, tuple) else (c,))]
    depths = [(c[0] if isinstance(c, tuple) else c).shape[1] for c in chunks]
    rows = arrays[0].shape[0]
    width, chans = in_weight.shape[1:]
    tile = min(512, chans)
    acc_spec = pl.BlockSpec((1, rows, tile), lambda i, c, p: (i, 0, c))
    sq_spec = pl.BlockSpec((rows, LANES), lambda i, c, p: (0, 0))
    in_specs = [pl.BlockSpec(a.shape, lambda i, c, p: (0, 0)) for a in arrays]
    in_specs += [pl.BlockSpec((1, 1, d), lambda i, c, p, j=j: (p[j], 0, 0)) for j, d in enumerate(depths)]
    in_specs += [pl.BlockSpec((1, d, tile), lambda i, c, p, j=j: (i, p[j], c)) for j, d in enumerate(depths)]
    out_specs = [acc_spec, sq_spec]
    out_shape = [
        jax.ShapeDtypeStruct((3, rows, chans), jnp.float32),
        jax.ShapeDtypeStruct((rows, LANES), jnp.float32),
    ]
    extra, aliases = [], {}
    before = 1 + len(arrays) + 2 * len(depths)
    for n, (held, spec) in enumerate(((acc, acc_spec), (square, sq_spec))):
        if held is not None:
            aliases[before + len(extra)] = n
            extra.append(held)
            in_specs.append(spec)
    if parts is not None:
        extra += parts
        in_specs += [pl.BlockSpec((1, KEEP, tile), lambda i, c, p: (i, rows // KEEP - 1, c))] * len(parts)
        out_specs.append(pl.BlockSpec((1, KEEP, tile), lambda i, c, p: (i, 0, c)))
        out_shape.append(jax.ShapeDtypeStruct((3, KEEP, chans), jnp.float32))
    scalars = list(places) + ([] if use_first is None else [use_first])
    part_count = None if parts is None else len(parts)
    return pl.pallas_call(
        functools.partial(
            accumulate_kernel, depths, pairs, width, acc is not None, square is not None, part_count
        ),
        grid_spec=pltpu.PrefetchScalarGridSpec(
            num_scalar_prefetch=1,
            grid=(3, chans // tile),
            in_specs=in_specs,
            out_specs=out_specs,
            scratch_shapes=[pltpu.VMEM((rows, sum(depths)), jnp.bfloat16)],
        ),
        out_shape=out_shape,
        input_output_aliases=aliases,
        compiler_params=pltpu.CompilerParams(vmem_limit_bytes=VMEM_LIMIT),
        cost_estimate=pl.CostEstimate(
            flops=rows * sum(depths) * chans,
            bytes_accessed=6 * sum(depths) * chans,
            transcendentals=0,
        ),
        name="accumulate",
    )(
        jnp.stack([jnp.asarray(n, jnp.int32) for n in scalars]),
        *arrays,
        *[gain.reshape(-1, 1, d) for d in depths],
        *[in_weight] * len(depths),
        *extra,
    )


def pieces_kernel(count, place_ref, gated_ref, w_ref, *refs):
    outs = refs[-count:]
    total = jnp.dot(gated_ref[...], w_ref[...], preferred_element_type=jnp.float32)
    for j in range(count):

        @pl.when(pl.program_id(0) == j)
        def _():
            outs[j][...] = total.astype(outs[j].dtype)


def pieces(out_weight, gated, wanted, *earlier):
    rows, chans = gated.shape
    count = len(wanted)
    out = pl.pallas_call(
        functools.partial(pieces_kernel, count),
        grid_spec=pltpu.PrefetchScalarGridSpec(
            num_scalar_prefetch=1,
            grid=(count,),
            in_specs=[
                pl.BlockSpec((rows, chans), lambda t, p: (0, 0)),
                pl.BlockSpec((chans, chans), lambda t, p: (0, p[t])),
            ]
            + [pl.BlockSpec(memory_space=pl.ANY)] * len(earlier),
            out_specs=[pl.BlockSpec((rows, chans), lambda t, p: (0, 0))] * count,
        ),
        out_shape=[jax.ShapeDtypeStruct((rows, chans), dtype) for place, dtype in wanted],
        compiler_params=pltpu.CompilerParams(vmem_limit_bytes=VMEM_LIMIT),
        cost_estimate=pl.CostEstimate(flops=count * 1000000, bytes_accessed=count * 100000, transcendentals=0),
        name="pieces",
    )(jnp.stack([place.astype(jnp.int32) for place, dtype in wanted]), gated, out_weight, *earlier)
    return list(out)


def finish_kernel(*refs):
    out_ref = refs[-1]
    count = (len(refs) - 1) // 2
    step, per_half = pl.program_id(0), pl.num_programs(0) // 2

    for h in range(2):

        @pl.when((step >= h * per_half) & (step < (h + 1) * per_half))
        def _():
            total = refs[h * count][...].astype(jnp.float32)
            for ref in refs[h * count + 1 : (h + 1) * count]:
                total = total + ref[...].astype(jnp.float32)
            out_ref[...] = total.astype(jnp.bfloat16)


def finish(upper, lower):
    rows, chans = upper[0].shape
    blk = min(128, rows)
    per_half = rows // blk
    spec = lambda h: pl.BlockSpec((blk, chans), lambda t: (jnp.clip(t - h * per_half, 0, per_half - 1), 0))
    return pl.pallas_call(
        finish_kernel,
        grid=(2 * per_half,),
        in_specs=[spec(0)] * len(upper) + [spec(1)] * len(lower),
        out_specs=pl.BlockSpec((blk, chans), lambda t: (t, 0)),
        out_shape=jax.ShapeDtypeStruct((2 * rows, chans), jnp.bfloat16),
        compiler_params=pltpu.CompilerParams(vmem_limit_bytes=VMEM_LIMIT),
        name="finish",
    )(*upper, *lower)


def along_line(block, pairs):
    return lax.ppermute(block, "chan", [(2 * a + y, 2 * b + y) for a, b in pairs for y in (0, 1)])


def after(block, *earlier):
    return lax.optimization_barrier((block,) + earlier)[0]


def across(block, *earlier):
    count = lax.axis_size("chan")
    if earlier:
        block = after(block, *earlier)
    return lax.ppermute(block, "chan", [(c, c ^ 1) for c in range(count)])


def total(*terms):
    return functools.reduce(lambda a, b: a + b, [t.astype(jnp.float32) for t in terms])


PAIRS = [(0, 1), (1, 0), (2, 3), (3, 2)]
MIDDLE = [(1, 2), (2, 1)]
OUTWARD = [(1, 0), (2, 3)]
INWARD = [(0, 1), (3, 2)]


def gather_and_project(tokens, gain, in_weight, params):
    me = lax.axis_index("chan")
    half = tokens.shape[1] // 2
    at_end = (me < 2) | (me >= 6)
    own_over = across(tokens)
    next_one = along_line(tokens, PAIRS)
    middle = along_line(tokens, MIDDLE)
    acc, square = accumulate([tokens], [me], gain, in_weight)
    next_over = across(next_one, own_over, square)
    second_out = along_line(after(middle, square), OUTWARD)
    second_mid = along_line(after(next_one, square), MIDDLE)
    square, *params = lax.optimization_barrier((square, *params))
    acc, square = accumulate([own_over, next_one], [me ^ 1, me ^ 2], gain, in_weight, acc, square)
    second = jnp.where(at_end, second_out, second_mid)
    second_over = across(second, next_over, square)
    third_out = along_line(after(second_mid, square), OUTWARD)
    rest_mid = along_line(after(own_over[:, half:], second_mid, square), MIDDLE)
    acc, square = accumulate([next_over, second], [me ^ 3, me ^ 4], gain, in_weight, acc, square)
    third_over = across(jnp.where(at_end, third_out[:, :half], middle[:, :half]), second_over, square)
    rest_out = along_line(after(second_over[:, half:], square), OUTWARD)
    third = (third_out, middle)
    more, square = accumulate(
        [second_over, third], [me ^ 5, me ^ 6], gain, in_weight, None, square, use_first=at_end
    )
    place = (me ^ 7) * 2
    rest, inv_rms, rim = accumulate(
        [third_over, (rest_out, rest_mid)],
        [place, place + 1],
        gain,
        in_weight,
        None,
        square,
        [acc, more],
        use_first=at_end,
    )
    return [acc, more, rest], inv_rms, rim, params


def project_and_reduce(upper, lower, out_weight, tokens):
    me = lax.axis_index("chan")
    half = tokens.shape[0] // 2
    send = lambda k: (me ^ (2 * k + 1), jnp.bfloat16)
    keep = lambda k: (me ^ (2 * k), jnp.float32)
    narrow = lambda a: a.astype(jnp.bfloat16)
    make = functools.partial(pieces, out_weight)
    both = (0, 1)

    third_send_0 = make(upper, [send(3)])[0]
    third_over = across(third_send_0)
    lower = lower(third_send_0)
    third_send_1 = make(lower, [send(3)])[0]
    rest_in = along_line(third_send_1, INWARD)
    rest_mid = along_line(third_send_1, MIDDLE)
    second_send_0, third_keep_0 = make(upper, [send(2), keep(3)], third_send_1)
    second_send_1, third_1 = make(lower, [send(2), (keep(3)[0], jnp.bfloat16)], second_send_0)
    third = [narrow(total(third_keep_0, third_over)), third_1]
    third_in = [along_line(third[h], INWARD) for h in both]
    second_send = [second_send_0, narrow(total(second_send_1, rest_in))]
    second_over = [across(second_send[h], third_over) for h in both]
    halves = (upper, lower)
    later_0 = make(upper, [keep(2), send(1)], third_1)
    later = [later_0, make(lower, [keep(2), send(1)], third_in[0])]
    second = [narrow(total(later[h][0], second_over[h], third_in[h])) for h in both]
    second_in = [along_line(second[h], INWARD) for h in both]
    second_mid = [along_line(second[h], MIDDLE) for h in both]
    next_over = [across(later[h][1], second_over[h]) for h in both]
    later_0 = make(upper, [keep(1), send(0)], later[1][0])
    later = [later_0, make(lower, [keep(1), send(0)], second_over[0])]
    own_send = [later[0][1], narrow(total(later[1][1], rest_mid))]
    next_one = [narrow(total(later[h][0], next_over[h], second_mid[h])) for h in both]
    next_in = [along_line(next_one[h], PAIRS) for h in both]
    middle_in = [along_line(narrow(total(third[h], second_in[h])), MIDDLE) for h in both]
    own_over = [across(own_send[h], next_over[h]) for h in both]
    own_keep = [make(halves[h], [keep(0)], second_over[1])[0] for h in both]
    base = [total(own_keep[h], tokens[h * half : (h + 1) * half]) for h in both]
    return finish(*[[base[h], own_over[h], next_in[h], middle_in[h]] for h in both])


def convolve_kernel(part_count, *refs):
    part_refs, refs = refs[:part_count], refs[part_count:]
    rms_ref, rim_ref, taps_ref, decay_ref, q_ref, prod_ref, end_ref, win_ref, state_ref = refs
    step = pl.program_id(0)
    rows = q_ref.shape[0]
    tap_count, groups = taps_ref.shape[1:3]
    poles = decay_ref.shape[0]
    keep = rim_ref.shape[1]
    unroll = 8

    @pl.when(step == 0)
    def _():
        for g in range(groups):
            for i in range(3):
                win_ref[i, pl.ds(g, keep, stride=groups), :] = rim_ref[i, :, g * LANES : (g + 1) * LANES]
        state_ref[...] = jnp.zeros_like(state_ref)

    inv_rms = rms_ref[:, :1]
    for i in range(3):
        for g in range(groups):
            cols = tree_sum([ref[i, :, g * LANES : (g + 1) * LANES] for ref in part_refs]) * inv_rms
            cols = cols.astype(jnp.bfloat16).astype(jnp.float32)
            win_ref[i, pl.ds(keep * groups + g, rows, stride=groups), :] = cols
    decay = [jnp.exp(decay_ref[n]) for n in range(poles)]

    def row_of(i, t):
        return win_ref[i, pl.ds(pl.multiple_of(t * groups, groups), groups), :]

    def advance(blk, state):
        state = list(state)
        first = blk * unroll
        conv = []
        for i in range(3):
            taps = [taps_ref[i, j] for j in range(tap_count)]
            held = [row_of(i, first + keep - (tap_count - 1) + r) for r in range(unroll + tap_count - 1)]
            conv.append(
                [
                    functools.reduce(
                        lambda a, b: a + b, [taps[j] * held[r + tap_count - 1 - j] for j in range(tap_count)]
                    )
                    for r in range(unroll)
                ]
            )
        for r in range(unroll):
            q_ref[first + r] = conv[0][r]
            product = conv[1][r] * conv[2][r]
            prod_ref[first + r] = product
            for n in range(poles):
                state[n] = decay[n] * state[n] + product
        return tuple(state)

    state = lax.fori_loop(0, rows // unroll, advance, tuple(state_ref[n] for n in range(poles)))
    for n in range(poles):
        state_ref[n] = state[n]
    win_ref[:, : keep * groups] = win_ref[:, rows * groups :]

    @pl.when(step == pl.num_programs(0) - 1)
    def _():
        for n in range(poles):
            end_ref[n] = state[n]


def convolve(parts, inv_rms, rim, taps, log_decay):
    rows, chans = parts[0].shape[1:]
    groups = chans // LANES
    tap_count, poles = taps.shape[1], log_decay.shape[0]
    keep = rim.shape[1]
    blk = min(128, rows)
    whole = lambda *shape: pl.BlockSpec(shape, lambda t: (0,) * len(shape))
    row_spec = pl.BlockSpec((blk, groups, LANES), lambda t: (t, 0, 0))
    return pl.pallas_call(
        functools.partial(convolve_kernel, len(parts)),
        grid=(rows // blk,),
        in_specs=[pl.BlockSpec((3, blk, chans), lambda t: (0, t, 0))] * len(parts)
        + [
            pl.BlockSpec((blk, LANES), lambda t: (t, 0)),
            whole(3, keep, chans),
            whole(3, tap_count, groups, LANES),
            whole(poles, groups, LANES),
        ],
        out_specs=[row_spec, row_spec, whole(poles, groups, LANES)],
        out_shape=[
            jax.ShapeDtypeStruct((rows, groups, LANES), jnp.float32),
            jax.ShapeDtypeStruct((rows, groups, LANES), jnp.float32),
            jax.ShapeDtypeStruct((poles, groups, LANES), jnp.float32),
        ],
        scratch_shapes=[
            pltpu.VMEM((3, (keep + blk) * groups, LANES), jnp.float32),
            pltpu.VMEM((poles, groups, LANES), jnp.float32),
        ],
        compiler_params=pltpu.CompilerParams(vmem_limit_bytes=VMEM_LIMIT),
        cost_estimate=pl.CostEstimate(
            flops=110 * rows * groups * LANES, bytes_accessed=20 * rows * groups * LANES, transcendentals=0
        ),
        name="convolve",
    )(*parts, inv_rms, rim, taps, log_decay)


def respond_kernel(q_ref, prod_ref, enter_ref, decay_ref, res_ref, skip_ref, *refs):
    out_ref, end_ref, state_ref, row_ref = refs[-4:]
    step = pl.program_id(0)
    rows, groups = q_ref.shape[:2]
    poles = decay_ref.shape[0]
    unroll = 8

    @pl.when(step == 0)
    def _():
        state_ref[...] = enter_ref[...]

    decay = [jnp.exp(decay_ref[n]) for n in range(poles)]
    res = [res_ref[n] for n in range(poles)]
    skip = skip_ref[0]

    def recur(blk, state):
        state = list(state)
        for r in range(unroll):
            t = blk * unroll + r
            product = prod_ref[t]
            sums = [skip * product]
            for n in range(poles):
                state[n] = decay[n] * state[n] + product
                term = res[n] * state[n]
                if n < 3:
                    sums.append(term)
                else:
                    sums[n % 4] = sums[n % 4] + term
            row_ref[pl.ds(pl.multiple_of(t * groups, groups), groups), :] = q_ref[t] * tree_sum(sums)
        return tuple(state)

    state = lax.fori_loop(0, rows // unroll, recur, tuple(state_ref[n] for n in range(poles)))
    for n in range(poles):
        state_ref[n] = state[n]
        end_ref[n] = state[n]
    for g in range(groups):
        out_ref[:, g * LANES : (g + 1) * LANES] = row_ref[pl.ds(g, rows, stride=groups), :].astype(jnp.bfloat16)


def respond(query, product, enter, log_decay, residue, skip, start, rows, *earlier):
    groups = query.shape[1]
    poles = log_decay.shape[0]
    blk = min(128, rows)
    whole = lambda *shape: pl.BlockSpec(shape, lambda t: (0,) * len(shape))
    row_spec = pl.BlockSpec((blk, groups, LANES), lambda t: (t + start // blk, 0, 0))
    return pl.pallas_call(
        respond_kernel,
        grid=(rows // blk,),
        in_specs=[row_spec, row_spec]
        + [whole(poles, groups, LANES)] * 3
        + [whole(1, groups, LANES)]
        + [pl.BlockSpec(memory_space=pl.ANY)] * len(earlier),
        out_specs=[pl.BlockSpec((blk, groups * LANES), lambda t: (t, 0)), whole(poles, groups, LANES)],
        out_shape=[
            jax.ShapeDtypeStruct((rows, groups * LANES), jnp.bfloat16),
            jax.ShapeDtypeStruct((poles, groups, LANES), jnp.float32),
        ],
        scratch_shapes=[
            pltpu.VMEM((poles, groups, LANES), jnp.float32),
            pltpu.VMEM((blk * groups, LANES), jnp.float32),
        ],
        compiler_params=pltpu.CompilerParams(vmem_limit_bytes=VMEM_LIMIT),
        cost_estimate=pl.CostEstimate(
            flops=70 * rows * groups * LANES, bytes_accessed=80 * rows * groups * LANES, transcendentals=0
        ),
        name="respond",
    )(query, product, enter, log_decay, residue, skip, *earlier)


def per_device(tokens, norm_gain, in_weight, short_weight, log_decay, residue, skip, out_weight):
    rows, chans = tokens.shape
    groups = chans // LANES
    by_lane = lambda a: a.reshape(a.shape[:-1] + (groups, LANES))
    taps, log_decay, residue = by_lane(short_weight), by_lane(log_decay), by_lane(residue)
    skip = by_lane(skip[None, :])

    paired_line = lax.axis_size("chan") == 8
    if paired_line:
        params = (taps, log_decay, residue, skip)
        parts, inv_rms, rim, params = gather_and_project(tokens, norm_gain, in_weight, params)
        taps, log_decay, residue, skip = params
    else:
        gathered = lax.all_gather(tokens, "chan", axis=1, tiled=True)
        depth = min(1024, gathered.shape[1])
        chunks = [gathered[:, k : k + depth] for k in range(0, gathered.shape[1], depth)]
        acc = square = None
        for k, chunk in enumerate(chunks[:-1]):
            acc, square = accumulate([chunk], [k], norm_gain, in_weight, acc, square)
        acc, inv_rms, rim = accumulate(chunks[-1:], [len(chunks) - 1], norm_gain, in_weight, acc, square, [])
        parts = [acc]
    rim = from_behind(rim, "seq", 1)
    query, product, end = convolve(parts, inv_rms, rim, taps, log_decay)
    shard_decay = jnp.exp(rows * log_decay)
    state, passing = jnp.zeros_like(end), end
    for _ in range(lax.axis_size("seq") - 1):
        passing = from_behind(passing, "seq", 1)
        state = state + passing
        passing = passing * shard_decay
    filt = (log_decay, residue, skip)
    if paired_line:
        half = rows // 2
        upper, state = respond(query, product, state, *filt, 0, half)
        lower = lambda *earlier: respond(query, product, state, *filt, half, half, *earlier)[0]
        return project_and_reduce(upper, lower, out_weight, tokens)
    gated = respond(query, product, state, *filt, 0, rows)[0]
    partial = jnp.dot(gated, out_weight, preferred_element_type=jnp.float32)
    branch = lax.psum_scatter(partial.astype(jnp.bfloat16), "chan", scatter_dimension=1, tiled=True)
    return (tokens.astype(jnp.float32) + branch.astype(jnp.float32)).astype(jnp.bfloat16)


def solution(mesh):
    return jax.shard_map(
        per_device,
        mesh=mesh,
        in_specs=(
            P(("groups", "seq"), "chan"),
            P(),
            P(None, None, "chan"),
            P(None, None, "chan"),
            P(None, "chan"),
            P(None, "chan"),
            P("chan"),
            P("chan", None),
        ),
        out_specs=P(("groups", "seq"), "chan"),
        check_vma=False,
    )
```

```python
import functools

import jax
import jax.numpy as jnp
from jax import lax
from jax.experimental import pallas as pl
from jax.experimental.pallas import tpu as pltpu
from jax.sharding import PartitionSpec as P

EPSILON = 1e-06
LANES = 128
KEEP = 8
VMEM_LIMIT = 48 * 1024 * 1024


def from_behind(block, axis, distance):
    count = lax.axis_size(axis)
    route = [(i - distance, i) for i in range(count) if i - distance >= 0]
    return lax.ppermute(block, axis, route)


def tree_sum(terms):
    while len(terms) > 1:
        pairs = [terms[i] + terms[i + 1] for i in range(0, len(terms) - 1, 2)]
        terms = pairs + terms[len(pairs) * 2 :]
    return terms[0]


def accumulate_kernel(depths, pairs, width, has_acc, has_sq, part_count, place_ref, *refs):
    def take(count):
        nonlocal refs
        taken, refs = refs[:count], refs[count:]
        return taken

    chunk_refs = take(len(depths) + sum(pairs))
    gain_refs, w_refs = take(len(depths)), take(len(depths))
    held_refs, held_sq_refs = take(int(has_acc)), take(int(has_sq))
    part_refs = take(part_count or 0)
    acc_ref, sq_ref = take(2)
    scaled_ref = refs[-1]
    feat, col = pl.program_id(0), pl.program_id(1)
    last = part_count is not None

    @pl.when((feat == 0) & (col == 0))
    def _():
        square = held_sq_refs[0][...] if has_sq else None
        start = at = 0
        for j, depth in enumerate(depths):
            x = chunk_refs[at][...]
            at += 1
            if pairs[j]:
                x = jnp.where(place_ref[place_ref.shape[0] - 1] == 1, x, chunk_refs[at][...])
                at += 1
            x = x.astype(jnp.float32)
            parts = [x[:, g : g + LANES] * x[:, g : g + LANES] for g in range(0, depth, LANES)]
            part = tree_sum(parts)
            square = part if square is None else square + part
            scaled_ref[:, start : start + depth] = (x * gain_refs[j][0]).astype(jnp.bfloat16)
            start += depth
        if last:
            total = jnp.sum(square, axis=1, keepdims=True)
            square = jnp.broadcast_to(lax.rsqrt(total / width + EPSILON), square.shape)
        sq_ref[...] = square

    start, part = 0, None
    for j, depth in enumerate(depths):
        one = jnp.dot(scaled_ref[:, start : start + depth], w_refs[j][0], preferred_element_type=jnp.float32)
        part = one if part is None else part + one
        start += depth
    acc_ref[0] = held_refs[0][0] + part if has_acc else part
    if last:
        rim_ref = refs[0]
        keep = rim_ref.shape[1]
        rows = acc_ref.shape[1]
        rim = acc_ref[0, rows - keep :, :]
        for ref in part_refs:
            rim = rim + ref[0]
        rim_ref[0] = (rim * sq_ref[rows - keep :, :1]).astype(jnp.bfloat16).astype(jnp.float32)


def accumulate(table, chunks, places, gain, in_weight, acc=None, square=None, parts=None):
    pairs = [isinstance(c, tuple) for c in chunks]
    arrays = [a for c in chunks for a in (c if isinstance(c, tuple) else (c,))]
    depths = [(c[0] if isinstance(c, tuple) else c).shape[1] for c in chunks]
    rows = arrays[0].shape[0]
    width, chans = in_weight.shape[1:]
    tile = min(512, chans)
    acc_spec = pl.BlockSpec((1, rows, tile), lambda i, c, p: (i, 0, c))
    sq_spec = pl.BlockSpec((rows, LANES), lambda i, c, p: (0, 0))
    in_specs = [pl.BlockSpec(a.shape, lambda i, c, p: (0, 0)) for a in arrays]
    for d, (k, per_shard, part) in zip(depths, places):
        place = lambda p, k=k, n=per_shard, part=part: p[k] * n + part
        in_specs.append(pl.BlockSpec((1, 1, d), lambda i, c, p, place=place: (place(p), 0, 0)))
    for d, (k, per_shard, part) in zip(depths, places):
        place = lambda p, k=k, n=per_shard, part=part: p[k] * n + part
        in_specs.append(pl.BlockSpec((1, d, tile), lambda i, c, p, place=place: (i, place(p), c)))
    out_specs = [acc_spec, sq_spec]
    out_shape = [
        jax.ShapeDtypeStruct((3, rows, chans), jnp.float32),
        jax.ShapeDtypeStruct((rows, LANES), jnp.float32),
    ]
    extra, aliases = [], {}
    before = 1 + len(arrays) + 2 * len(depths)
    for n, (held, spec) in enumerate(((acc, acc_spec), (square, sq_spec))):
        if held is not None:
            aliases[before + len(extra)] = n
            extra.append(held)
            in_specs.append(spec)
    if parts is not None:
        extra += parts
        in_specs += [pl.BlockSpec((1, KEEP, tile), lambda i, c, p: (i, rows // KEEP - 1, c))] * len(parts)
        out_specs.append(pl.BlockSpec((1, KEEP, tile), lambda i, c, p: (i, 0, c)))
        out_shape.append(jax.ShapeDtypeStruct((3, KEEP, chans), jnp.float32))
    part_count = None if parts is None else len(parts)
    return pl.pallas_call(
        functools.partial(
            accumulate_kernel, depths, pairs, width, acc is not None, square is not None, part_count
        ),
        grid_spec=pltpu.PrefetchScalarGridSpec(
            num_scalar_prefetch=1,
            grid=(3, chans // tile),
            in_specs=in_specs,
            out_specs=out_specs,
            scratch_shapes=[pltpu.VMEM((rows, sum(depths)), jnp.bfloat16)],
        ),
        out_shape=out_shape,
        input_output_aliases=aliases,
        compiler_params=pltpu.CompilerParams(vmem_limit_bytes=VMEM_LIMIT),
        cost_estimate=pl.CostEstimate(
            flops=rows * sum(depths) * chans,
            bytes_accessed=6 * sum(depths) * chans,
            transcendentals=0,
        ),
        name="accumulate",
    )(
        table,
        *arrays,
        *[gain.reshape(-1, 1, d) for d in depths],
        *[in_weight] * len(depths),
        *extra,
    )


def pieces_kernel(count, place_ref, gated_ref, w_ref, *refs):
    outs = refs[-count:]
    total = jnp.dot(gated_ref[...], w_ref[...], preferred_element_type=jnp.float32)
    for j in range(count):

        @pl.when(pl.program_id(0) == j)
        def _():
            outs[j][...] = total.astype(outs[j].dtype)


def pieces(table, out_weight, gated, wanted, *earlier):
    rows, chans = gated.shape
    count = len(wanted)

    def place(t, p):
        shard = p[wanted[0][0]]
        for j in range(1, count):
            shard = jnp.where(t == j, p[wanted[j][0]], shard)
        return shard

    out = pl.pallas_call(
        functools.partial(pieces_kernel, count),
        grid_spec=pltpu.PrefetchScalarGridSpec(
            num_scalar_prefetch=1,
            grid=(count,),
            in_specs=[
                pl.BlockSpec((rows, chans), lambda t, p: (0, 0)),
                pl.BlockSpec((chans, chans), lambda t, p: (0, place(t, p))),
            ]
            + [pl.BlockSpec(memory_space=pl.ANY)] * len(earlier),
            out_specs=[pl.BlockSpec((rows, chans), lambda t, p: (0, 0))] * count,
        ),
        out_shape=[jax.ShapeDtypeStruct((rows, chans), dtype) for k, dtype in wanted],
        compiler_params=pltpu.CompilerParams(vmem_limit_bytes=VMEM_LIMIT),
        cost_estimate=pl.CostEstimate(flops=count * 1000000, bytes_accessed=count * 100000, transcendentals=0),
        name="pieces",
    )(table, gated, out_weight, *earlier)
    return list(out)


def finish_kernel(*refs):
    out_ref = refs[-1]
    count = (len(refs) - 1) // 2
    step, per_half = pl.program_id(0), pl.num_programs(0) // 2

    for h in range(2):

        @pl.when((step >= h * per_half) & (step < (h + 1) * per_half))
        def _():
            total = refs[h * count][...].astype(jnp.float32)
            for ref in refs[h * count + 1 : (h + 1) * count]:
                total = total + ref[...].astype(jnp.float32)
            out_ref[...] = total.astype(jnp.bfloat16)


def finish(upper, lower):
    rows, chans = upper[0].shape
    blk = min(128, rows)
    per_half = rows // blk
    spec = lambda h: pl.BlockSpec((blk, chans), lambda t: (jnp.clip(t - h * per_half, 0, per_half - 1), 0))
    return pl.pallas_call(
        finish_kernel,
        grid=(2 * per_half,),
        in_specs=[spec(0)] * len(upper) + [spec(1)] * len(lower),
        out_specs=pl.BlockSpec((blk, chans), lambda t: (t, 0)),
        out_shape=jax.ShapeDtypeStruct((2 * rows, chans), jnp.bfloat16),
        compiler_params=pltpu.CompilerParams(vmem_limit_bytes=VMEM_LIMIT),
        name="finish",
    )(*upper, *lower)


def along_line(block, pairs):
    return lax.ppermute(block, "chan", [(2 * a + y, 2 * b + y) for a, b in pairs for y in (0, 1)])


def after(block, *earlier):
    return lax.optimization_barrier((block,) + earlier)[0]


def across(block, *earlier):
    count = lax.axis_size("chan")
    if earlier:
        block = after(block, *earlier)
    return lax.ppermute(block, "chan", [(c, c ^ 1) for c in range(count)])


def total(*terms):
    return functools.reduce(lambda a, b: a + b, [t.astype(jnp.float32) for t in terms])


PAIRS = [(0, 1), (1, 0), (2, 3), (3, 2)]
MIDDLE = [(1, 2), (2, 1)]
OUTWARD = [(1, 0), (2, 3)]
INWARD = [(0, 1), (3, 2)]


def gather_and_project(table, tokens, gain, in_weight, params):
    me = lax.axis_index("chan")
    half = tokens.shape[1] // 2
    at_end = (me < 2) | (me >= 6)
    whole = lambda k: (k, 1, 0)
    own_over = across(tokens)
    next_one = along_line(tokens, PAIRS)
    middle = along_line(tokens, MIDDLE)
    acc, square = accumulate(table, [tokens], [whole(0)], gain, in_weight)
    next_over = across(next_one, own_over, square)
    second_out = along_line(after(middle, square), OUTWARD)
    second_mid = along_line(after(next_one, square), MIDDLE)
    square, *params = lax.optimization_barrier((square, *params))
    acc, square = accumulate(table, [own_over, next_one], [whole(1), whole(2)], gain, in_weight, acc, square)
    second = jnp.where(at_end, second_out, second_mid)
    second_over = across(second, next_over, square)
    third_out = along_line(after(second_mid, square), OUTWARD)
    rest_mid = along_line(after(own_over[:, half:], second_mid, square), MIDDLE)
    acc, square = accumulate(table, [next_over, second], [whole(3), whole(4)], gain, in_weight, acc, square)
    third_over = across(jnp.where(at_end, third_out[:, :half], middle[:, :half]), second_over, square)
    rest_out = along_line(after(second_over[:, half:], square), OUTWARD)
    third = (third_out, middle)
    more, square = accumulate(
        table, [second_over, third], [whole(5), whole(6)], gain, in_weight, None, square
    )
    last = [third_over, (rest_out, rest_mid)]
    places = [(7, 2, 0), (7, 2, 1)]
    rest, inv_rms, rim = accumulate(
        table, last, places, gain, in_weight, None, square, [acc, more]
    )
    return [acc, more, rest], inv_rms, rim, params


def project_and_reduce(table, upper, lower, out_weight, tokens):
    half = tokens.shape[0] // 2
    send = lambda k: (2 * k + 1, jnp.bfloat16)
    keep = lambda k: (2 * k, jnp.float32)
    narrow = lambda a: a.astype(jnp.bfloat16)
    make = functools.partial(pieces, table, out_weight)
    both = (0, 1)

    third_send_0 = make(upper, [send(3)])[0]
    third_over = across(third_send_0)
    lower = lower(third_send_0)
    third_send_1 = make(lower, [send(3)])[0]
    rest_in = along_line(third_send_1, INWARD)
    rest_mid = along_line(third_send_1, MIDDLE)
    second_send_0, third_keep_0 = make(upper, [send(2), keep(3)], third_send_1)
    second_send_1, third_1 = make(lower, [send(2), (keep(3)[0], jnp.bfloat16)], third_over)
    third = [narrow(total(third_keep_0, third_over)), third_1]
    third_in = [along_line(third[h], INWARD) for h in both]
    second_send = [second_send_0, narrow(total(second_send_1, rest_in))]
    second_over = [across(second_send[h], third_over) for h in both]
    halves = (upper, lower)
    later_0 = make(upper, [keep(2), send(1)], third_1)
    later = [later_0, make(lower, [keep(2), send(1)], third_in[0])]
    second = [narrow(total(later[h][0], second_over[h], third_in[h])) for h in both]
    second_in = [along_line(second[h], INWARD) for h in both]
    second_mid = [along_line(second[h], MIDDLE) for h in both]
    next_over = [across(later[h][1], second_over[h]) for h in both]
    later_0 = make(upper, [keep(1), send(0)], second_in[0])
    later = [later_0, make(lower, [keep(1), send(0)], second[1])]
    own_send = [later[0][1], narrow(total(later[1][1], rest_mid))]
    next_one = [narrow(total(later[h][0], next_over[h], second_mid[h])) for h in both]
    next_in = [along_line(next_one[h], PAIRS) for h in both]
    middle_in = [along_line(narrow(total(third[h], second_in[h])), MIDDLE) for h in both]
    own_over = [across(own_send[h], next_over[h]) for h in both]
    own_keep = [make(halves[h], [keep(0)], second_over[1])[0] for h in both]
    base = [total(own_keep[h], tokens[h * half : (h + 1) * half]) for h in both]
    return finish(*[[base[h], own_over[h], next_in[h], middle_in[h]] for h in both])


def convolve_kernel(part_count, after_rows, *refs):
    part_refs, refs = refs[:part_count], refs[part_count:]
    rms_ref, refs = refs[0], refs[1:]
    taps_ref, decay_ref, refs = refs[0], refs[1], refs[2:]
    own_rim = after_rows is None
    if own_rim:
        rim_refs, rim_rms_ref = refs[:part_count], refs[part_count]
    else:
        rim_ref, later_ref = refs[:2]
    q_ref, prod_ref, end_ref, win_ref, state_ref = refs[-5:]
    step = pl.program_id(0)
    rows = q_ref.shape[0]
    tap_count, groups = taps_ref.shape[1:3]
    poles = decay_ref.shape[0]
    keep = win_ref.shape[1] // groups - rows
    unroll = 8

    def rounded(sources, scale, i, g):
        cols = tree_sum([ref[i, :, g * LANES : (g + 1) * LANES] for ref in sources]) * scale
        return cols.astype(jnp.bfloat16).astype(jnp.float32)

    @pl.when(step == 0)
    def _():
        for g in range(groups):
            for i in range(3):
                if own_rim:
                    rim = rounded(rim_refs, rim_rms_ref[:, :1], i, g)
                else:
                    rim = rim_ref[i, :, g * LANES : (g + 1) * LANES]
                win_ref[i, pl.ds(g, keep, stride=groups), :] = rim
        state_ref[...] = jnp.zeros_like(state_ref)

    inv_rms = rms_ref[:, :1]
    for i in range(3):
        for g in range(groups):
            win_ref[i, pl.ds(keep * groups + g, rows, stride=groups), :] = rounded(part_refs, inv_rms, i, g)
    decay = [jnp.exp(decay_ref[n]) for n in range(poles)]

    def row_of(i, t):
        return win_ref[i, pl.ds(pl.multiple_of(t * groups, groups), groups), :]

    def advance(blk, state):
        state = list(state)
        first = blk * unroll
        conv = []
        for i in range(3):
            taps = [taps_ref[i, j] for j in range(tap_count)]
            held = [row_of(i, first + keep - (tap_count - 1) + r) for r in range(unroll + tap_count - 1)]
            conv.append(
                [
                    functools.reduce(
                        lambda a, b: a + b, [taps[j] * held[r + tap_count - 1 - j] for j in range(tap_count)]
                    )
                    for r in range(unroll)
                ]
            )
        for r in range(unroll):
            q_ref[first + r] = conv[0][r]
            product = conv[1][r] * conv[2][r]
            prod_ref[first + r] = product
            for n in range(poles):
                state[n] = decay[n] * state[n] + product
        return tuple(state)

    state = lax.fori_loop(0, rows // unroll, advance, tuple(state_ref[n] for n in range(poles)))
    for n in range(poles):
        state_ref[n] = state[n]
    win_ref[:, : keep * groups] = win_ref[:, rows * groups :]

    @pl.when(step == pl.num_programs(0) - 1)
    def _():
        for n in range(poles):
            if own_rim:
                end_ref[n] = state[n]
            else:
                end_ref[n] = later_ref[n] + jnp.exp(float(after_rows) * decay_ref[n]) * state[n]


def convolve(parts, inv_rms, taps, log_decay, rim=None, done=None):
    rows, chans = parts[0].shape[1:]
    groups = chans // LANES
    tap_count, poles = taps.shape[1], log_decay.shape[0]
    count = len(parts)
    blk = min(128, rows // 2)
    whole = lambda *shape: pl.BlockSpec(shape, lambda t: (0,) * len(shape))
    start = 1 if rim is None else 0
    row_spec = pl.BlockSpec((blk, groups, LANES), lambda t: (t + start, 0, 0))
    state_spec = whole(poles, groups, LANES)
    in_specs = [pl.BlockSpec((3, blk, chans), lambda t: (0, t + start, 0))] * count
    in_specs += [pl.BlockSpec((blk, LANES), lambda t: (t + start, 0)), whole(3, tap_count, groups, LANES), state_spec]
    operands, aliases = [*parts, inv_rms, taps, log_decay], {}
    if rim is None:
        at = blk // KEEP - 1
        in_specs += [pl.BlockSpec((3, KEEP, chans), lambda t: (0, at, 0))] * count
        in_specs += [pl.BlockSpec((KEEP, LANES), lambda t: (at, 0))]
        operands += [*parts, inv_rms]
    else:
        query, product, end = done
        in_specs += [whole(3, KEEP, chans), state_spec] + [pl.BlockSpec(memory_space=pl.ANY)] * 2
        operands += [rim, end, query, product]
        aliases = {len(operands) - 2: 0, len(operands) - 1: 1}
    return pl.pallas_call(
        functools.partial(convolve_kernel, count, None if rim is None else rows - blk),
        grid=(rows // blk - 1 if rim is None else 1,),
        in_specs=in_specs,
        out_specs=[row_spec, row_spec, state_spec],
        out_shape=[
            jax.ShapeDtypeStruct((rows, groups, LANES), jnp.float32),
            jax.ShapeDtypeStruct((rows, groups, LANES), jnp.float32),
            jax.ShapeDtypeStruct((poles, groups, LANES), jnp.float32),
        ],
        scratch_shapes=[
            pltpu.VMEM((3, (KEEP + blk) * groups, LANES), jnp.float32),
            pltpu.VMEM((poles, groups, LANES), jnp.float32),
        ],
        input_output_aliases=aliases,
        compiler_params=pltpu.CompilerParams(vmem_limit_bytes=VMEM_LIMIT),
        cost_estimate=pl.CostEstimate(
            flops=80 * rows * groups * LANES, bytes_accessed=20 * rows * groups * LANES, transcendentals=0
        ),
        name="convolve",
    )(*operands)


def respond_kernel(q_ref, prod_ref, enter_ref, decay_ref, res_ref, skip_ref, *refs):
    out_ref, end_ref, state_ref, row_ref = refs[-4:]
    step = pl.program_id(0)
    rows, groups = q_ref.shape[:2]
    poles = decay_ref.shape[0]
    unroll = 8

    @pl.when(step == 0)
    def _():
        state_ref[...] = enter_ref[...]

    decay = [jnp.exp(decay_ref[n]) for n in range(poles)]
    res = [res_ref[n] for n in range(poles)]
    skip = skip_ref[0]

    def recur(blk, state):
        state = list(state)
        for r in range(unroll):
            t = blk * unroll + r
            product = prod_ref[t]
            sums = [skip * product]
            for n in range(poles):
                state[n] = decay[n] * state[n] + product
                term = res[n] * state[n]
                if n < 3:
                    sums.append(term)
                else:
                    sums[n % 4] = sums[n % 4] + term
            row_ref[pl.ds(pl.multiple_of(t * groups, groups), groups), :] = q_ref[t] * tree_sum(sums)
        return tuple(state)

    state = lax.fori_loop(0, rows // unroll, recur, tuple(state_ref[n] for n in range(poles)))
    for n in range(poles):
        state_ref[n] = state[n]
        end_ref[n] = state[n]
    for g in range(groups):
        out_ref[:, g * LANES : (g + 1) * LANES] = row_ref[pl.ds(g, rows, stride=groups), :].astype(jnp.bfloat16)


def respond(query, product, enter, log_decay, residue, skip, start, rows, *earlier):
    groups = query.shape[1]
    poles = log_decay.shape[0]
    blk = min(128, rows)
    whole = lambda *shape: pl.BlockSpec(shape, lambda t: (0,) * len(shape))
    row_spec = pl.BlockSpec((blk, groups, LANES), lambda t: (t + start // blk, 0, 0))
    return pl.pallas_call(
        respond_kernel,
        grid=(rows // blk,),
        in_specs=[row_spec, row_spec]
        + [whole(poles, groups, LANES)] * 3
        + [whole(1, groups, LANES)]
        + [pl.BlockSpec(memory_space=pl.ANY)] * len(earlier),
        out_specs=[pl.BlockSpec((blk, groups * LANES), lambda t: (t, 0)), whole(poles, groups, LANES)],
        out_shape=[
            jax.ShapeDtypeStruct((rows, groups * LANES), jnp.bfloat16),
            jax.ShapeDtypeStruct((poles, groups, LANES), jnp.float32),
        ],
        scratch_shapes=[
            pltpu.VMEM((poles, groups, LANES), jnp.float32),
            pltpu.VMEM((blk * groups, LANES), jnp.float32),
        ],
        compiler_params=pltpu.CompilerParams(vmem_limit_bytes=VMEM_LIMIT),
        cost_estimate=pl.CostEstimate(
            flops=70 * rows * groups * LANES, bytes_accessed=80 * rows * groups * LANES, transcendentals=0
        ),
        name="respond",
    )(query, product, enter, log_decay, residue, skip, *earlier)


def per_device(tokens, norm_gain, in_weight, short_weight, log_decay, residue, skip, out_weight):
    rows, chans = tokens.shape
    groups = chans // LANES
    by_lane = lambda a: a.reshape(a.shape[:-1] + (groups, LANES))
    taps, log_decay, residue = by_lane(short_weight), by_lane(log_decay), by_lane(residue)
    skip = by_lane(skip[None, :])

    paired_line = lax.axis_size("chan") == 8
    if paired_line:
        me = lax.axis_index("chan")
        at_end = ((me < 2) | (me >= 6)).astype(jnp.int32)
        table = jnp.concatenate([me ^ jnp.arange(8, dtype=jnp.int32), at_end[None]])
        params = (taps, log_decay, residue, skip)
        parts, inv_rms, rim, params = gather_and_project(table, tokens, norm_gain, in_weight, params)
        taps, log_decay, residue, skip = params
    else:
        gathered = lax.all_gather(tokens, "chan", axis=1, tiled=True)
        depth = min(1024, gathered.shape[1])
        chunks = [gathered[:, k : k + depth] for k in range(0, gathered.shape[1], depth)]
        table = jnp.arange(len(chunks), dtype=jnp.int32)
        acc = square = None
        for k, chunk in enumerate(chunks[:-1]):
            acc, square = accumulate(table, [chunk], [(k, 1, 0)], norm_gain, in_weight, acc, square)
        places = [(len(chunks) - 1, 1, 0)]
        acc, inv_rms, rim = accumulate(table, chunks[-1:], places, norm_gain, in_weight, acc, square, [])
        parts = [acc]
    rim = from_behind(rim, "seq", 1)
    done = convolve(parts, inv_rms, taps, log_decay)
    query, product, end = convolve(parts, inv_rms, taps, log_decay, rim, done)
    shard_decay = jnp.exp(rows * log_decay)
    state, passing = jnp.zeros_like(end), end
    for _ in range(lax.axis_size("seq") - 1):
        passing = from_behind(passing, "seq", 1)
        state = state + passing
        passing = passing * shard_decay
    filt = (log_decay, residue, skip)
    if paired_line:
        half = rows // 2
        upper, state = respond(query, product, state, *filt, 0, half)
        lower = lambda *earlier: respond(query, product, state, *filt, half, half, *earlier)[0]
        return project_and_reduce(table, upper, lower, out_weight, tokens)
    gated = respond(query, product, state, *filt, 0, rows)[0]
    partial = jnp.dot(gated, out_weight, preferred_element_type=jnp.float32)
    branch = lax.psum_scatter(partial.astype(jnp.bfloat16), "chan", scatter_dimension=1, tiled=True)
    return (tokens.astype(jnp.float32) + branch.astype(jnp.float32)).astype(jnp.bfloat16)


def solution(mesh):
    return jax.shard_map(
        per_device,
        mesh=mesh,
        in_specs=(
            P(("groups", "seq"), "chan"),
            P(),
            P(None, None, "chan"),
            P(None, None, "chan"),
            P(None, "chan"),
            P(None, "chan"),
            P("chan"),
            P("chan", None),
        ),
        out_specs=P(("groups", "seq"), "chan"),
        check_vma=False,
    )
```

```python
import functools

import jax
import jax.numpy as jnp
from jax import lax
from jax.experimental import pallas as pl
from jax.experimental.pallas import tpu as pltpu
from jax.sharding import PartitionSpec as P

EPSILON = 1e-06
LANES = 128
KEEP = 8
VMEM_LIMIT = 48 * 1024 * 1024


def from_behind(block, axis, distance):
    count = lax.axis_size(axis)
    route = [(i - distance, i) for i in range(count) if i - distance >= 0]
    return lax.ppermute(block, axis, route)


def tree_sum(terms):
    while len(terms) > 1:
        pairs = [terms[i] + terms[i + 1] for i in range(0, len(terms) - 1, 2)]
        terms = pairs + terms[len(pairs) * 2 :]
    return terms[0]


def accumulate_kernel(depths, pairs, width, has_acc, has_sq, part_count, place_ref, *refs):
    def take(count):
        nonlocal refs
        taken, refs = refs[:count], refs[count:]
        return taken

    chunk_refs = take(len(depths) + sum(pairs))
    gain_refs, w_refs = take(len(depths)), take(len(depths))
    held_refs, held_sq_refs = take(int(has_acc)), take(int(has_sq))
    part_refs = take(part_count or 0)
    acc_ref, sq_ref = take(2)
    scaled_ref = refs[-1]
    feat, col = pl.program_id(0), pl.program_id(1)
    last = part_count is not None

    @pl.when((feat == 0) & (col == 0))
    def _():
        square = held_sq_refs[0][...] if has_sq else None
        start = at = 0
        for j, depth in enumerate(depths):
            x = chunk_refs[at][...]
            at += 1
            if pairs[j]:
                x = jnp.where(place_ref[place_ref.shape[0] - 1] == 1, x, chunk_refs[at][...])
                at += 1
            x = x.astype(jnp.float32)
            parts = [x[:, g : g + LANES] * x[:, g : g + LANES] for g in range(0, depth, LANES)]
            part = tree_sum(parts)
            square = part if square is None else square + part
            scaled_ref[:, start : start + depth] = (x * gain_refs[j][0]).astype(jnp.bfloat16)
            start += depth
        if last:
            total = jnp.sum(square, axis=1, keepdims=True)
            square = jnp.broadcast_to(lax.rsqrt(total / width + EPSILON), square.shape)
        sq_ref[...] = square

    start, part = 0, None
    for j, depth in enumerate(depths):
        one = jnp.dot(scaled_ref[:, start : start + depth], w_refs[j][0], preferred_element_type=jnp.float32)
        part = one if part is None else part + one
        start += depth
    acc_ref[0] = held_refs[0][0] + part if has_acc else part
    if last:
        rim_ref = refs[0]
        keep = rim_ref.shape[1]
        rows = acc_ref.shape[1]
        rim = acc_ref[0, rows - keep :, :]
        for ref in part_refs:
            rim = rim + ref[0]
        rim_ref[0] = (rim * sq_ref[rows - keep :, :1]).astype(jnp.bfloat16).astype(jnp.float32)


def accumulate(table, chunks, places, gain, in_weight, acc=None, square=None, parts=None):
    pairs = [isinstance(c, tuple) for c in chunks]
    arrays = [a for c in chunks for a in (c if isinstance(c, tuple) else (c,))]
    depths = [(c[0] if isinstance(c, tuple) else c).shape[1] for c in chunks]
    rows = arrays[0].shape[0]
    width, chans = in_weight.shape[1:]
    tile = min(512, chans)
    acc_spec = pl.BlockSpec((1, rows, tile), lambda i, c, p: (i, 0, c))
    sq_spec = pl.BlockSpec((rows, LANES), lambda i, c, p: (0, 0))
    in_specs = [pl.BlockSpec(a.shape, lambda i, c, p: (0, 0)) for a in arrays]
    for d, (k, per_shard, part) in zip(depths, places):
        place = lambda p, k=k, n=per_shard, part=part: p[k] * n + part
        in_specs.append(pl.BlockSpec((1, 1, d), lambda i, c, p, place=place: (place(p), 0, 0)))
    for d, (k, per_shard, part) in zip(depths, places):
        place = lambda p, k=k, n=per_shard, part=part: p[k] * n + part
        in_specs.append(pl.BlockSpec((1, d, tile), lambda i, c, p, place=place: (i, place(p), c)))
    out_specs = [acc_spec, sq_spec]
    out_shape = [
        jax.ShapeDtypeStruct((3, rows, chans), jnp.float32),
        jax.ShapeDtypeStruct((rows, LANES), jnp.float32),
    ]
    extra, aliases = [], {}
    before = 1 + len(arrays) + 2 * len(depths)
    for n, (held, spec) in enumerate(((acc, acc_spec), (square, sq_spec))):
        if held is not None:
            aliases[before + len(extra)] = n
            extra.append(held)
            in_specs.append(spec)
    if parts is not None:
        extra += parts
        in_specs += [pl.BlockSpec((1, KEEP, tile), lambda i, c, p: (i, rows // KEEP - 1, c))] * len(parts)
        out_specs.append(pl.BlockSpec((1, KEEP, tile), lambda i, c, p: (i, 0, c)))
        out_shape.append(jax.ShapeDtypeStruct((3, KEEP, chans), jnp.float32))
    part_count = None if parts is None else len(parts)
    return pl.pallas_call(
        functools.partial(
            accumulate_kernel, depths, pairs, width, acc is not None, square is not None, part_count
        ),
        grid_spec=pltpu.PrefetchScalarGridSpec(
            num_scalar_prefetch=1,
            grid=(3, chans // tile),
            in_specs=in_specs,
            out_specs=out_specs,
            scratch_shapes=[pltpu.VMEM((rows, sum(depths)), jnp.bfloat16)],
        ),
        out_shape=out_shape,
        input_output_aliases=aliases,
        compiler_params=pltpu.CompilerParams(vmem_limit_bytes=VMEM_LIMIT),
        cost_estimate=pl.CostEstimate(
            flops=rows * sum(depths) * chans,
            bytes_accessed=6 * sum(depths) * chans,
            transcendentals=0,
        ),
        name="accumulate",
    )(
        table,
        *arrays,
        *[gain.reshape(-1, 1, d) for d in depths],
        *[in_weight] * len(depths),
        *extra,
    )


def pieces_kernel(count, place_ref, gated_ref, w_ref, *refs):
    outs = refs[-count:]
    total = jnp.dot(gated_ref[...], w_ref[...], preferred_element_type=jnp.float32)
    for j in range(count):

        @pl.when(pl.program_id(0) == j)
        def _():
            outs[j][...] = total.astype(outs[j].dtype)


def pieces(table, out_weight, gated, wanted, *earlier):
    rows, chans = gated.shape
    count = len(wanted)

    def place(t, p):
        shard = p[wanted[0][0]]
        for j in range(1, count):
            shard = jnp.where(t == j, p[wanted[j][0]], shard)
        return shard

    out = pl.pallas_call(
        functools.partial(pieces_kernel, count),
        grid_spec=pltpu.PrefetchScalarGridSpec(
            num_scalar_prefetch=1,
            grid=(count,),
            in_specs=[
                pl.BlockSpec((rows, chans), lambda t, p: (0, 0)),
                pl.BlockSpec((chans, chans), lambda t, p: (0, place(t, p))),
            ]
            + [pl.BlockSpec(memory_space=pl.ANY)] * len(earlier),
            out_specs=[pl.BlockSpec((rows, chans), lambda t, p: (0, 0))] * count,
        ),
        out_shape=[jax.ShapeDtypeStruct((rows, chans), dtype) for k, dtype in wanted],
        compiler_params=pltpu.CompilerParams(vmem_limit_bytes=VMEM_LIMIT),
        cost_estimate=pl.CostEstimate(flops=count * 1000000, bytes_accessed=count * 100000, transcendentals=0),
        name="pieces",
    )(table, gated, out_weight, *earlier)
    return list(out)


def finish_kernel(*refs):
    out_ref = refs[-1]
    count = (len(refs) - 1) // 2
    step, per_half = pl.program_id(0), pl.num_programs(0) // 2

    for h in range(2):

        @pl.when((step >= h * per_half) & (step < (h + 1) * per_half))
        def _():
            total = refs[h * count][...].astype(jnp.float32)
            for ref in refs[h * count + 1 : (h + 1) * count]:
                total = total + ref[...].astype(jnp.float32)
            out_ref[...] = total.astype(jnp.bfloat16)


def finish(upper, lower):
    rows, chans = upper[0].shape
    blk = min(128, rows)
    per_half = rows // blk
    spec = lambda h: pl.BlockSpec((blk, chans), lambda t: (jnp.clip(t - h * per_half, 0, per_half - 1), 0))
    return pl.pallas_call(
        finish_kernel,
        grid=(2 * per_half,),
        in_specs=[spec(0)] * len(upper) + [spec(1)] * len(lower),
        out_specs=pl.BlockSpec((blk, chans), lambda t: (t, 0)),
        out_shape=jax.ShapeDtypeStruct((2 * rows, chans), jnp.bfloat16),
        compiler_params=pltpu.CompilerParams(vmem_limit_bytes=VMEM_LIMIT),
        name="finish",
    )(*upper, *lower)


def along_line(block, pairs):
    return lax.ppermute(block, "chan", [(2 * a + y, 2 * b + y) for a, b in pairs for y in (0, 1)])


def after(block, *earlier):
    return lax.optimization_barrier((block,) + earlier)[0]


def across(block, *earlier):
    count = lax.axis_size("chan")
    if earlier:
        block = after(block, *earlier)
    return lax.ppermute(block, "chan", [(c, c ^ 1) for c in range(count)])


def total(*terms):
    return functools.reduce(lambda a, b: a + b, [t.astype(jnp.float32) for t in terms])


PAIRS = [(0, 1), (1, 0), (2, 3), (3, 2)]
MIDDLE = [(1, 2), (2, 1)]
OUTWARD = [(1, 0), (2, 3)]
INWARD = [(0, 1), (3, 2)]


def gather_and_project(table, tokens, gain, in_weight, params):
    me = lax.axis_index("chan")
    half = tokens.shape[1] // 2
    at_end = (me < 2) | (me >= 6)
    whole = lambda k: (k, 1, 0)
    own_over = across(tokens)
    next_one = along_line(tokens, PAIRS)
    middle = along_line(tokens, MIDDLE)
    acc, square = accumulate(table, [tokens], [whole(0)], gain, in_weight)
    next_over = across(next_one, own_over, square)
    second_out = along_line(after(middle, square), OUTWARD)
    second_mid = along_line(after(next_one, square), MIDDLE)
    square, *params = lax.optimization_barrier((square, *params))
    acc, square = accumulate(table, [own_over, next_one], [whole(1), whole(2)], gain, in_weight, acc, square)
    second = jnp.where(at_end, second_out, second_mid)
    second_over = across(second, next_over, square)
    third_out = along_line(after(second_mid, square), OUTWARD)
    rest_mid = along_line(after(own_over[:, half:], second_mid, square), MIDDLE)
    acc, square = accumulate(table, [next_over, second], [whole(3), whole(4)], gain, in_weight, acc, square)
    third_over = across(jnp.where(at_end, third_out[:, :half], middle[:, :half]), second_over, square)
    rest_out = along_line(after(second_over[:, half:], square), OUTWARD)
    third = (third_out, middle)
    more, square = accumulate(
        table, [second_over, third], [whole(5), whole(6)], gain, in_weight, None, square
    )
    last = [third_over, (rest_out, rest_mid)]
    places = [(7, 2, 0), (7, 2, 1)]
    rest, inv_rms, rim = accumulate(
        table, last, places, gain, in_weight, None, square, [acc, more]
    )
    return [acc, more, rest], inv_rms, rim, params


def project_and_reduce(table, upper, lower, out_weight, tokens):
    half = tokens.shape[0] // 2
    send = lambda k: (2 * k + 1, jnp.bfloat16)
    keep = lambda k: (2 * k, jnp.float32)
    narrow = lambda a: a.astype(jnp.bfloat16)
    make = functools.partial(pieces, table, out_weight)
    both = (0, 1)

    third_send_0 = make(upper, [send(3)])[0]
    third_over = across(third_send_0)
    lower = lower(third_send_0)
    third_send_1 = make(lower, [send(3)])[0]
    rest_in = along_line(third_send_1, INWARD)
    rest_mid = along_line(third_send_1, MIDDLE)
    second_send_0, third_keep_0 = make(upper, [send(2), keep(3)], third_send_1)
    second_send_1, third_1 = make(lower, [send(2), (keep(3)[0], jnp.bfloat16)], third_over)
    third = [narrow(total(third_keep_0, third_over)), third_1]
    third_in = [along_line(third[h], INWARD) for h in both]
    second_send = [second_send_0, narrow(total(second_send_1, rest_in))]
    second_over = [across(second_send[h], third_over) for h in both]
    halves = (upper, lower)
    later_0 = make(upper, [keep(2), send(1)], third_1)
    later = [later_0, make(lower, [keep(2), send(1)], third_in[0])]
    second = [narrow(total(later[h][0], second_over[h], third_in[h])) for h in both]
    second_in = [along_line(second[h], INWARD) for h in both]
    second_mid = [along_line(second[h], MIDDLE) for h in both]
    next_over = [across(later[h][1], second_over[h]) for h in both]
    later_0 = make(upper, [keep(1), send(0)], second_in[0])
    later = [later_0, make(lower, [keep(1), send(0)], second[1])]
    own_send = [later[0][1], narrow(total(later[1][1], rest_mid))]
    next_one = [narrow(total(later[h][0], next_over[h], second_mid[h])) for h in both]
    next_in = [along_line(next_one[h], PAIRS) for h in both]
    middle_in = [along_line(narrow(total(third[h], second_in[h])), MIDDLE) for h in both]
    own_over = [across(own_send[h], next_over[h]) for h in both]
    own_keep = [make(halves[h], [keep(0)], second_over[1])[0] for h in both]
    base = [total(own_keep[h], tokens[h * half : (h + 1) * half]) for h in both]
    return finish(*[[base[h], own_over[h], next_in[h], middle_in[h]] for h in both])


def convolve_kernel(part_count, *refs):
    part_refs, refs = refs[:part_count], refs[part_count:]
    rms_ref, rim_ref, taps_ref, decay_ref, q_ref, prod_ref, end_ref, win_ref, state_ref = refs
    step = pl.program_id(0)
    rows = q_ref.shape[0]
    tap_count, groups = taps_ref.shape[1:3]
    poles = decay_ref.shape[0]
    keep = rim_ref.shape[1]
    unroll = 8

    @pl.when(step == 0)
    def _():
        for g in range(groups):
            for i in range(3):
                win_ref[i, pl.ds(g, keep, stride=groups), :] = rim_ref[i, :, g * LANES : (g + 1) * LANES]
        state_ref[...] = jnp.zeros_like(state_ref)

    inv_rms = rms_ref[:, :1]
    for i in range(3):
        for g in range(groups):
            cols = tree_sum([ref[i, :, g * LANES : (g + 1) * LANES] for ref in part_refs]) * inv_rms
            cols = cols.astype(jnp.bfloat16).astype(jnp.float32)
            win_ref[i, pl.ds(keep * groups + g, rows, stride=groups), :] = cols
    decay = [jnp.exp(decay_ref[n]) for n in range(poles)]

    def row_of(i, t):
        return win_ref[i, pl.ds(pl.multiple_of(t * groups, groups), groups), :]

    def advance(blk, state):
        state = list(state)
        first = blk * unroll
        conv = []
        for i in range(3):
            taps = [taps_ref[i, j] for j in range(tap_count)]
            held = [row_of(i, first + keep - (tap_count - 1) + r) for r in range(unroll + tap_count - 1)]
            conv.append(
                [
                    functools.reduce(
                        lambda a, b: a + b, [taps[j] * held[r + tap_count - 1 - j] for j in range(tap_count)]
                    )
                    for r in range(unroll)
                ]
            )
        for r in range(unroll):
            q_ref[first + r] = conv[0][r]
            product = conv[1][r] * conv[2][r]
            prod_ref[first + r] = product
            for n in range(poles):
                state[n] = decay[n] * state[n] + product
        return tuple(state)

    state = lax.fori_loop(0, rows // unroll, advance, tuple(state_ref[n] for n in range(poles)))
    for n in range(poles):
        state_ref[n] = state[n]
    win_ref[:, : keep * groups] = win_ref[:, rows * groups :]

    @pl.when(step == pl.num_programs(0) - 1)
    def _():
        for n in range(poles):
            end_ref[n] = state[n]


def convolve(parts, inv_rms, rim, taps, log_decay):
    rows, chans = parts[0].shape[1:]
    groups = chans // LANES
    tap_count, poles = taps.shape[1], log_decay.shape[0]
    keep = rim.shape[1]
    blk = min(128, rows)
    whole = lambda *shape: pl.BlockSpec(shape, lambda t: (0,) * len(shape))
    row_spec = pl.BlockSpec((blk, groups, LANES), lambda t: (t, 0, 0))
    return pl.pallas_call(
        functools.partial(convolve_kernel, len(parts)),
        grid=(rows // blk,),
        in_specs=[pl.BlockSpec((3, blk, chans), lambda t: (0, t, 0))] * len(parts)
        + [
            pl.BlockSpec((blk, LANES), lambda t: (t, 0)),
            whole(3, keep, chans),
            whole(3, tap_count, groups, LANES),
            whole(poles, groups, LANES),
        ],
        out_specs=[row_spec, row_spec, whole(poles, groups, LANES)],
        out_shape=[
            jax.ShapeDtypeStruct((rows, groups, LANES), jnp.float32),
            jax.ShapeDtypeStruct((rows, groups, LANES), jnp.float32),
            jax.ShapeDtypeStruct((poles, groups, LANES), jnp.float32),
        ],
        scratch_shapes=[
            pltpu.VMEM((3, (keep + blk) * groups, LANES), jnp.float32),
            pltpu.VMEM((poles, groups, LANES), jnp.float32),
        ],
        compiler_params=pltpu.CompilerParams(vmem_limit_bytes=VMEM_LIMIT),
        cost_estimate=pl.CostEstimate(
            flops=110 * rows * groups * LANES, bytes_accessed=20 * rows * groups * LANES, transcendentals=0
        ),
        name="convolve",
    )(*parts, inv_rms, rim, taps, log_decay)


def respond_kernel(q_ref, prod_ref, enter_ref, decay_ref, res_ref, skip_ref, *refs):
    out_ref, end_ref, state_ref, row_ref = refs[-4:]
    step = pl.program_id(0)
    rows, groups = q_ref.shape[:2]
    poles = decay_ref.shape[0]
    unroll = 8

    @pl.when(step == 0)
    def _():
        state_ref[...] = enter_ref[...]

    decay = [jnp.exp(decay_ref[n]) for n in range(poles)]
    res = [res_ref[n] for n in range(poles)]
    skip = skip_ref[0]

    def recur(blk, state):
        state = list(state)
        for r in range(unroll):
            t = blk * unroll + r
            product = prod_ref[t]
            sums = [skip * product]
            for n in range(poles):
                state[n] = decay[n] * state[n] + product
                term = res[n] * state[n]
                if n < 3:
                    sums.append(term)
                else:
                    sums[n % 4] = sums[n % 4] + term
            row_ref[pl.ds(pl.multiple_of(t * groups, groups), groups), :] = q_ref[t] * tree_sum(sums)
        return tuple(state)

    state = lax.fori_loop(0, rows // unroll, recur, tuple(state_ref[n] for n in range(poles)))
    for n in range(poles):
        state_ref[n] = state[n]
        end_ref[n] = state[n]
    for g in range(groups):
        out_ref[:, g * LANES : (g + 1) * LANES] = row_ref[pl.ds(g, rows, stride=groups), :].astype(jnp.bfloat16)


def respond(query, product, enter, log_decay, residue, skip, start, rows, *earlier):
    groups = query.shape[1]
    poles = log_decay.shape[0]
    blk = min(128, rows)
    whole = lambda *shape: pl.BlockSpec(shape, lambda t: (0,) * len(shape))
    row_spec = pl.BlockSpec((blk, groups, LANES), lambda t: (t + start // blk, 0, 0))
    return pl.pallas_call(
        respond_kernel,
        grid=(rows // blk,),
        in_specs=[row_spec, row_spec]
        + [whole(poles, groups, LANES)] * 3
        + [whole(1, groups, LANES)]
        + [pl.BlockSpec(memory_space=pl.ANY)] * len(earlier),
        out_specs=[pl.BlockSpec((blk, groups * LANES), lambda t: (t, 0)), whole(poles, groups, LANES)],
        out_shape=[
            jax.ShapeDtypeStruct((rows, groups * LANES), jnp.bfloat16),
            jax.ShapeDtypeStruct((poles, groups, LANES), jnp.float32),
        ],
        scratch_shapes=[
            pltpu.VMEM((poles, groups, LANES), jnp.float32),
            pltpu.VMEM((blk * groups, LANES), jnp.float32),
        ],
        compiler_params=pltpu.CompilerParams(vmem_limit_bytes=VMEM_LIMIT),
        cost_estimate=pl.CostEstimate(
            flops=70 * rows * groups * LANES, bytes_accessed=80 * rows * groups * LANES, transcendentals=0
        ),
        name="respond",
    )(query, product, enter, log_decay, residue, skip, *earlier)


def per_device(tokens, norm_gain, in_weight, short_weight, log_decay, residue, skip, out_weight):
    rows, chans = tokens.shape
    groups = chans // LANES
    by_lane = lambda a: a.reshape(a.shape[:-1] + (groups, LANES))
    taps, log_decay, residue = by_lane(short_weight), by_lane(log_decay), by_lane(residue)
    skip = by_lane(skip[None, :])

    paired_line = lax.axis_size("chan") == 8
    if paired_line:
        me = lax.axis_index("chan")
        at_end = ((me < 2) | (me >= 6)).astype(jnp.int32)
        table = jnp.concatenate([me ^ jnp.arange(8, dtype=jnp.int32), at_end[None]])
        params = (taps, log_decay, residue, skip)
        parts, inv_rms, rim, params = gather_and_project(table, tokens, norm_gain, in_weight, params)
        taps, log_decay, residue, skip = params
    else:
        gathered = lax.all_gather(tokens, "chan", axis=1, tiled=True)
        depth = min(1024, gathered.shape[1])
        chunks = [gathered[:, k : k + depth] for k in range(0, gathered.shape[1], depth)]
        table = jnp.arange(len(chunks), dtype=jnp.int32)
        acc = square = None
        for k, chunk in enumerate(chunks[:-1]):
            acc, square = accumulate(table, [chunk], [(k, 1, 0)], norm_gain, in_weight, acc, square)
        places = [(len(chunks) - 1, 1, 0)]
        acc, inv_rms, rim = accumulate(table, chunks[-1:], places, norm_gain, in_weight, acc, square, [])
        parts = [acc]
    rim = from_behind(rim, "seq", 1)
    query, product, end = convolve(parts, inv_rms, rim, taps, log_decay)
    shard_decay = jnp.exp(rows * log_decay)
    state, passing = jnp.zeros_like(end), end
    for _ in range(lax.axis_size("seq") - 1):
        passing = from_behind(passing, "seq", 1)
        state = state + passing
        passing = passing * shard_decay
    filt = (log_decay, residue, skip)
    if paired_line:
        half = rows // 2
        upper, state = respond(query, product, state, *filt, 0, half)
        lower = lambda *earlier: respond(query, product, state, *filt, half, half, *earlier)[0]
        return project_and_reduce(table, upper, lower, out_weight, tokens)
    gated = respond(query, product, state, *filt, 0, rows)[0]
    partial = jnp.dot(gated, out_weight, preferred_element_type=jnp.float32)
    branch = lax.psum_scatter(partial.astype(jnp.bfloat16), "chan", scatter_dimension=1, tiled=True)
    return (tokens.astype(jnp.float32) + branch.astype(jnp.float32)).astype(jnp.bfloat16)


def solution(mesh):
    return jax.shard_map(
        per_device,
        mesh=mesh,
        in_specs=(
            P(("groups", "seq"), "chan"),
            P(),
            P(None, None, "chan"),
            P(None, None, "chan"),
            P(None, "chan"),
            P(None, "chan"),
            P("chan"),
            P("chan", None),
        ),
        out_specs=P(("groups", "seq"), "chan"),
        check_vma=False,
    )
```

```python
import functools

import jax
import jax.numpy as jnp
from jax import lax
from jax.experimental import pallas as pl
from jax.experimental.pallas import tpu as pltpu
from jax.sharding import PartitionSpec as P

EPSILON = 1e-06
LANES = 128
KEEP = 8
VMEM_LIMIT = 48 * 1024 * 1024


def from_behind(block, axis, distance):
    count = lax.axis_size(axis)
    route = [(i - distance, i) for i in range(count) if i - distance >= 0]
    return lax.ppermute(block, axis, route)


def tree_sum(terms):
    while len(terms) > 1:
        pairs = [terms[i] + terms[i + 1] for i in range(0, len(terms) - 1, 2)]
        terms = pairs + terms[len(pairs) * 2 :]
    return terms[0]


def accumulate_kernel(depths, pairs, width, has_acc, has_sq, part_count, place_ref, *refs):
    def take(count):
        nonlocal refs
        taken, refs = refs[:count], refs[count:]
        return taken

    chunk_refs = take(len(depths) + sum(pairs))
    gain_refs, w_refs = take(len(depths)), take(len(depths))
    held_refs, held_sq_refs = take(int(has_acc)), take(int(has_sq))
    part_refs = take(part_count or 0)
    acc_ref, sq_ref = take(2)
    scaled_ref = refs[-1]
    feat, col = pl.program_id(0), pl.program_id(1)
    last = part_count is not None

    @pl.when((feat == 0) & (col == 0))
    def _():
        square = held_sq_refs[0][...] if has_sq else None
        start = at = 0
        for j, depth in enumerate(depths):
            x = chunk_refs[at][...]
            at += 1
            if pairs[j]:
                x = jnp.where(place_ref[place_ref.shape[0] - 1] == 1, x, chunk_refs[at][...])
                at += 1
            x = x.astype(jnp.float32)
            parts = [x[:, g : g + LANES] * x[:, g : g + LANES] for g in range(0, depth, LANES)]
            part = tree_sum(parts)
            square = part if square is None else square + part
            scaled_ref[:, start : start + depth] = (x * gain_refs[j][0]).astype(jnp.bfloat16)
            start += depth
        if last:
            total = jnp.sum(square, axis=1, keepdims=True)
            square = jnp.broadcast_to(lax.rsqrt(total / width + EPSILON), square.shape)
        sq_ref[...] = square

    start, part = 0, None
    for j, depth in enumerate(depths):
        one = jnp.dot(scaled_ref[:, start : start + depth], w_refs[j][0], preferred_element_type=jnp.float32)
        part = one if part is None else part + one
        start += depth
    acc_ref[0] = held_refs[0][0] + part if has_acc else part
    if last:
        rim_ref = refs[0]
        keep = rim_ref.shape[1]
        rows = acc_ref.shape[1]
        rim = acc_ref[0, rows - keep :, :]
        for ref in part_refs:
            rim = rim + ref[0]
        rim_ref[0] = (rim * sq_ref[rows - keep :, :1]).astype(jnp.bfloat16).astype(jnp.float32)


def accumulate(table, chunks, places, gain, in_weight, acc=None, square=None, parts=None):
    pairs = [isinstance(c, tuple) for c in chunks]
    arrays = [a for c in chunks for a in (c if isinstance(c, tuple) else (c,))]
    depths = [(c[0] if isinstance(c, tuple) else c).shape[1] for c in chunks]
    rows = arrays[0].shape[0]
    width, chans = in_weight.shape[1:]
    tile = min(512, chans)
    acc_spec = pl.BlockSpec((1, rows, tile), lambda i, c, p: (i, 0, c))
    sq_spec = pl.BlockSpec((rows, LANES), lambda i, c, p: (0, 0))
    in_specs = [pl.BlockSpec(a.shape, lambda i, c, p: (0, 0)) for a in arrays]
    for d, (k, per_shard, part) in zip(depths, places):
        place = lambda p, k=k, n=per_shard, part=part: p[k] * n + part
        in_specs.append(pl.BlockSpec((1, 1, d), lambda i, c, p, place=place: (place(p), 0, 0)))
    for d, (k, per_shard, part) in zip(depths, places):
        place = lambda p, k=k, n=per_shard, part=part: p[k] * n + part
        in_specs.append(pl.BlockSpec((1, d, tile), lambda i, c, p, place=place: (i, place(p), c)))
    out_specs = [acc_spec, sq_spec]
    out_shape = [
        jax.ShapeDtypeStruct((3, rows, chans), jnp.float32),
        jax.ShapeDtypeStruct((rows, LANES), jnp.float32),
    ]
    extra, aliases = [], {}
    before = 1 + len(arrays) + 2 * len(depths)
    for n, (held, spec) in enumerate(((acc, acc_spec), (square, sq_spec))):
        if held is not None:
            aliases[before + len(extra)] = n
            extra.append(held)
            in_specs.append(spec)
    if parts is not None:
        extra += parts
        in_specs += [pl.BlockSpec((1, KEEP, tile), lambda i, c, p: (i, rows // KEEP - 1, c))] * len(parts)
        out_specs.append(pl.BlockSpec((1, KEEP, tile), lambda i, c, p: (i, 0, c)))
        out_shape.append(jax.ShapeDtypeStruct((3, KEEP, chans), jnp.float32))
    part_count = None if parts is None else len(parts)
    return pl.pallas_call(
        functools.partial(
            accumulate_kernel, depths, pairs, width, acc is not None, square is not None, part_count
        ),
        grid_spec=pltpu.PrefetchScalarGridSpec(
            num_scalar_prefetch=1,
            grid=(3, chans // tile),
            in_specs=in_specs,
            out_specs=out_specs,
            scratch_shapes=[pltpu.VMEM((rows, sum(depths)), jnp.bfloat16)],
        ),
        out_shape=out_shape,
        input_output_aliases=aliases,
        compiler_params=pltpu.CompilerParams(vmem_limit_bytes=VMEM_LIMIT),
        cost_estimate=pl.CostEstimate(
            flops=rows * sum(depths) * chans,
            bytes_accessed=6 * sum(depths) * chans,
            transcendentals=0,
        ),
        name="accumulate",
    )(
        table,
        *arrays,
        *[gain.reshape(-1, 1, d) for d in depths],
        *[in_weight] * len(depths),
        *extra,
    )


def pieces_kernel(count, place_ref, gated_ref, w_ref, *refs):
    outs = refs[-count:]
    total = jnp.dot(gated_ref[...], w_ref[...], preferred_element_type=jnp.float32)
    for j in range(count):

        @pl.when(pl.program_id(0) == j)
        def _():
            outs[j][...] = total.astype(outs[j].dtype)


def pieces(out_weight, gated, wanted, *earlier):
    rows, chans = gated.shape
    count = len(wanted)
    out = pl.pallas_call(
        functools.partial(pieces_kernel, count),
        grid_spec=pltpu.PrefetchScalarGridSpec(
            num_scalar_prefetch=1,
            grid=(count,),
            in_specs=[
                pl.BlockSpec((rows, chans), lambda t, p: (0, 0)),
                pl.BlockSpec((chans, chans), lambda t, p: (0, p[t])),
            ]
            + [pl.BlockSpec(memory_space=pl.ANY)] * len(earlier),
            out_specs=[pl.BlockSpec((rows, chans), lambda t, p: (0, 0))] * count,
        ),
        out_shape=[jax.ShapeDtypeStruct((rows, chans), dtype) for place, dtype in wanted],
        compiler_params=pltpu.CompilerParams(vmem_limit_bytes=VMEM_LIMIT),
        cost_estimate=pl.CostEstimate(flops=count * 1000000, bytes_accessed=count * 100000, transcendentals=0),
        name="pieces",
    )(jnp.stack([place.astype(jnp.int32) for place, dtype in wanted]), gated, out_weight, *earlier)
    return list(out)


def finish_kernel(*refs):
    out_ref = refs[-1]
    count = (len(refs) - 1) // 2
    step, per_half = pl.program_id(0), pl.num_programs(0) // 2

    for h in range(2):

        @pl.when((step >= h * per_half) & (step < (h + 1) * per_half))
        def _():
            total = refs[h * count][...].astype(jnp.float32)
            for ref in refs[h * count + 1 : (h + 1) * count]:
                total = total + ref[...].astype(jnp.float32)
            out_ref[...] = total.astype(jnp.bfloat16)


def finish(upper, lower):
    rows, chans = upper[0].shape
    blk = min(128, rows)
    per_half = rows // blk
    spec = lambda h: pl.BlockSpec((blk, chans), lambda t: (jnp.clip(t - h * per_half, 0, per_half - 1), 0))
    return pl.pallas_call(
        finish_kernel,
        grid=(2 * per_half,),
        in_specs=[spec(0)] * len(upper) + [spec(1)] * len(lower),
        out_specs=pl.BlockSpec((blk, chans), lambda t: (t, 0)),
        out_shape=jax.ShapeDtypeStruct((2 * rows, chans), jnp.bfloat16),
        compiler_params=pltpu.CompilerParams(vmem_limit_bytes=VMEM_LIMIT),
        name="finish",
    )(*upper, *lower)


def along_line(block, pairs):
    return lax.ppermute(block, "chan", [(2 * a + y, 2 * b + y) for a, b in pairs for y in (0, 1)])


def after(block, *earlier):
    return lax.optimization_barrier((block,) + earlier)[0]


def across(block, *earlier):
    count = lax.axis_size("chan")
    if earlier:
        block = after(block, *earlier)
    return lax.ppermute(block, "chan", [(c, c ^ 1) for c in range(count)])


def total(*terms):
    return functools.reduce(lambda a, b: a + b, [t.astype(jnp.float32) for t in terms])


PAIRS = [(0, 1), (1, 0), (2, 3), (3, 2)]
MIDDLE = [(1, 2), (2, 1)]
OUTWARD = [(1, 0), (2, 3)]
INWARD = [(0, 1), (3, 2)]


def gather_and_project(table, tokens, gain, in_weight, params):
    me = lax.axis_index("chan")
    half = tokens.shape[1] // 2
    at_end = (me < 2) | (me >= 6)
    whole = lambda k: (k, 1, 0)
    own_over = across(tokens)
    next_one = along_line(tokens, PAIRS)
    middle = along_line(tokens, MIDDLE)
    acc, square = accumulate(table, [tokens], [whole(0)], gain, in_weight)
    next_over = across(next_one, own_over, square)
    second_out = along_line(after(middle, square), OUTWARD)
    second_mid = along_line(after(next_one, square), MIDDLE)
    square, *params = lax.optimization_barrier((square, *params))
    acc, square = accumulate(table, [own_over, next_one], [whole(1), whole(2)], gain, in_weight, acc, square)
    second = jnp.where(at_end, second_out, second_mid)
    second_over = across(second, next_over, square)
    third_out = along_line(after(second_mid, square), OUTWARD)
    rest_mid = along_line(after(own_over[:, half:], second_mid, square), MIDDLE)
    acc, square = accumulate(table, [next_over, second], [whole(3), whole(4)], gain, in_weight, acc, square)
    third_over = across(jnp.where(at_end, third_out[:, :half], middle[:, :half]), second_over, square)
    rest_out = along_line(after(second_over[:, half:], square), OUTWARD)
    third = (third_out, middle)
    more, square = accumulate(
        table, [second_over, third], [whole(5), whole(6)], gain, in_weight, None, square
    )
    last = [third_over, (rest_out, rest_mid)]
    places = [(7, 2, 0), (7, 2, 1)]
    rest, inv_rms, rim = accumulate(
        table, last, places, gain, in_weight, None, square, [acc, more]
    )
    return [acc, more, rest], inv_rms, rim, params


def project_and_reduce(upper, lower, out_weight, tokens):
    half = tokens.shape[0] // 2
    me = lax.axis_index("chan")
    send = lambda k: (me ^ (2 * k + 1), jnp.bfloat16)
    keep = lambda k: (me ^ (2 * k), jnp.float32)
    narrow = lambda a: a.astype(jnp.bfloat16)
    make = functools.partial(pieces, out_weight)
    both = (0, 1)

    third_send_0 = make(upper, [send(3)])[0]
    third_over = across(third_send_0)
    lower = lower(third_send_0)
    third_send_1 = make(lower, [send(3)])[0]
    rest_in = along_line(third_send_1, INWARD)
    rest_mid = along_line(third_send_1, MIDDLE)
    second_send_0, third_keep_0 = make(upper, [send(2), keep(3)], third_send_1)
    second_send_1, third_1 = make(lower, [send(2), (keep(3)[0], jnp.bfloat16)], third_over)
    third = [narrow(total(third_keep_0, third_over)), third_1]
    third_in = [along_line(third[h], INWARD) for h in both]
    second_send = [second_send_0, narrow(total(second_send_1, rest_in))]
    second_over = [across(second_send[h], third_over) for h in both]
    halves = (upper, lower)
    later_0 = make(upper, [keep(2), send(1)], third_1)
    later = [later_0, make(lower, [keep(2), send(1)], third_in[0])]
    second = [narrow(total(later[h][0], second_over[h], third_in[h])) for h in both]
    second_in = [along_line(second[h], INWARD) for h in both]
    second_mid = [along_line(second[h], MIDDLE) for h in both]
    next_over = [across(later[h][1], second_over[h]) for h in both]
    later_0 = make(upper, [keep(1), send(0)], second_in[0])
    later = [later_0, make(lower, [keep(1), send(0)], second[1])]
    own_send = [later[0][1], narrow(total(later[1][1], rest_mid))]
    next_one = [narrow(total(later[h][0], next_over[h], second_mid[h])) for h in both]
    next_in = [along_line(next_one[h], PAIRS) for h in both]
    middle_in = [along_line(narrow(total(third[h], second_in[h])), MIDDLE) for h in both]
    own_over = [across(own_send[h], next_over[h]) for h in both]
    own_keep = [make(halves[h], [keep(0)], second_over[1])[0] for h in both]
    base = [total(own_keep[h], tokens[h * half : (h + 1) * half]) for h in both]
    return finish(*[[base[h], own_over[h], next_in[h], middle_in[h]] for h in both])


def convolve_kernel(part_count, *refs):
    part_refs, refs = refs[:part_count], refs[part_count:]
    rms_ref, rim_ref, taps_ref, decay_ref, q_ref, prod_ref, end_ref, win_ref, state_ref = refs
    step = pl.program_id(0)
    rows = q_ref.shape[0]
    tap_count, groups = taps_ref.shape[1:3]
    poles = decay_ref.shape[0]
    keep = rim_ref.shape[1]
    unroll = 8

    @pl.when(step == 0)
    def _():
        for g in range(groups):
            for i in range(3):
                win_ref[i, pl.ds(g, keep, stride=groups), :] = rim_ref[i, :, g * LANES : (g + 1) * LANES]
        state_ref[...] = jnp.zeros_like(state_ref)

    inv_rms = rms_ref[:, :1]
    for i in range(3):
        for g in range(groups):
            cols = tree_sum([ref[i, :, g * LANES : (g + 1) * LANES] for ref in part_refs]) * inv_rms
            cols = cols.astype(jnp.bfloat16).astype(jnp.float32)
            win_ref[i, pl.ds(keep * groups + g, rows, stride=groups), :] = cols
    decay = [jnp.exp(decay_ref[n]) for n in range(poles)]

    def row_of(i, t):
        return win_ref[i, pl.ds(pl.multiple_of(t * groups, groups), groups), :]

    def advance(blk, state):
        state = list(state)
        first = blk * unroll
        conv = []
        for i in range(3):
            taps = [taps_ref[i, j] for j in range(tap_count)]
            held = [row_of(i, first + keep - (tap_count - 1) + r) for r in range(unroll + tap_count - 1)]
            conv.append(
                [
                    functools.reduce(
                        lambda a, b: a + b, [taps[j] * held[r + tap_count - 1 - j] for j in range(tap_count)]
                    )
                    for r in range(unroll)
                ]
            )
        for r in range(unroll):
            q_ref[first + r] = conv[0][r]
            product = conv[1][r] * conv[2][r]
            prod_ref[first + r] = product
            for n in range(poles):
                state[n] = decay[n] * state[n] + product
        return tuple(state)

    state = lax.fori_loop(0, rows // unroll, advance, tuple(state_ref[n] for n in range(poles)))
    for n in range(poles):
        state_ref[n] = state[n]
    win_ref[:, : keep * groups] = win_ref[:, rows * groups :]

    @pl.when(step == pl.num_programs(0) - 1)
    def _():
        for n in range(poles):
            end_ref[n] = state[n]


def convolve(parts, inv_rms, rim, taps, log_decay):
    rows, chans = parts[0].shape[1:]
    groups = chans // LANES
    tap_count, poles = taps.shape[1], log_decay.shape[0]
    keep = rim.shape[1]
    blk = min(128, rows)
    whole = lambda *shape: pl.BlockSpec(shape, lambda t: (0,) * len(shape))
    row_spec = pl.BlockSpec((blk, groups, LANES), lambda t: (t, 0, 0))
    return pl.pallas_call(
        functools.partial(convolve_kernel, len(parts)),
        grid=(rows // blk,),
        in_specs=[pl.BlockSpec((3, blk, chans), lambda t: (0, t, 0))] * len(parts)
        + [
            pl.BlockSpec((blk, LANES), lambda t: (t, 0)),
            whole(3, keep, chans),
            whole(3, tap_count, groups, LANES),
            whole(poles, groups, LANES),
        ],
        out_specs=[row_spec, row_spec, whole(poles, groups, LANES)],
        out_shape=[
            jax.ShapeDtypeStruct((rows, groups, LANES), jnp.float32),
            jax.ShapeDtypeStruct((rows, groups, LANES), jnp.float32),
            jax.ShapeDtypeStruct((poles, groups, LANES), jnp.float32),
        ],
        scratch_shapes=[
            pltpu.VMEM((3, (keep + blk) * groups, LANES), jnp.float32),
            pltpu.VMEM((poles, groups, LANES), jnp.float32),
        ],
        compiler_params=pltpu.CompilerParams(vmem_limit_bytes=VMEM_LIMIT),
        cost_estimate=pl.CostEstimate(
            flops=110 * rows * groups * LANES, bytes_accessed=20 * rows * groups * LANES, transcendentals=0
        ),
        name="convolve",
    )(*parts, inv_rms, rim, taps, log_decay)


def respond_kernel(q_ref, prod_ref, enter_ref, decay_ref, res_ref, skip_ref, *refs):
    out_ref, end_ref, state_ref, row_ref = refs[-4:]
    step = pl.program_id(0)
    rows, groups = q_ref.shape[:2]
    poles = decay_ref.shape[0]
    unroll = 8

    @pl.when(step == 0)
    def _():
        state_ref[...] = enter_ref[...]

    decay = [jnp.exp(decay_ref[n]) for n in range(poles)]
    res = [res_ref[n] for n in range(poles)]
    skip = skip_ref[0]

    def recur(blk, state):
        state = list(state)
        for r in range(unroll):
            t = blk * unroll + r
            product = prod_ref[t]
            sums = [skip * product]
            for n in range(poles):
                state[n] = decay[n] * state[n] + product
                term = res[n] * state[n]
                if n < 3:
                    sums.append(term)
                else:
                    sums[n % 4] = sums[n % 4] + term
            row_ref[pl.ds(pl.multiple_of(t * groups, groups), groups), :] = q_ref[t] * tree_sum(sums)
        return tuple(state)

    state = lax.fori_loop(0, rows // unroll, recur, tuple(state_ref[n] for n in range(poles)))
    for n in range(poles):
        state_ref[n] = state[n]
        end_ref[n] = state[n]
    for g in range(groups):
        out_ref[:, g * LANES : (g + 1) * LANES] = row_ref[pl.ds(g, rows, stride=groups), :].astype(jnp.bfloat16)


def respond(query, product, enter, log_decay, residue, skip, start, rows, *earlier):
    groups = query.shape[1]
    poles = log_decay.shape[0]
    blk = min(128, rows)
    whole = lambda *shape: pl.BlockSpec(shape, lambda t: (0,) * len(shape))
    row_spec = pl.BlockSpec((blk, groups, LANES), lambda t: (t + start // blk, 0, 0))
    return pl.pallas_call(
        respond_kernel,
        grid=(rows // blk,),
        in_specs=[row_spec, row_spec]
        + [whole(poles, groups, LANES)] * 3
        + [whole(1, groups, LANES)]
        + [pl.BlockSpec(memory_space=pl.ANY)] * len(earlier),
        out_specs=[pl.BlockSpec((blk, groups * LANES), lambda t: (t, 0)), whole(poles, groups, LANES)],
        out_shape=[
            jax.ShapeDtypeStruct((rows, groups * LANES), jnp.bfloat16),
            jax.ShapeDtypeStruct((poles, groups, LANES), jnp.float32),
        ],
        scratch_shapes=[
            pltpu.VMEM((poles, groups, LANES), jnp.float32),
            pltpu.VMEM((blk * groups, LANES), jnp.float32),
        ],
        compiler_params=pltpu.CompilerParams(vmem_limit_bytes=VMEM_LIMIT),
        cost_estimate=pl.CostEstimate(
            flops=70 * rows * groups * LANES, bytes_accessed=80 * rows * groups * LANES, transcendentals=0
        ),
        name="respond",
    )(query, product, enter, log_decay, residue, skip, *earlier)


def per_device(tokens, norm_gain, in_weight, short_weight, log_decay, residue, skip, out_weight):
    rows, chans = tokens.shape
    groups = chans // LANES
    by_lane = lambda a: a.reshape(a.shape[:-1] + (groups, LANES))
    taps, log_decay, residue = by_lane(short_weight), by_lane(log_decay), by_lane(residue)
    skip = by_lane(skip[None, :])

    paired_line = lax.axis_size("chan") == 8
    if paired_line:
        me = lax.axis_index("chan")
        at_end = ((me < 2) | (me >= 6)).astype(jnp.int32)
        table = jnp.concatenate([me ^ jnp.arange(8, dtype=jnp.int32), at_end[None]])
        params = (taps, log_decay, residue, skip)
        parts, inv_rms, rim, params = gather_and_project(table, tokens, norm_gain, in_weight, params)
        taps, log_decay, residue, skip = params
    else:
        gathered = lax.all_gather(tokens, "chan", axis=1, tiled=True)
        depth = min(1024, gathered.shape[1])
        chunks = [gathered[:, k : k + depth] for k in range(0, gathered.shape[1], depth)]
        table = jnp.arange(len(chunks), dtype=jnp.int32)
        acc = square = None
        for k, chunk in enumerate(chunks[:-1]):
            acc, square = accumulate(table, [chunk], [(k, 1, 0)], norm_gain, in_weight, acc, square)
        places = [(len(chunks) - 1, 1, 0)]
        acc, inv_rms, rim = accumulate(table, chunks[-1:], places, norm_gain, in_weight, acc, square, [])
        parts = [acc]
    rim = from_behind(rim, "seq", 1)
    query, product, end = convolve(parts, inv_rms, rim, taps, log_decay)
    shard_decay = jnp.exp(rows * log_decay)
    state, passing = jnp.zeros_like(end), end
    for _ in range(lax.axis_size("seq") - 1):
        passing = from_behind(passing, "seq", 1)
        state = state + passing
        passing = passing * shard_decay
    filt = (log_decay, residue, skip)
    if paired_line:
        half = rows // 2
        upper, state = respond(query, product, state, *filt, 0, half)
        lower = lambda *earlier: respond(query, product, state, *filt, half, half, *earlier)[0]
        return project_and_reduce(upper, lower, out_weight, tokens)
    gated = respond(query, product, state, *filt, 0, rows)[0]
    partial = jnp.dot(gated, out_weight, preferred_element_type=jnp.float32)
    branch = lax.psum_scatter(partial.astype(jnp.bfloat16), "chan", scatter_dimension=1, tiled=True)
    return (tokens.astype(jnp.float32) + branch.astype(jnp.float32)).astype(jnp.bfloat16)


def solution(mesh):
    return jax.shard_map(
        per_device,
        mesh=mesh,
        in_specs=(
            P(("groups", "seq"), "chan"),
            P(),
            P(None, None, "chan"),
            P(None, None, "chan"),
            P(None, "chan"),
            P(None, "chan"),
            P("chan"),
            P("chan", None),
        ),
        out_specs=P(("groups", "seq"), "chan"),
        check_vma=False,
    )
```

```python
import functools

import jax
import jax.numpy as jnp
from jax import lax
from jax.experimental import pallas as pl
from jax.experimental.pallas import tpu as pltpu
from jax.sharding import PartitionSpec as P

EPSILON = 1e-06
LANES = 128
KEEP = 8
VMEM_LIMIT = 48 * 1024 * 1024


def from_behind(block, axis, distance):
    count = lax.axis_size(axis)
    route = [(i - distance, i) for i in range(count) if i - distance >= 0]
    return lax.ppermute(block, axis, route)


def tree_sum(terms):
    while len(terms) > 1:
        pairs = [terms[i] + terms[i + 1] for i in range(0, len(terms) - 1, 2)]
        terms = pairs + terms[len(pairs) * 2 :]
    return terms[0]


def accumulate_kernel(depths, pairs, width, has_acc, has_sq, part_count, place_ref, *refs):
    def take(count):
        nonlocal refs
        taken, refs = refs[:count], refs[count:]
        return taken

    chunk_refs = take(len(depths) + sum(pairs))
    gain_refs, w_refs = take(len(depths)), take(len(depths))
    held_refs, held_sq_refs = take(int(has_acc)), take(int(has_sq))
    part_refs = take(part_count or 0)
    acc_ref, sq_ref = take(2)
    scaled_ref = refs[-1]
    feat, col = pl.program_id(0), pl.program_id(1)
    last = part_count is not None

    @pl.when((feat == 0) & (col == 0))
    def _():
        square = held_sq_refs[0][...] if has_sq else None
        start = at = 0
        for j, depth in enumerate(depths):
            x = chunk_refs[at][...]
            at += 1
            if pairs[j]:
                x = jnp.where(place_ref[place_ref.shape[0] - 1] == 1, x, chunk_refs[at][...])
                at += 1
            x = x.astype(jnp.float32)
            parts = [x[:, g : g + LANES] * x[:, g : g + LANES] for g in range(0, depth, LANES)]
            part = tree_sum(parts)
            square = part if square is None else square + part
            scaled_ref[:, start : start + depth] = (x * gain_refs[j][0]).astype(jnp.bfloat16)
            start += depth
        if last:
            total = jnp.sum(square, axis=1, keepdims=True)
            square = jnp.broadcast_to(lax.rsqrt(total / width + EPSILON), square.shape)
        sq_ref[...] = square

    start, part = 0, None
    for j, depth in enumerate(depths):
        one = jnp.dot(scaled_ref[:, start : start + depth], w_refs[j][0], preferred_element_type=jnp.float32)
        part = one if part is None else part + one
        start += depth
    acc_ref[0] = held_refs[0][0] + part if has_acc else part
    if last:
        rim_ref = refs[0]
        keep = rim_ref.shape[1]
        rows = acc_ref.shape[1]
        rim = acc_ref[0, rows - keep :, :]
        for ref in part_refs:
            rim = rim + ref[0]
        rim_ref[0] = (rim * sq_ref[rows - keep :, :1]).astype(jnp.bfloat16).astype(jnp.float32)


def accumulate(table, chunks, places, gain, in_weight, acc=None, square=None, parts=None):
    pairs = [isinstance(c, tuple) for c in chunks]
    arrays = [a for c in chunks for a in (c if isinstance(c, tuple) else (c,))]
    depths = [(c[0] if isinstance(c, tuple) else c).shape[1] for c in chunks]
    rows = arrays[0].shape[0]
    width, chans = in_weight.shape[1:]
    tile = min(512, chans)
    acc_spec = pl.BlockSpec((1, rows, tile), lambda i, c, p: (i, 0, c))
    sq_spec = pl.BlockSpec((rows, LANES), lambda i, c, p: (0, 0))
    in_specs = [pl.BlockSpec(a.shape, lambda i, c, p: (0, 0)) for a in arrays]
    for d, (k, per_shard, part) in zip(depths, places):
        place = lambda p, k=k, n=per_shard, part=part: p[k] * n + part
        in_specs.append(pl.BlockSpec((1, 1, d), lambda i, c, p, place=place: (place(p), 0, 0)))
    for d, (k, per_shard, part) in zip(depths, places):
        place = lambda p, k=k, n=per_shard, part=part: p[k] * n + part
        in_specs.append(pl.BlockSpec((1, d, tile), lambda i, c, p, place=place: (i, place(p), c)))
    out_specs = [acc_spec, sq_spec]
    out_shape = [
        jax.ShapeDtypeStruct((3, rows, chans), jnp.float32),
        jax.ShapeDtypeStruct((rows, LANES), jnp.float32),
    ]
    extra, aliases = [], {}
    before = 1 + len(arrays) + 2 * len(depths)
    for n, (held, spec) in enumerate(((acc, acc_spec), (square, sq_spec))):
        if held is not None:
            aliases[before + len(extra)] = n
            extra.append(held)
            in_specs.append(spec)
    if parts is not None:
        extra += parts
        in_specs += [pl.BlockSpec((1, KEEP, tile), lambda i, c, p: (i, rows // KEEP - 1, c))] * len(parts)
        out_specs.append(pl.BlockSpec((1, KEEP, tile), lambda i, c, p: (i, 0, c)))
        out_shape.append(jax.ShapeDtypeStruct((3, KEEP, chans), jnp.float32))
    part_count = None if parts is None else len(parts)
    return pl.pallas_call(
        functools.partial(
            accumulate_kernel, depths, pairs, width, acc is not None, square is not None, part_count
        ),
        grid_spec=pltpu.PrefetchScalarGridSpec(
            num_scalar_prefetch=1,
            grid=(3, chans // tile),
            in_specs=in_specs,
            out_specs=out_specs,
            scratch_shapes=[pltpu.VMEM((rows, sum(depths)), jnp.bfloat16)],
        ),
        out_shape=out_shape,
        input_output_aliases=aliases,
        compiler_params=pltpu.CompilerParams(vmem_limit_bytes=VMEM_LIMIT),
        cost_estimate=pl.CostEstimate(
            flops=rows * sum(depths) * chans,
            bytes_accessed=6 * sum(depths) * chans,
            transcendentals=0,
        ),
        name="accumulate",
    )(
        table,
        *arrays,
        *[gain.reshape(-1, 1, d) for d in depths],
        *[in_weight] * len(depths),
        *extra,
    )


def pieces_kernel(count, place_ref, gated_ref, w_ref, *refs):
    outs = refs[-count:]
    total = jnp.dot(gated_ref[...], w_ref[...], preferred_element_type=jnp.float32)
    for j in range(count):

        @pl.when(pl.program_id(0) == j)
        def _():
            outs[j][...] = total.astype(outs[j].dtype)


def pieces(table, out_weight, gated, wanted, *earlier):
    rows, chans = gated.shape
    count = len(wanted)

    def place(t, p):
        shard = p[wanted[0][0]]
        for j in range(1, count):
            shard = jnp.where(t == j, p[wanted[j][0]], shard)
        return shard

    out = pl.pallas_call(
        functools.partial(pieces_kernel, count),
        grid_spec=pltpu.PrefetchScalarGridSpec(
            num_scalar_prefetch=1,
            grid=(count,),
            in_specs=[
                pl.BlockSpec((rows, chans), lambda t, p: (0, 0)),
                pl.BlockSpec((chans, chans), lambda t, p: (0, place(t, p))),
            ]
            + [pl.BlockSpec(memory_space=pl.ANY)] * len(earlier),
            out_specs=[pl.BlockSpec((rows, chans), lambda t, p: (0, 0))] * count,
        ),
        out_shape=[jax.ShapeDtypeStruct((rows, chans), dtype) for k, dtype in wanted],
        compiler_params=pltpu.CompilerParams(vmem_limit_bytes=VMEM_LIMIT),
        cost_estimate=pl.CostEstimate(flops=count * 1000000, bytes_accessed=count * 100000, transcendentals=0),
        name="pieces",
    )(table, gated, out_weight, *earlier)
    return list(out)


def finish_kernel(*refs):
    out_ref = refs[-1]
    count = (len(refs) - 1) // 2
    step, per_half = pl.program_id(0), pl.num_programs(0) // 2

    for h in range(2):

        @pl.when((step >= h * per_half) & (step < (h + 1) * per_half))
        def _():
            total = refs[h * count][...].astype(jnp.float32)
            for ref in refs[h * count + 1 : (h + 1) * count]:
                total = total + ref[...].astype(jnp.float32)
            out_ref[...] = total.astype(jnp.bfloat16)


def finish(upper, lower):
    rows, chans = upper[0].shape
    blk = min(128, rows)
    per_half = rows // blk
    spec = lambda h: pl.BlockSpec((blk, chans), lambda t: (jnp.clip(t - h * per_half, 0, per_half - 1), 0))
    return pl.pallas_call(
        finish_kernel,
        grid=(2 * per_half,),
        in_specs=[spec(0)] * len(upper) + [spec(1)] * len(lower),
        out_specs=pl.BlockSpec((blk, chans), lambda t: (t, 0)),
        out_shape=jax.ShapeDtypeStruct((2 * rows, chans), jnp.bfloat16),
        compiler_params=pltpu.CompilerParams(vmem_limit_bytes=VMEM_LIMIT),
        name="finish",
    )(*upper, *lower)


def along_line(block, pairs):
    return lax.ppermute(block, "chan", [(2 * a + y, 2 * b + y) for a, b in pairs for y in (0, 1)])


def after(block, *earlier):
    return lax.optimization_barrier((block,) + earlier)[0]


def across(block, *earlier):
    count = lax.axis_size("chan")
    if earlier:
        block = after(block, *earlier)
    return lax.ppermute(block, "chan", [(c, c ^ 1) for c in range(count)])


def total(*terms):
    return functools.reduce(lambda a, b: a + b, [t.astype(jnp.float32) for t in terms])


PAIRS = [(0, 1), (1, 0), (2, 3), (3, 2)]
MIDDLE = [(1, 2), (2, 1)]
OUTWARD = [(1, 0), (2, 3)]
INWARD = [(0, 1), (3, 2)]


def gather_and_project(table, tokens, gain, in_weight, params):
    me = lax.axis_index("chan")
    half = tokens.shape[1] // 2
    at_end = (me < 2) | (me >= 6)
    whole = lambda k: (k, 1, 0)
    own_over = across(tokens)
    next_one = along_line(tokens, PAIRS)
    middle = along_line(tokens, MIDDLE)
    acc, square = accumulate(table, [tokens], [whole(0)], gain, in_weight)
    next_over = across(next_one, own_over, square)
    second_out = along_line(after(middle, square), OUTWARD)
    second_mid = along_line(after(next_one, square), MIDDLE)
    square, *params = lax.optimization_barrier((square, *params))
    acc, square = accumulate(table, [own_over, next_one], [whole(1), whole(2)], gain, in_weight, acc, square)
    second = jnp.where(at_end, second_out, second_mid)
    second_over = across(second, next_over, square)
    third_out = along_line(after(second_mid, square), OUTWARD)
    rest_mid = along_line(after(own_over[:, half:], second_mid, square), MIDDLE)
    acc, square = accumulate(table, [next_over, second], [whole(3), whole(4)], gain, in_weight, acc, square)
    third_over = across(jnp.where(at_end, third_out[:, :half], middle[:, :half]), second_over, square)
    rest_out = along_line(after(second_over[:, half:], square), OUTWARD)
    third = (third_out, middle)
    more, square = accumulate(
        table, [second_over, third], [whole(5), whole(6)], gain, in_weight, None, square
    )
    last = [third_over, (rest_out, rest_mid)]
    places = [(7, 2, 0), (7, 2, 1)]
    rest, inv_rms, rim = accumulate(
        table, last, places, gain, in_weight, None, square, [acc, more]
    )
    return [acc, more, rest], inv_rms, rim, params


def project_and_reduce(table, upper, lower, out_weight, tokens):
    half = tokens.shape[0] // 2
    send = lambda k: (2 * k + 1, jnp.bfloat16)
    keep = lambda k: (2 * k, jnp.float32)
    narrow = lambda a: a.astype(jnp.bfloat16)
    make = functools.partial(pieces, table, out_weight)
    both = (0, 1)

    third_send_0 = make(upper, [send(3)])[0]
    third_over = across(third_send_0)
    lower = lower(third_send_0)
    third_send_1 = make(lower, [send(3)])[0]
    rest_in = along_line(third_send_1, INWARD)
    rest_mid = along_line(third_send_1, MIDDLE)
    second_send_0, third_keep_0 = make(upper, [send(2), keep(3)], third_send_1)
    second_send_1, third_1 = make(lower, [send(2), (keep(3)[0], jnp.bfloat16)], third_over)
    third = [narrow(total(third_keep_0, third_over)), third_1]
    third_in = [along_line(third[h], INWARD) for h in both]
    second_send = [second_send_0, narrow(total(second_send_1, rest_in))]
    second_over = [across(second_send[h], third_over) for h in both]
    halves = (upper, lower)
    later_0 = make(upper, [keep(2), send(1)], third_1)
    later = [later_0, make(lower, [keep(2), send(1)], third_in[0])]
    second = [narrow(total(later[h][0], second_over[h], third_in[h])) for h in both]
    second_in = [along_line(second[h], INWARD) for h in both]
    second_mid = [along_line(second[h], MIDDLE) for h in both]
    next_over = [across(later[h][1], second_over[h]) for h in both]
    later_0 = make(upper, [keep(1), send(0)], second_in[0])
    later = [later_0, make(lower, [keep(1), send(0)], second[1])]
    own_send = [later[0][1], narrow(total(later[1][1], rest_mid))]
    next_one = [narrow(total(later[h][0], next_over[h], second_mid[h])) for h in both]
    next_in = [along_line(next_one[h], PAIRS) for h in both]
    middle_in = [along_line(narrow(total(third[h], second_in[h])), MIDDLE) for h in both]
    own_over = [across(own_send[h], next_over[h]) for h in both]
    own_keep = [make(halves[h], [keep(0)], second_over[1])[0] for h in both]
    base = [total(own_keep[h], tokens[h * half : (h + 1) * half]) for h in both]
    return finish(*[[base[h], own_over[h], next_in[h], middle_in[h]] for h in both])


def convolve_kernel(part_count, after_rows, *refs):
    part_refs, refs = refs[:part_count], refs[part_count:]
    rms_ref, refs = refs[0], refs[1:]
    taps_ref, decay_ref, refs = refs[0], refs[1], refs[2:]
    own_rim = after_rows is None
    if own_rim:
        rim_refs, rim_rms_ref = refs[:part_count], refs[part_count]
    else:
        rim_ref, later_ref = refs[:2]
    q_ref, prod_ref, end_ref, win_ref, state_ref = refs[-5:]
    step = pl.program_id(0)
    rows = q_ref.shape[0]
    tap_count, groups = taps_ref.shape[1:3]
    poles = decay_ref.shape[0]
    keep = win_ref.shape[1] // groups - rows
    unroll = 8

    def rounded(sources, scale, i, g):
        cols = tree_sum([ref[i, :, g * LANES : (g + 1) * LANES] for ref in sources]) * scale
        return cols.astype(jnp.bfloat16).astype(jnp.float32)

    @pl.when(step == 0)
    def _():
        for g in range(groups):
            for i in range(3):
                if own_rim:
                    rim = rounded(rim_refs, rim_rms_ref[:, :1], i, g)
                else:
                    rim = rim_ref[i, :, g * LANES : (g + 1) * LANES]
                win_ref[i, pl.ds(g, keep, stride=groups), :] = rim
        state_ref[...] = jnp.zeros_like(state_ref)

    inv_rms = rms_ref[:, :1]
    for i in range(3):
        for g in range(groups):
            win_ref[i, pl.ds(keep * groups + g, rows, stride=groups), :] = rounded(part_refs, inv_rms, i, g)
    decay = [jnp.exp(decay_ref[n]) for n in range(poles)]

    def row_of(i, t):
        return win_ref[i, pl.ds(pl.multiple_of(t * groups, groups), groups), :]

    def advance(blk, state):
        state = list(state)
        first = blk * unroll
        conv = []
        for i in range(3):
            taps = [taps_ref[i, j] for j in range(tap_count)]
            held = [row_of(i, first + keep - (tap_count - 1) + r) for r in range(unroll + tap_count - 1)]
            conv.append(
                [
                    functools.reduce(
                        lambda a, b: a + b, [taps[j] * held[r + tap_count - 1 - j] for j in range(tap_count)]
                    )
                    for r in range(unroll)
                ]
            )
        for r in range(unroll):
            q_ref[first + r] = conv[0][r]
            product = conv[1][r] * conv[2][r]
            prod_ref[first + r] = product
            for n in range(poles):
                state[n] = decay[n] * state[n] + product
        return tuple(state)

    state = lax.fori_loop(0, rows // unroll, advance, tuple(state_ref[n] for n in range(poles)))
    for n in range(poles):
        state_ref[n] = state[n]
    win_ref[:, : keep * groups] = win_ref[:, rows * groups :]

    @pl.when(step == pl.num_programs(0) - 1)
    def _():
        for n in range(poles):
            if own_rim:
                end_ref[n] = state[n]
            else:
                end_ref[n] = later_ref[n] + jnp.exp(float(after_rows) * decay_ref[n]) * state[n]


def convolve(parts, inv_rms, taps, log_decay, rim=None, done=None):
    rows, chans = parts[0].shape[1:]
    groups = chans // LANES
    tap_count, poles = taps.shape[1], log_decay.shape[0]
    count = len(parts)
    blk = min(64, rows // 2)
    whole = lambda *shape: pl.BlockSpec(shape, lambda t: (0,) * len(shape))
    start = 1 if rim is None else 0
    row_spec = pl.BlockSpec((blk, groups, LANES), lambda t: (t + start, 0, 0))
    state_spec = whole(poles, groups, LANES)
    in_specs = [pl.BlockSpec((3, blk, chans), lambda t: (0, t + start, 0))] * count
    in_specs += [pl.BlockSpec((blk, LANES), lambda t: (t + start, 0)), whole(3, tap_count, groups, LANES), state_spec]
    operands, aliases = [*parts, inv_rms, taps, log_decay], {}
    if rim is None:
        at = blk // KEEP - 1
        in_specs += [pl.BlockSpec((3, KEEP, chans), lambda t: (0, at, 0))] * count
        in_specs += [pl.BlockSpec((KEEP, LANES), lambda t: (at, 0))]
        operands += [*parts, inv_rms]
    else:
        query, product, end = done
        in_specs += [whole(3, KEEP, chans), state_spec] + [pl.BlockSpec(memory_space=pl.ANY)] * 2
        operands += [rim, end, query, product]
        aliases = {len(operands) - 2: 0, len(operands) - 1: 1}
    return pl.pallas_call(
        functools.partial(convolve_kernel, count, None if rim is None else rows - blk),
        grid=(rows // blk - 1 if rim is None else 1,),
        in_specs=in_specs,
        out_specs=[row_spec, row_spec, state_spec],
        out_shape=[
            jax.ShapeDtypeStruct((rows, groups, LANES), jnp.float32),
            jax.ShapeDtypeStruct((rows, groups, LANES), jnp.float32),
            jax.ShapeDtypeStruct((poles, groups, LANES), jnp.float32),
        ],
        scratch_shapes=[
            pltpu.VMEM((3, (KEEP + blk) * groups, LANES), jnp.float32),
            pltpu.VMEM((poles, groups, LANES), jnp.float32),
        ],
        input_output_aliases=aliases,
        compiler_params=pltpu.CompilerParams(vmem_limit_bytes=VMEM_LIMIT),
        cost_estimate=pl.CostEstimate(
            flops=80 * rows * groups * LANES, bytes_accessed=20 * rows * groups * LANES, transcendentals=0
        ),
        name="convolve",
    )(*operands)


def respond_kernel(q_ref, prod_ref, enter_ref, decay_ref, res_ref, skip_ref, *refs):
    out_ref, end_ref, state_ref, row_ref = refs[-4:]
    step = pl.program_id(0)
    rows, groups = q_ref.shape[:2]
    poles = decay_ref.shape[0]
    unroll = 8

    @pl.when(step == 0)
    def _():
        state_ref[...] = enter_ref[...]

    decay = [jnp.exp(decay_ref[n]) for n in range(poles)]
    res = [res_ref[n] for n in range(poles)]
    skip = skip_ref[0]

    def recur(blk, state):
        state = list(state)
        for r in range(unroll):
            t = blk * unroll + r
            product = prod_ref[t]
            sums = [skip * product]
            for n in range(poles):
                state[n] = decay[n] * state[n] + product
                term = res[n] * state[n]
                if n < 3:
                    sums.append(term)
                else:
                    sums[n % 4] = sums[n % 4] + term
            row_ref[pl.ds(pl.multiple_of(t * groups, groups), groups), :] = q_ref[t] * tree_sum(sums)
        return tuple(state)

    state = lax.fori_loop(0, rows // unroll, recur, tuple(state_ref[n] for n in range(poles)))
    for n in range(poles):
        state_ref[n] = state[n]
        end_ref[n] = state[n]
    for g in range(groups):
        out_ref[:, g * LANES : (g + 1) * LANES] = row_ref[pl.ds(g, rows, stride=groups), :].astype(jnp.bfloat16)


def respond(query, product, enter, log_decay, residue, skip, start, rows, *earlier):
    groups = query.shape[1]
    poles = log_decay.shape[0]
    blk = min(128, rows)
    whole = lambda *shape: pl.BlockSpec(shape, lambda t: (0,) * len(shape))
    row_spec = pl.BlockSpec((blk, groups, LANES), lambda t: (t + start // blk, 0, 0))
    return pl.pallas_call(
        respond_kernel,
        grid=(rows // blk,),
        in_specs=[row_spec, row_spec]
        + [whole(poles, groups, LANES)] * 3
        + [whole(1, groups, LANES)]
        + [pl.BlockSpec(memory_space=pl.ANY)] * len(earlier),
        out_specs=[pl.BlockSpec((blk, groups * LANES), lambda t: (t, 0)), whole(poles, groups, LANES)],
        out_shape=[
            jax.ShapeDtypeStruct((rows, groups * LANES), jnp.bfloat16),
            jax.ShapeDtypeStruct((poles, groups, LANES), jnp.float32),
        ],
        scratch_shapes=[
            pltpu.VMEM((poles, groups, LANES), jnp.float32),
            pltpu.VMEM((blk * groups, LANES), jnp.float32),
        ],
        compiler_params=pltpu.CompilerParams(vmem_limit_bytes=VMEM_LIMIT),
        cost_estimate=pl.CostEstimate(
            flops=70 * rows * groups * LANES, bytes_accessed=80 * rows * groups * LANES, transcendentals=0
        ),
        name="respond",
    )(query, product, enter, log_decay, residue, skip, *earlier)


def per_device(tokens, norm_gain, in_weight, short_weight, log_decay, residue, skip, out_weight):
    rows, chans = tokens.shape
    groups = chans // LANES
    by_lane = lambda a: a.reshape(a.shape[:-1] + (groups, LANES))
    taps, log_decay, residue = by_lane(short_weight), by_lane(log_decay), by_lane(residue)
    skip = by_lane(skip[None, :])

    paired_line = lax.axis_size("chan") == 8
    if paired_line:
        me = lax.axis_index("chan")
        at_end = ((me < 2) | (me >= 6)).astype(jnp.int32)
        table = jnp.concatenate([me ^ jnp.arange(8, dtype=jnp.int32), at_end[None]])
        params = (taps, log_decay, residue, skip)
        parts, inv_rms, rim, params = gather_and_project(table, tokens, norm_gain, in_weight, params)
        taps, log_decay, residue, skip = params
    else:
        gathered = lax.all_gather(tokens, "chan", axis=1, tiled=True)
        depth = min(1024, gathered.shape[1])
        chunks = [gathered[:, k : k + depth] for k in range(0, gathered.shape[1], depth)]
        table = jnp.arange(len(chunks), dtype=jnp.int32)
        acc = square = None
        for k, chunk in enumerate(chunks[:-1]):
            acc, square = accumulate(table, [chunk], [(k, 1, 0)], norm_gain, in_weight, acc, square)
        places = [(len(chunks) - 1, 1, 0)]
        acc, inv_rms, rim = accumulate(table, chunks[-1:], places, norm_gain, in_weight, acc, square, [])
        parts = [acc]
    rim = from_behind(rim, "seq", 1)
    done = convolve(parts, inv_rms, taps, log_decay)
    query, product, end = convolve(parts, inv_rms, taps, log_decay, rim, done)
    shard_decay = jnp.exp(rows * log_decay)
    state, passing = jnp.zeros_like(end), end
    for _ in range(lax.axis_size("seq") - 1):
        passing = from_behind(passing, "seq", 1)
        state = state + passing
        passing = passing * shard_decay
    filt = (log_decay, residue, skip)
    if paired_line:
        half = rows // 2
        upper, state = respond(query, product, state, *filt, 0, half)
        lower = lambda *earlier: respond(query, product, state, *filt, half, half, *earlier)[0]
        return project_and_reduce(table, upper, lower, out_weight, tokens)
    gated = respond(query, product, state, *filt, 0, rows)[0]
    partial = jnp.dot(gated, out_weight, preferred_element_type=jnp.float32)
    branch = lax.psum_scatter(partial.astype(jnp.bfloat16), "chan", scatter_dimension=1, tiled=True)
    return (tokens.astype(jnp.float32) + branch.astype(jnp.float32)).astype(jnp.bfloat16)


def solution(mesh):
    return jax.shard_map(
        per_device,
        mesh=mesh,
        in_specs=(
            P(("groups", "seq"), "chan"),
            P(),
            P(None, None, "chan"),
            P(None, None, "chan"),
            P(None, "chan"),
            P(None, "chan"),
            P("chan"),
            P("chan", None),
        ),
        out_specs=P(("groups", "seq"), "chan"),
        check_vma=False,
    )
```
